128 devices in a mesh: rows: 32 (over x, y_lo, z), cols: 4 (over y_hi, core).
Axes of the slice: x: 4, y: 4 (y_hi: 2, y_lo: 2; y = y_hi * 2 + y_lo), z: 4, core: 2. Of those that a mesh axis runs over, the one named last changes fastest.
Arguments:
- pair_feature_input: bfloat16 [64, 1024, 2048], P(None, 'rows', 'cols'), may hold values from -6 to 6
- tile_mask: int32 [8, 16], replicated, may hold values 0 or 1
- row_kernel_weights: bfloat16 [2, 3, 64, 64], replicated, may hold values from -0.4375 to 0.4375
- column_kernel_weights: bfloat16 [2, 3, 64, 64], replicated, may hold values from -0.4375 to 0.4375
- cotangent: bfloat16 [64, 1024, 2048], P(None, 'rows', 'cols'), may hold values from -6 to 6
Outputs:
- final_output_map: bfloat16 [64, 1024, 2048], P(None, 'rows', 'cols')
- map_grad: bfloat16 [64, 1024, 2048], P(None, 'rows', 'cols')
- row_grad: float32 [2, 3, 64, 64], replicated
- col_grad: float32 [2, 3, 64, 64], replicated
The draws below stay inside these ranges and needn't reach their ends.
All inputs are finite; a program needn't handle non-finite values.
Results may differ from the reference program's by a relative error of at most 0.0075.
Values may be sent and summed in bfloat16 or wider, within the bound.
No kernel may reach another device: no remote copies, remote signals or barrier semaphores. Data moves between devices by JAX's collectives and lax.ppermute only.
A program may use at most 192 MiB of HBM per device.

```python
import math
import jax
import jax.numpy as jnp
from jax import lax

C = 64
FIRST_SPACING = 4
SECOND_SPACING = 8
TILE = 128
MAP_ROWS = 1024
MAP_COLS = 2048
TILE_ROWS = 8
TILE_COLS = 16


def place_ends(values, own_key, low, largest):
    extent = values.shape
    spot = [jax.random.randint(jax.random.fold_in(own_key, axis), (), 0, extent[axis]) for axis in range(len(extent))]
    values = values.at[tuple(spot)].set(low)
    longest = extent.index(max(extent))
    spot[longest] = (spot[longest] + 1) % extent[longest]
    return values.at[tuple(spot)].set(largest)


def level_of(own_key, shape, shards, smallest, top_value):
    def one(axis_at, parts):
        heights = jax.random.uniform(jax.random.fold_in(jax.random.fold_in(own_key, 6), axis_at), (parts,), jnp.float32, smallest / len(shards), top_value / len(shards))
        return jnp.repeat(jnp.exp(heights), shape[axis_at] // parts).reshape((-1,) + (1,) * (len(shape) - axis_at - 1))

    loudness = one(*shards[0])
    for cut in shards[1:]:
        loudness = loudness * one(*cut)
    return loudness


def bell_draw(stream_key, shape, deviation, most, shards=(), held_as=jnp.bfloat16):
    array = jax.random.normal(stream_key, shape, jnp.float32) * deviation
    if len(shards) > 0:
        array = level_of(stream_key, shape, shards, -0.22, 0.18) * array
    return jnp.clip(array, min=-most, max=most).astype(held_as)


def setup_inputs(seed: int = 0) -> dict:
    streams_of = jax.random.split(jax.random.key(seed), 6)
    return {
        "pair_feature_input": bell_draw(streams_of[0], (C, MAP_ROWS, MAP_COLS), 1.0, 6.0, ((1, 32), (2, 4))),
        "tile_mask": place_ends((jax.random.randint(streams_of[1], (TILE_ROWS, TILE_COLS), 0, 4) < 3).astype(jnp.int32), jax.random.fold_in(streams_of[1], 1), 0, 1),
        "row_kernel_weights": bell_draw(streams_of[2], (2, 3, C, C), (3 * C) ** -0.5, 0.4375),
        "column_kernel_weights": bell_draw(streams_of[3], (2, 3, C, C), (3 * C) ** -0.5, 0.4375),
        "cotangent": bell_draw(streams_of[4], (C, MAP_ROWS, MAP_COLS), 1.0, 6.0, ((1, 32), (2, 4))),
    }


def shifted(values, k, along):
    if k == 0:
        return values
    size_along = values.shape[along]
    widths = [(0, 0)] * values.ndim
    widths[along] = (abs(k), abs(k))
    padded = jnp.pad(values, widths)
    return lax.slice_in_dim(padded, abs(k) + k, abs(k) + k + size_along, axis=along)

def channel_mix(matrix, values):
    flat = values.reshape(values.shape[0], values.shape[1] * values.shape[2])
    mixed = jnp.dot(matrix, flat, preferred_element_type=jnp.float32)
    return mixed.reshape(matrix.shape[0], values.shape[1], values.shape[2])

def conv_taps(values, weights, reach, along, direction):
    total = jnp.zeros(values.shape, jnp.float32)
    for j in range(3):
        matrix = weights[j] if direction > 0 else weights[j].T
        total = total + channel_mix(matrix, shifted(values, direction * (j - 1) * reach, along))
    return total

def flat_product(first, second):
    left = first.reshape(first.shape[0], first.shape[1] * first.shape[2])
    right = second.reshape(second.shape[0], second.shape[1] * second.shape[2])
    return jnp.dot(left, right.T, preferred_element_type=jnp.float32)

def tap_grads(upstream_gradient, values, reach, along):
    return jnp.stack([flat_product(shifted(upstream_gradient, -(j - 1) * reach, along), values) for j in range(3)])

def cell_mask(tile_mask):
    row_tiles = jnp.arange(MAP_ROWS, dtype=jnp.int32) // TILE
    col_tiles = jnp.arange(MAP_COLS, dtype=jnp.int32) // TILE
    return tile_mask[row_tiles][:, col_tiles].astype(jnp.float32)

def residual_block_apply(block_in, row_taps, col_taps, reach, chain_pair_mask):
    pre_act = conv_taps(block_in, row_taps, reach, 2, 1)
    hidden = (jax.nn.elu(pre_act) * chain_pair_mask).astype(jnp.bfloat16)
    col_out = conv_taps(hidden, col_taps, reach, 1, 1).astype(jnp.bfloat16)
    col_out = lax.optimization_barrier(col_out).astype(jnp.float32)
    return (block_in.astype(jnp.float32) + chain_pair_mask * col_out).astype(jnp.bfloat16)

def residual_block_reverse(block_in, out_grad, row_taps, col_taps, reach, chain_pair_mask):
    pre_act = conv_taps(block_in, row_taps, reach, 2, 1)
    hidden = (jax.nn.elu(pre_act) * chain_pair_mask).astype(jnp.bfloat16)
    slope = jnp.where(pre_act > 0, 1.0, jnp.exp(jnp.minimum(pre_act, 0.0))).astype(jnp.float32)
    masked_grad = (chain_pair_mask * out_grad).astype(jnp.bfloat16)
    hid_grad = conv_taps(masked_grad, col_taps, reach, 1, -1)
    col_wgrad = tap_grads(masked_grad, hidden, reach, 1)
    act_grad = (hid_grad * chain_pair_mask * slope).astype(jnp.bfloat16)
    row_wgrad = tap_grads(act_grad, block_in, reach, 2)
    in_grad = out_grad + conv_taps(act_grad, row_taps, reach, 2, -1)
    return (in_grad, row_wgrad, col_wgrad)

def reference(pair_feature_input, tile_mask, row_kernel_weights, column_kernel_weights, cotangent):
    chain_pair_mask = cell_mask(tile_mask)
    first_block_output = residual_block_apply(pair_feature_input, row_kernel_weights[0], column_kernel_weights[0], FIRST_SPACING, chain_pair_mask)
    final_output_map = residual_block_apply(first_block_output, row_kernel_weights[1], column_kernel_weights[1], SECOND_SPACING, chain_pair_mask)
    upstream_gradient = cotangent.astype(jnp.float32)
    upstream_gradient, second_row_conv, second_column_conv = residual_block_reverse(first_block_output, upstream_gradient, row_kernel_weights[1], column_kernel_weights[1], SECOND_SPACING, chain_pair_mask)
    upstream_gradient, first_row_conv, first_column_conv = residual_block_reverse(pair_feature_input, upstream_gradient, row_kernel_weights[0], column_kernel_weights[0], FIRST_SPACING, chain_pair_mask)
    factor = 1.0 / math.sqrt(MAP_ROWS * MAP_COLS)
    return (final_output_map, upstream_gradient.astype(jnp.bfloat16), jnp.stack([first_row_conv, second_row_conv]) * factor, jnp.stack([first_column_conv, second_column_conv]) * factor)
```

```python
import functools
import math

import jax
import jax.numpy as jnp
from jax import lax
from jax.experimental import pallas as pl
from jax.experimental.pallas import tpu as pltpu
from jax.sharding import Mesh, PartitionSpec as P

FIRST_SPACING = 4
SECOND_SPACING = 8
TILE = 128
C = 64
R = 32
W = 512
E = 640
HALO = 12
EDGE = 32
GROUPS = R // 4
HG = HALO // 4
F32 = jnp.float32
BF16 = jnp.bfloat16
VMEM_LIMIT = 60 * 1024 * 1024


def dot(a, b):
    return jnp.dot(a, b, preferred_element_type=F32)


def dot_nt(a, b):
    return lax.dot_general(a, b, (((1,), (1,)), ((), ())), preferred_element_type=F32)


def pack_kernel(x_ref, c_ref, xt, xtop, xbot, ct, ctop, cbot, to_left, to_right, scratch):
    w = pl.program_id(0)
    i = pl.program_id(1)
    lane = lax.broadcasted_iota(jnp.int32, (C, 128), 1)
    for a, (src, dst, top, bot) in enumerate(((x_ref, xt, xtop, xbot), (c_ref, ct, ctop, cbot))):
        scratch[...] = src[...].astype(F32).reshape(C * 16, 128)

        def row(r):
            return scratch[pl.ds(r, C, stride=16), :]

        for r in range(16):
            dst[r] = row(r).astype(BF16)

        @pl.when(i == 0)
        def _():
            top[...] = dst[0:HALO]

        @pl.when(i == 1)
        def _():
            bot[...] = dst[16 - HALO : 16]

        def pack(out, first):
            for g in range(4):
                acc = jnp.zeros((C, 128), F32)
                for k in range(4):
                    v = row(4 * g + k)
                    shift = (32 * k - first) % 128
                    if shift:
                        v = pltpu.roll(v, shift, 1)
                    acc = jnp.where(lane // 32 == k, v, acc)
                out[a, i * 4 + g] = acc.astype(BF16)

        @pl.when(w == 0)
        def _():
            pack(to_left, 0)

        @pl.when(w == W // 128 - 1)
        def _():
            pack(to_right, 96)


def pack_call(x, c):
    native = pl.BlockSpec((C, 16, 128), lambda w, i: (0, i, w))
    turned = pl.BlockSpec((16, C, 128), lambda w, i: (i, 0, w))
    halo = pl.BlockSpec((HALO, C, 128), lambda w, i: (0, 0, w))
    edge = pl.BlockSpec((2, GROUPS, C, 128), lambda w, i: (0, 0, 0, 0))
    full = jax.ShapeDtypeStruct((R, C, W), BF16)
    part = jax.ShapeDtypeStruct((HALO, C, W), BF16)
    edges = jax.ShapeDtypeStruct((2, GROUPS, C, 128), BF16)
    return pl.pallas_call(
        pack_kernel,
        grid=(W // 128, 2),
        in_specs=[native, native],
        out_specs=[turned, halo, halo, turned, halo, halo, edge, edge],
        out_shape=[full, part, part, full, part, part, edges, edges],
        scratch_shapes=[pltpu.VMEM((C * 16, 128), F32)],
        compiler_params=pltpu.CompilerParams(vmem_limit_bytes=VMEM_LIMIT),
    )(x, c)


def build_mask(tiles, mask):
    row_dev, col_dev = lax.axis_index("rows"), lax.axis_index("cols")
    n_rows, n_cols = tiles.shape
    first_row, first_tile = row_dev * R, col_dev * (W // TILE)
    lane = lax.broadcasted_iota(jnp.int32, (8, 128), 1)

    def value(p, ct):
        cell = first_row + (-1, 0, R)[p]
        inside = (cell >= 0) & (cell < n_rows * TILE) & (ct >= 0) & (ct < n_cols)
        rt = jnp.clip(cell, 0, n_rows * TILE - 1) // TILE
        return jnp.where(inside, tiles[rt, jnp.clip(ct, 0, n_cols - 1)], 0)

    for p in range(3):
        for t in range(W // 128):
            mask[p, :, t * 128 : (t + 1) * 128] = jnp.full((8, 128), value(p, first_tile + t), jnp.int32).astype(F32)
        right = jnp.full((8, 128), value(p, first_tile + W // TILE), jnp.int32)
        left = jnp.full((8, 128), value(p, first_tile - 1), jnp.int32)
        mask[p, :, W:E] = jnp.where(lane < 64, right, left).astype(F32)


def mask_row(mask, r):
    p = (r >= 0).astype(jnp.int32) + (r >= R).astype(jnp.int32)
    return mask[p][0:1, :]


def unpack_edges(left, right, dst, first):
    lane = lax.broadcasted_iota(jnp.int32, (C, 128), 1)
    for k in range(4):
        rv, lv = right.astype(F32), left.astype(F32)
        if k:
            rv = pltpu.roll(rv, 128 - 32 * k, 1)
        if k != 3:
            lv = pltpu.roll(lv, 96 - 32 * k, 1)
        tile = jnp.where(lane < EDGE, rv, jnp.where(lane >= 128 - EDGE, lv, 0.0))
        dst[first + k, :, W:E] = tile.astype(BF16)


def unpack_all(a, col_left, col_right, cor_top, cor_bot, dst):
    for g in range(HG):
        unpack_edges(cor_top[a, 0, g], cor_top[a, 1, g], dst, 4 * g)
        unpack_edges(cor_bot[a, 0, g], cor_bot[a, 1, g], dst, HALO + R + 4 * g)

    def own(g, _):
        unpack_edges(col_left[a, g], col_right[a, g], dst, HALO + 4 * g)
        return 0

    lax.fori_loop(0, GROUPS, own, 0)


def shifted(v, d):
    n = v.shape[1]
    return pltpu.roll(v, (-d) % n, 1)


def row_stack(v, d, reverse):
    ahead, behind = shifted(v, d), shifted(v, -d)
    parts = [ahead, v, behind] if reverse else [behind, v, ahead]
    return jnp.concatenate(parts, axis=0)


def col_stack(ref, r, d, reverse, width=E):
    parts = [ref[r - d, :, :width], ref[r, :, :width], ref[r + d, :, :width]]
    return jnp.concatenate(parts[::-1] if reverse else parts, axis=0)


def forward_matrix(w):
    return jnp.concatenate([w[j].astype(F32).T for j in range(3)], axis=0).T.astype(BF16)


def backward_matrix(w):
    return w.reshape(3 * C, C).astype(F32).T.astype(BF16)


def elu(p):
    return jnp.where(p > 0, p, jnp.exp(jnp.minimum(p, 0.0)) - 1.0)


def pairs(count, body):
    def step(i, _):
        body(2 * i)
        return 0

    lax.fori_loop(0, count // 2, step, 0)


def two(stack, matrix):
    both = dot(matrix, jnp.concatenate(stack, axis=1))
    n = stack[0].shape[1]
    return both[:, :n], both[:, n:]


def put_flat(flat, r, v):
    for t in range(W // 128):
        flat[t, pl.ds(r, C, stride=R), :] = v[:, t * 128 : (t + 1) * 128]


def narrow(flat, out):
    def channel(c, _):
        for t in range(W // 128):
            out[c, :, t * 128 : (t + 1) * 128] = flat[t, pl.ds(pl.multiple_of(c * R, R), R), :].astype(BF16)
        return 0

    lax.fori_loop(0, C, channel, 0)


def forward_kernel(
    tiles, x, xtop, xbot, col_left, col_right, cor_top, cor_bot, wr, wc,
    out, h1_out, b1_out, h2_out,
    xe, h1, b1, h2, flat, mask, sems,
):
    loads = [
        pltpu.make_async_copy(x, xe.at[HALO : HALO + R, :, 0:W], sems.at[0]),
        pltpu.make_async_copy(xtop, xe.at[0:HALO, :, 0:W], sems.at[1]),
        pltpu.make_async_copy(xbot, xe.at[HALO + R :, :, 0:W], sems.at[2]),
    ]
    for load in loads:
        load.start()
    build_mask(tiles, mask)
    unpack_all(0, col_left, col_right, cor_top, cor_bot, xe)
    wr1, wr2 = forward_matrix(wr[0]), forward_matrix(wr[1])
    wc1, wc2 = forward_matrix(wc[0]), forward_matrix(wc[1])
    for load in loads:
        load.wait()

    d1, d2 = FIRST_SPACING, SECOND_SPACING

    def hidden_one(r):
        pre = two([row_stack(xe[r + q], d1, False) for q in range(2)], wr1)
        for q in range(2):
            h1[r + q] = (elu(pre[q]) * mask_row(mask, r + q - HALO)).astype(BF16)

    pairs(R + 2 * HALO, hidden_one)
    save_h1 = pltpu.make_async_copy(h1.at[HALO : HALO + R], h1_out, sems.at[3])
    save_h1.start()

    def block_one(r):
        col = two([col_stack(h1, r + q + d1, d1, False) for q in range(2)], wc1)
        for q in range(2):
            kept = mask_row(mask, r + q + d1 - HALO) * col[q].astype(BF16).astype(F32)
            b1[r + q] = (xe[r + q + d1].astype(F32) + kept).astype(BF16)

    pairs(R + 2 * d2, block_one)
    save_b1 = pltpu.make_async_copy(b1.at[d2 : d2 + R], b1_out, sems.at[4])
    save_b1.start()

    def hidden_two(r):
        pre = two([row_stack(b1[r + q], d2, False) for q in range(2)], wr2)
        for q in range(2):
            h2[r + q] = (elu(pre[q]) * mask_row(mask, r + q - d2)).astype(BF16)

    pairs(R + 2 * d2, hidden_two)
    save_h2 = pltpu.make_async_copy(h2.at[d2 - d1 : d2 + R + d1], h2_out, sems.at[5])
    save_h2.start()

    def last(r):
        col = two([col_stack(h2, r + q + d2, d2, False, W) for q in range(2)], wc2)
        for q in range(2):
            kept = mask_row(mask, r + q)[:, :W] * col[q].astype(BF16).astype(F32)
            put_flat(flat, r + q, b1[r + q + d2, :, :W].astype(F32) + kept)

    pairs(R, last)

    narrow(flat, out)
    save_h1.wait()
    save_b1.wait()
    save_h2.wait()


ANY = pl.BlockSpec(memory_space=pl.ANY)
VM = pl.BlockSpec(memory_space=pltpu.VMEM)
SM = pl.BlockSpec(memory_space=pltpu.SMEM)


def forward_call(tiles, x, xtop, xbot, col_left, col_right, cor_top, cor_bot, wr, wc):
    d1, d2 = FIRST_SPACING, SECOND_SPACING
    return pl.pallas_call(
        forward_kernel,
        in_specs=[SM, ANY, ANY, ANY, VM, VM, VM, VM, VM, VM],
        out_specs=[VM, ANY, ANY, ANY],
        out_shape=[
            jax.ShapeDtypeStruct((C, R, W), BF16),
            jax.ShapeDtypeStruct((R, C, E), BF16),
            jax.ShapeDtypeStruct((R, C, E), BF16),
            jax.ShapeDtypeStruct((R + 2 * d1, C, E), BF16),
        ],
        scratch_shapes=[
            pltpu.VMEM((R + 2 * HALO, C, E), BF16),
            pltpu.VMEM((R + 2 * HALO, C, E), BF16),
            pltpu.VMEM((R + 2 * d2, C, E), BF16),
            pltpu.VMEM((R + 2 * d2, C, E), BF16),
            pltpu.VMEM((W // 128, C * R, 128), F32),
            pltpu.VMEM((3, 8, E), F32),
            pltpu.SemaphoreType.DMA((6,)),
        ],
        compiler_params=pltpu.CompilerParams(vmem_limit_bytes=VMEM_LIMIT),
    )(tiles, x, xtop, xbot, col_left, col_right, cor_top, cor_bot, wr, wc)


def backward_kernel(
    tiles, c, ctop, cbot, col_left, col_right, cor_top, cor_bot, wr, wc, x_in, h1_in, b1_in, h2_in,
    out, taps,
    ce, h1, b1, h2, x, a2, cg1, g1, a1, flat, mask, sems,
):
    d1, d2 = FIRST_SPACING, SECOND_SPACING
    loads = [
        pltpu.make_async_copy(c, ce.at[HALO : HALO + R, :, 0:W], sems.at[0]),
        pltpu.make_async_copy(ctop, ce.at[0:HALO, :, 0:W], sems.at[1]),
        pltpu.make_async_copy(cbot, ce.at[HALO + R :, :, 0:W], sems.at[2]),
    ]
    late = [
        pltpu.make_async_copy(h2_in, h2, sems.at[3]),
        pltpu.make_async_copy(b1_in, b1, sems.at[4]),
        pltpu.make_async_copy(h1_in, h1, sems.at[5]),
        pltpu.make_async_copy(x_in, x, sems.at[6]),
    ]
    for load in loads + late:
        load.start()
    build_mask(tiles, mask)
    unpack_all(1, col_left, col_right, cor_top, cor_bot, ce)
    wr1, wr2 = backward_matrix(wr[0]), backward_matrix(wr[1])
    wc1, wc2 = backward_matrix(wc[0]), backward_matrix(wc[1])
    taps[...] = jnp.zeros_like(taps)
    for load in loads + late:
        load.wait()

    def mask_cot(r):
        for q in range(2):
            v = ce[r + q]
            m = mask_row(mask, r + q - HALO)
            ce[r + q] = (v.astype(F32) * m).astype(BF16)

    def keep_cot(r):
        for q in range(2):
            g1[r + q] = ce[HALO - d1 + r + q].astype(F32)

    pairs(R + 2 * d1, keep_cot)
    pairs(R + 2 * HALO, mask_cot)

    def act_two(r):
        stacks = [col_stack(ce, r + q + HALO - d1, d2, True) for q in range(2)]
        hid = two(stacks, wc2)
        for q in range(2):
            m = mask_row(mask, r + q - d1)
            slope = 1.0 + jnp.minimum(h2[r + q].astype(F32), 0.0)
            a2[r + q] = (hid[q] * m * slope).astype(BF16)

    pairs(R + 2 * d1, act_two)

    def col_taps_two(r):
        acc = taps[0]
        for q in range(2):
            acc = acc + dot_nt(col_stack(ce, r + q + HALO, d2, True, W), h2[r + q + d1, :, :W])
        taps[0] = acc

    pairs(R, col_taps_two)

    def grad_one(r):
        stacks = [row_stack(a2[r + q], d2, True) for q in range(2)]
        mixed = two(stacks, wr2)
        for q in range(2):
            g = g1[r + q] + mixed[q]
            g1[r + q] = g
            cg1[r + q] = (g * mask_row(mask, r + q - d1)).astype(BF16)

    pairs(R + 2 * d1, grad_one)

    def row_taps_two(r):
        acc = taps[1]
        for q in range(2):
            stack = row_stack(a2[r + q + d1], d2, True)
            acc = acc + dot_nt(stack[:, :W], b1[r + q, :, :W])
        taps[1] = acc

    pairs(R, row_taps_two)

    def act_one(r):
        stacks = [col_stack(cg1, r + q + d1, d1, True) for q in range(2)]
        hid = two(stacks, wc1)
        acc = taps[2]
        for q in range(2):
            m = mask_row(mask, r + q)
            h = h1[r + q]
            slope = 1.0 + jnp.minimum(h.astype(F32), 0.0)
            a1[r + q] = (hid[q] * m * slope).astype(BF16)
            acc = acc + dot_nt(stacks[q][:, :W], h[:, :W])
        taps[2] = acc

    pairs(R, act_one)

    def last(r):
        stacks = [row_stack(a1[r + q], d1, True)[:, :W] for q in range(2)]
        mixed = two(stacks, wr1)
        acc = taps[3]
        for q in range(2):
            put_flat(flat, r + q, g1[r + q + d1, :, :W] + mixed[q])
            acc = acc + dot_nt(stacks[q], x[r + q])
        taps[3] = acc

    pairs(R, last)

    narrow(flat, out)


def backward_call(tiles, c, ctop, cbot, col_left, col_right, cor_top, cor_bot, wr, wc, x, h1, b1, h2):
    d1 = FIRST_SPACING
    return pl.pallas_call(
        backward_kernel,
        in_specs=[SM, ANY, ANY, ANY, VM, VM, VM, VM, VM, VM, ANY, ANY, ANY, ANY],
        out_specs=[VM, VM],
        out_shape=[
            jax.ShapeDtypeStruct((C, R, W), BF16),
            jax.ShapeDtypeStruct((4, 3 * C, C), F32),
        ],
        scratch_shapes=[
            pltpu.VMEM((R + 2 * HALO, C, E), BF16),
            pltpu.VMEM((R, C, E), BF16),
            pltpu.VMEM((R, C, E), BF16),
            pltpu.VMEM((R + 2 * d1, C, E), BF16),
            pltpu.VMEM((R, C, W), BF16),
            pltpu.VMEM((R + 2 * d1, C, E), BF16),
            pltpu.VMEM((R + 2 * d1, C, E), BF16),
            pltpu.VMEM((R + 2 * d1, C, E), F32),
            pltpu.VMEM((R, C, E), BF16),
            pltpu.VMEM((W // 128, C * R, 128), F32),
            pltpu.VMEM((3, 8, E), F32),
            pltpu.SemaphoreType.DMA((7,)),
        ],
        compiler_params=pltpu.CompilerParams(vmem_limit_bytes=VMEM_LIMIT),
    )(tiles, c, ctop, cbot, col_left, col_right, cor_top, cor_bot, wr, wc, x, h1, b1, h2)


def tap_sum(taps):
    flat = taps.reshape(-1, 128)
    wide = lax.axis_size("rows")
    part = lax.all_to_all(flat, "rows", 0, 0, tiled=True).reshape(wide, -1, 128).sum(0)
    cols = lax.axis_size("cols")
    spread = jnp.broadcast_to(part[None], (cols,) + part.shape).reshape(-1, 128)
    part = lax.all_to_all(spread, "cols", 0, 0, tiled=True).reshape(cols, -1, 128).sum(0)
    spread = jnp.broadcast_to(part[None], (wide,) + part.shape).reshape(-1, 128)
    whole = lax.all_to_all(spread, "rows", 0, 0, tiled=True)
    return whole.reshape(4, 3, C, C)


def on_device(x, tile_mask, wr, wc, cot):
    n_rows, n_cols = lax.axis_size("rows"), lax.axis_size("cols")
    factor = 1.0 / math.sqrt(R * n_rows * W * n_cols)
    down = [(i, i + 1) for i in range(n_rows - 1)]
    up = [(i + 1, i) for i in range(n_rows - 1)]
    right = [(i, i + 1) for i in range(n_cols - 1)]
    left = [(i + 1, i) for i in range(n_cols - 1)]

    xt, xtop, xbot, ct, ctop, cbot, to_left, to_right = pack_call(x, cot)
    col_right = lax.ppermute(to_left, "cols", left)
    col_left = lax.ppermute(to_right, "cols", right)
    xabove = lax.ppermute(xbot, "rows", down)
    xbelow = lax.ppermute(xtop, "rows", up)
    first = jnp.stack([col_left[:, :HG], col_right[:, :HG]], axis=1)
    last = jnp.stack([col_left[:, GROUPS - HG :], col_right[:, GROUPS - HG :]], axis=1)
    cor_bot = lax.ppermute(first, "rows", up)
    cor_top = lax.ppermute(last, "rows", down)
    cabove = lax.ppermute(cbot, "rows", down)
    cbelow = lax.ppermute(ctop, "rows", up)

    final, h1, b1, h2 = forward_call(
        tile_mask, xt, xabove, xbelow, col_left, col_right, cor_top, cor_bot, wr, wc
    )
    map_grad, taps = backward_call(
        tile_mask, ct, cabove, cbelow, col_left, col_right, cor_top, cor_bot, wr, wc, xt, h1, b1, h2
    )
    total = tap_sum(taps) * factor
    row_grad = jnp.stack([total[3], total[1]])
    col_grad = jnp.stack([total[2], total[0]])
    return final, map_grad, row_grad, col_grad


def solution(mesh):
    placed = (P(None, "rows", "cols"), P(), P(), P(), P(None, "rows", "cols"))
    return jax.shard_map(
        on_device,
        mesh=mesh,
        in_specs=placed,
        out_specs=(P(None, "rows", "cols"), P(None, "rows", "cols"), P(), P()),
        check_vma=False,
    )
```

```python
import functools
import math

import jax
import jax.numpy as jnp
from jax import lax
from jax.experimental import pallas as pl
from jax.experimental.pallas import tpu as pltpu
from jax.sharding import Mesh, PartitionSpec as P

FIRST_SPACING = 4
SECOND_SPACING = 8
TILE = 128
C = 64
R = 32
W = 512
E = 640
HALO = 12
EDGE = 32
GROUPS = R // 4
HG = HALO // 4
F32 = jnp.float32
BF16 = jnp.bfloat16
VMEM_LIMIT = 60 * 1024 * 1024


def dot(a, b):
    return jnp.dot(a, b, preferred_element_type=F32)


def dot_nt(a, b):
    return lax.dot_general(a, b, (((1,), (1,)), ((), ())), preferred_element_type=F32)


def turn(block):
    return jnp.swapaxes(block, 0, 1)


def pack(out, a, i, block, first):
    lane = lax.broadcasted_iota(jnp.int32, (C, 128), 1)
    for g in range(4):
        acc = jnp.zeros((C, 128), F32)
        for k in range(4):
            v = block[4 * g + k].astype(F32)
            shift = (32 * k - first) % 128
            if shift:
                v = pltpu.roll(v, shift, 1)
            acc = jnp.where(lane // 32 == k, v, acc)
        out[a, i * 4 + g] = acc.astype(BF16)


def pack_x_kernel(x_ref, c_ref, xt, xtop, xbot, to_left, to_right):
    w = pl.program_id(0)
    i = pl.program_id(1)
    xt[...] = turn(x_ref[...])

    @pl.when(i == 0)
    def _():
        xtop[...] = xt[0:HALO]

    @pl.when(i == 1)
    def _():
        xbot[...] = xt[16 - HALO : 16]

    for out, at, first in ((to_left, 0, 0), (to_right, W // 128 - 1, 96)):

        @pl.when(w == at)
        def _():
            pack(out, 0, i, xt[...], first)
            pack(out, 1, i, turn(c_ref[...]), first)


def turn_c_kernel(c_ref, after, ct, ctop, cbot):
    i = pl.program_id(1)
    ct[...] = turn(c_ref[...])

    @pl.when(i == 0)
    def _():
        ctop[...] = ct[0:HALO]

    @pl.when(i == 1)
    def _():
        cbot[...] = ct[16 - HALO : 16]


NATIVE = pl.BlockSpec((C, 16, 128), lambda w, i: (0, i, w))
TURNED = pl.BlockSpec((16, C, 128), lambda w, i: (i, 0, w))
HALO_ROWS = pl.BlockSpec((HALO, C, 128), lambda w, i: (0, 0, w))
FULL = jax.ShapeDtypeStruct((R, C, W), BF16)
PART = jax.ShapeDtypeStruct((HALO, C, W), BF16)


def pack_x(x, c):
    edge = pl.BlockSpec((2, GROUPS, C, 128), lambda w, i: (0, 0, 0, 0))
    edges = jax.ShapeDtypeStruct((2, GROUPS, C, 128), BF16)
    return pl.pallas_call(
        pack_x_kernel,
        grid=(W // 128, 2),
        in_specs=[NATIVE, NATIVE],
        out_specs=[TURNED, HALO_ROWS, HALO_ROWS, edge, edge],
        out_shape=[FULL, PART, PART, edges, edges],
        compiler_params=pltpu.CompilerParams(vmem_limit_bytes=VMEM_LIMIT),
        name="pack_x",
    )(x, c)


def turn_c(c, after):
    return pl.pallas_call(
        turn_c_kernel,
        grid=(W // 128, 2),
        in_specs=[NATIVE, pl.BlockSpec(memory_space=pl.ANY)],
        out_specs=[TURNED, HALO_ROWS, HALO_ROWS],
        out_shape=[FULL, PART, PART],
        compiler_params=pltpu.CompilerParams(vmem_limit_bytes=VMEM_LIMIT),
        name="turn_c",
    )(c, after)


def build_mask(tiles, mask):
    row_dev, col_dev = lax.axis_index("rows"), lax.axis_index("cols")
    n_rows, n_cols = tiles.shape
    first_row, first_tile = row_dev * R, col_dev * (W // TILE)
    lane = lax.broadcasted_iota(jnp.int32, (16, 128), 1)

    def value(p, ct):
        cell = first_row + (-1, 0, R)[p]
        inside = (cell >= 0) & (cell < n_rows * TILE) & (ct >= 0) & (ct < n_cols)
        rt = jnp.clip(cell, 0, n_rows * TILE - 1) // TILE
        return jnp.where(inside, tiles[rt, jnp.clip(ct, 0, n_cols - 1)], 0)

    for p in range(3):
        for t in range(W // 128):
            cell = jnp.full((16, 128), value(p, first_tile + t), jnp.int32)
            mask[p, :, t * 128 : (t + 1) * 128] = cell.astype(F32).astype(BF16)
        right = jnp.full((16, 128), value(p, first_tile + W // TILE), jnp.int32)
        left = jnp.full((16, 128), value(p, first_tile - 1), jnp.int32)
        mask[p, :, W:E] = jnp.where(lane < 64, right, left).astype(F32).astype(BF16)


def masked(v, mask, r, at):
    if isinstance(r, int):
        p = int(r >= 0) + int(r >= R)
    else:
        p = (r >= 0).astype(jnp.int32) + (r >= R).astype(jnp.int32)
    m = mask[p, :, at]
    return v * jnp.concatenate([m] * (C // 16), axis=0)


def unpack_edges(left, right, dst, first):
    lane = lax.broadcasted_iota(jnp.int32, (C, 128), 1)
    for k in range(4):
        rv, lv = right.astype(F32), left.astype(F32)
        if k:
            rv = pltpu.roll(rv, 128 - 32 * k, 1)
        if k != 3:
            lv = pltpu.roll(lv, 96 - 32 * k, 1)
        tile = jnp.where(lane < EDGE, rv, jnp.where(lane >= 128 - EDGE, lv, 0.0))
        dst[first + k, :, W:E] = tile.astype(BF16)


def unpack_all(a, col_left, col_right, cor_top, cor_bot, dst):
    for g in range(HG):
        unpack_edges(cor_top[a, 0, g], cor_top[a, 1, g], dst, 4 * g)
        unpack_edges(cor_bot[a, 0, g], cor_bot[a, 1, g], dst, HALO + R + 4 * g)

    def own(g, _):
        unpack_edges(col_left[a, g], col_right[a, g], dst, HALO + 4 * g)
        return 0

    lax.fori_loop(0, GROUPS, own, 0)


def shifted(v, d):
    return pltpu.roll(v, (-d) % v.shape[1], 1)


def row_stack(v, d, reverse):
    ahead, behind = shifted(v, d), shifted(v, -d)
    parts = [ahead, v, behind] if reverse else [behind, v, ahead]
    return jnp.concatenate(parts, axis=0)


def col_stack(ref, r, d, at):
    return jnp.concatenate([ref[r + d, :, at], ref[r, :, at], ref[r - d, :, at]], axis=0)


def forward_matrix(w):
    return jnp.concatenate([w[j].astype(F32).T for j in range(3)], axis=0).T.astype(BF16)


def backward_matrix(w, order=(0, 1, 2)):
    return jnp.concatenate([w[j].astype(F32) for j in order], axis=0).T.astype(BF16)


def two_rows(matrix):
    none = jnp.zeros((C, C), BF16)
    return jnp.concatenate(
        [jnp.concatenate([matrix, none], axis=1), jnp.concatenate([none, matrix], axis=1)], axis=0
    )


MAIN = (slice(0, 256), slice(256, 512))
TAIL = slice(W, E)


def loop(count, step, body):
    def one(i, _):
        body(i * step)
        return 0

    lax.fori_loop(0, count // step, one, 0)


def conv_columns(ref, rows, d, matrix, post, tail=True):
    def window(r, at):
        return jnp.concatenate([ref[r + k * d, :, at] for k in (-1, 0, 1, 2)], axis=0)

    for r in rows:
        for at in MAIN:
            both = dot(matrix, window(r, at))
            post(r, at, both[:C])
            post(r + d, at, both[C:])
    if tail:
        for r, s in zip(rows[::2], rows[1::2]):
            both = dot(matrix, jnp.concatenate([window(r, TAIL), window(s, TAIL)], axis=1))
            for row, half in ((r, both[:, :128]), (s, both[:, 128:])):
                post(row, TAIL, half[:C])
                post(row + d, TAIL, half[C:])


def conv_columns_single(ref, rows, d, matrix, post):
    def window(r, at):
        return jnp.concatenate([ref[r + k * d, :, at] for k in (-1, 0, 1)], axis=0)

    for r in rows:
        for at in MAIN:
            post(r, at, dot(matrix, window(r, at)))
    for r, s in zip(rows[::2], rows[1::2]):
        both = dot(matrix, jnp.concatenate([window(r, TAIL), window(s, TAIL)], axis=1))
        post(r, TAIL, both[:, :128])
        post(s, TAIL, both[:, 128:])


def conv_rows(ref, rows, d, reverse, matrix, post, tail=True):
    stacks = []
    for r in rows:
        stack = row_stack(ref[r], d, reverse)
        stacks.append(stack)
        for at in MAIN:
            post(r, at, dot(matrix, stack[:, at]))
    if tail:
        for q in range(0, len(rows), 2):
            both = dot(matrix, jnp.concatenate([stacks[q][:, TAIL], stacks[q + 1][:, TAIL]], axis=1))
            post(rows[q], TAIL, both[:, :128])
            post(rows[q + 1], TAIL, both[:, 128:])
    return stacks


def elu(p):
    return jnp.where(p > 0, p, jnp.exp(p) - 1.0)


def turn_out(src, out):
    for i in range(R // 16):
        for t in range(W // 128):
            at = slice(t * 128, (t + 1) * 128)
            out[:, i * 16 : (i + 1) * 16, at] = turn(src[i * 16 : (i + 1) * 16, :, at])


def forward_kernel(
    tiles, x, xtop, xbot, col_left, col_right, cor_top, cor_bot, wr, wc,
    out, h1_out, b1_out, h2_out,
    xe, h1, b1, h2, flat, mask, sems,
):
    loads = [
        pltpu.make_async_copy(x, xe.at[HALO : HALO + R, :, 0:W], sems.at[0]),
        pltpu.make_async_copy(xtop, xe.at[0:HALO, :, 0:W], sems.at[1]),
        pltpu.make_async_copy(xbot, xe.at[HALO + R :, :, 0:W], sems.at[2]),
    ]
    for load in loads:
        load.start()
    build_mask(tiles, mask)
    unpack_all(0, col_left, col_right, cor_top, cor_bot, xe)
    wr1, wr2 = forward_matrix(wr[0]), forward_matrix(wr[1])
    wc1, wc2 = two_rows(forward_matrix(wc[0])), two_rows(forward_matrix(wc[1]))
    for load in loads:
        load.wait()

    d1, d2 = FIRST_SPACING, SECOND_SPACING

    def hidden_one(r):
        def post(row, at, pre):
            h1[row, :, at] = masked(elu(pre).astype(BF16), mask, row - HALO, at)

        conv_rows(xe, [r + q for q in range(STEP)], d1, False, wr1, post)

    loop(R + 2 * HALO, STEP, hidden_one)
    save_h1 = pltpu.make_async_copy(h1.at[HALO : HALO + R], h1_out, sems.at[3])
    save_h1.start()

    def block_one(r):
        def post(row, at, col):
            b1[row - d1, :, at] = xe[row, :, at] + masked(col.astype(BF16), mask, row - HALO, at)

        conv_columns(h1, [r + d1 + q for q in range(d1)], d1, wc1, post)

    loop(R + 2 * d2, 2 * d1, block_one)
    save_b1 = pltpu.make_async_copy(b1.at[d2 : d2 + R], b1_out, sems.at[4])
    save_b1.start()

    def hidden_two(r):
        def post(row, at, pre):
            h2[row, :, at] = masked(elu(pre).astype(BF16), mask, row - d2, at)

        conv_rows(b1, [r + q for q in range(STEP)], d2, False, wr2, post)

    loop(R + 2 * d2, STEP, hidden_two)
    save_h2 = pltpu.make_async_copy(h2.at[d2 - d1 : d2 + R + d1], h2_out, sems.at[5])
    save_h2.start()

    def last(i):
        r = (i // d2) * 2 * d2 + i % d2

        def post(row, at, col):
            flat[row - d2, :, at] = b1[row, :, at] + masked(col.astype(BF16), mask, row - d2, at)

        conv_columns(h2, [r + d2 + q for q in range(4)], d2, wc2, post, tail=False)

    loop(R // 2, 4, last)
    turn_out(flat, out)
    save_h1.wait()
    save_b1.wait()
    save_h2.wait()


ANY = pl.BlockSpec(memory_space=pl.ANY)
VM = pl.BlockSpec(memory_space=pltpu.VMEM)
SM = pl.BlockSpec(memory_space=pltpu.SMEM)
STEP = 8


def forward_call(tiles, x, xtop, xbot, col_left, col_right, cor_top, cor_bot, wr, wc):
    d1, d2 = FIRST_SPACING, SECOND_SPACING
    return pl.pallas_call(
        forward_kernel,
        in_specs=[SM, ANY, ANY, ANY, VM, VM, VM, VM, VM, VM],
        out_specs=[VM, ANY, ANY, ANY],
        out_shape=[
            jax.ShapeDtypeStruct((C, R, W), BF16),
            jax.ShapeDtypeStruct((R, C, E), BF16),
            jax.ShapeDtypeStruct((R, C, E), BF16),
            jax.ShapeDtypeStruct((R + 2 * d1, C, E), BF16),
        ],
        scratch_shapes=[
            pltpu.VMEM((R + 2 * HALO, C, E), BF16),
            pltpu.VMEM((R + 2 * HALO, C, E), BF16),
            pltpu.VMEM((R + 2 * d2, C, E), BF16),
            pltpu.VMEM((R + 2 * d2, C, E), BF16),
            pltpu.VMEM((R, C, W), BF16),
            pltpu.VMEM((3, 16, E), BF16),
            pltpu.SemaphoreType.DMA((6,)),
        ],
        compiler_params=pltpu.CompilerParams(vmem_limit_bytes=VMEM_LIMIT),
        cost_estimate=pl.CostEstimate(flops=20_000_000_000, bytes_accessed=20_000_000, transcendentals=0),
        name="forward",
    )(tiles, x, xtop, xbot, col_left, col_right, cor_top, cor_bot, wr, wc)


def backward_kernel(
    tiles, c, ctop, cbot, col_left, col_right, cor_top, cor_bot, wr, wc, x_in, h1_in, b1_in, h2_in,
    out, taps,
    ce, cm, h1, b1, h2, x, a2, cg1, g1, a1, flat, mask, sems,
):
    d1, d2 = FIRST_SPACING, SECOND_SPACING
    loads = [
        pltpu.make_async_copy(c, ce.at[HALO : HALO + R, :, 0:W], sems.at[0]),
        pltpu.make_async_copy(ctop, ce.at[0:HALO, :, 0:W], sems.at[1]),
        pltpu.make_async_copy(cbot, ce.at[HALO + R :, :, 0:W], sems.at[2]),
    ]
    late = [
        pltpu.make_async_copy(h2_in, h2, sems.at[3]),
        pltpu.make_async_copy(b1_in, b1, sems.at[4]),
        pltpu.make_async_copy(h1_in, h1, sems.at[5]),
        pltpu.make_async_copy(x_in, x, sems.at[6]),
    ]
    for load in loads + late:
        load.start()
    build_mask(tiles, mask)
    unpack_all(1, col_left, col_right, cor_top, cor_bot, ce)
    wr1, wr2 = backward_matrix(wr[0]), backward_matrix(wr[1])
    wc1, wc2 = backward_matrix(wc[0], (2, 1, 0)), backward_matrix(wc[1], (2, 1, 0))
    wc1w, wc2w = two_rows(wc1), two_rows(wc2)
    taps[...] = jnp.zeros_like(taps)
    for load in loads:
        load.wait()

    def mask_cot(r):
        for q in range(4):
            cm[r + q] = masked(ce[r + q], mask, r + q - HALO, slice(0, E))

    loop(R + 2 * HALO, 4, mask_cot)
    late[0].wait()

    up = HALO - d1

    def post_two(row, at, hid):
        slope = 1.0 + jnp.minimum(h2[row - up, :, at], 0).astype(F32)
        a2[row - up, :, at] = masked((hid * slope).astype(BF16), mask, row - HALO, at)

    def act_two(i):
        r = (i // d2) * 2 * d2 + i % d2
        conv_columns(cm, [r + up + q for q in range(4)], d2, wc2w, post_two)

    loop(R // 2, 4, act_two)
    conv_columns_single(cm, [R + up + q for q in range(2 * d1)], d2, wc2, post_two)
    late[1].wait()

    def add_taps(k, left, right):
        taps[k] += dot_nt(jnp.concatenate(left, axis=1), jnp.concatenate(right, axis=1))

    own = slice(0, W)

    def col_taps_two(r):
        rows = [r + q for q in range(4)]
        add_taps(0, [col_stack(cm, s + HALO, d2, own) for s in rows], [h2[s + d1, :, own] for s in rows])

    loop(R, 4, col_taps_two)

    def post_one(row, at, mixed):
        g = ce[row + up, :, at].astype(F32) + mixed
        cg1[row, :, at] = masked(g.astype(BF16), mask, row - d1, at)
        if at != TAIL:
            g1[row, :, at] = g

    def grad_one(r):
        rows = [r + q + d1 for q in range(4)]
        stacks = conv_rows(a2, rows, d2, True, wr2, post_one)
        add_taps(1, [s[:, own] for s in stacks], [b1[s - d1, :, own] for s in rows])

    for first in (0, R + d1):
        conv_rows(a2, [first + q for q in range(d1)], d2, True, wr2, post_one)
    loop(R, 4, grad_one)
    late[2].wait()
    late[3].wait()

    def act_one(r):
        def post(row, at, hid):
            slope = 1.0 + jnp.minimum(h1[row - d1, :, at], 0).astype(F32)
            a1[row - d1, :, at] = masked((hid * slope).astype(BF16), mask, row - d1, at)

        rows = [r + q for q in range(2 * d1)]
        conv_columns(cg1, [s + d1 for s in rows[:d1]], d1, wc1w, post)
        add_taps(2, [col_stack(cg1, s + d1, d1, own) for s in rows], [h1[s, :, own] for s in rows])

    loop(R, 2 * d1, act_one)

    def last(r):
        def post(row, at, mixed):
            flat[row, :, at] = (g1[row + d1, :, at] + mixed).astype(BF16)

        rows = [r + q for q in range(4)]
        stacks = conv_rows(a1, rows, d1, True, wr1, post, tail=False)
        add_taps(3, [s[:, own] for s in stacks], [x[s] for s in rows])

    loop(R, 4, last)
    turn_out(flat, out)


def backward_call(tiles, c, ctop, cbot, col_left, col_right, cor_top, cor_bot, wr, wc, x, h1, b1, h2):
    d1 = FIRST_SPACING
    return pl.pallas_call(
        backward_kernel,
        in_specs=[SM, ANY, ANY, ANY, VM, VM, VM, VM, VM, VM, ANY, ANY, ANY, ANY],
        out_specs=[VM, VM],
        out_shape=[
            jax.ShapeDtypeStruct((C, R, W), BF16),
            jax.ShapeDtypeStruct((4, 3 * C, C), F32),
        ],
        scratch_shapes=[
            pltpu.VMEM((R + 2 * HALO, C, E), BF16),
            pltpu.VMEM((R + 2 * HALO, C, E), BF16),
            pltpu.VMEM((R, C, E), BF16),
            pltpu.VMEM((R, C, E), BF16),
            pltpu.VMEM((R + 2 * d1, C, E), BF16),
            pltpu.VMEM((R, C, W), BF16),
            pltpu.VMEM((R + 2 * d1, C, E), BF16),
            pltpu.VMEM((R + 2 * d1, C, E), BF16),
            pltpu.VMEM((R + 2 * d1, C, W), F32),
            pltpu.VMEM((R, C, E), BF16),
            pltpu.VMEM((R, C, W), BF16),
            pltpu.VMEM((3, 16, E), BF16),
            pltpu.SemaphoreType.DMA((7,)),
        ],
        compiler_params=pltpu.CompilerParams(vmem_limit_bytes=VMEM_LIMIT),
        cost_estimate=pl.CostEstimate(flops=20_000_000_000, bytes_accessed=20_000_000, transcendentals=0),
        name="backward",
    )(tiles, c, ctop, cbot, col_left, col_right, cor_top, cor_bot, wr, wc, x, h1, b1, h2)


def tap_sum(taps):
    flat = taps.reshape(-1, 128)
    wide = lax.axis_size("rows")
    part = lax.all_to_all(flat, "rows", 0, 0, tiled=True).reshape(wide, -1, 128).sum(0)
    cols = lax.axis_size("cols")
    spread = jnp.broadcast_to(part[None], (cols,) + part.shape).reshape(-1, 128)
    part = lax.all_to_all(spread, "cols", 0, 0, tiled=True).reshape(cols, -1, 128).sum(0)
    spread = jnp.broadcast_to(part[None], (wide,) + part.shape).reshape(-1, 128)
    whole = lax.all_to_all(spread, "rows", 0, 0, tiled=True)
    return whole.reshape(4, 3, C, C)


def on_device(x, tile_mask, wr, wc, cot):
    n_rows, n_cols = lax.axis_size("rows"), lax.axis_size("cols")
    factor = 1.0 / math.sqrt(R * n_rows * W * n_cols)
    down = [(i, i + 1) for i in range(n_rows - 1)]
    up = [(i + 1, i) for i in range(n_rows - 1)]
    right = [(i, i + 1) for i in range(n_cols - 1)]
    left = [(i + 1, i) for i in range(n_cols - 1)]

    xt, xtop, xbot, to_left, to_right = pack_x(x, cot)
    col_right = lax.ppermute(to_left, "cols", left)
    col_left = lax.ppermute(to_right, "cols", right)
    xabove = lax.ppermute(xbot, "rows", down)
    xbelow = lax.ppermute(xtop, "rows", up)
    first = jnp.stack([col_left[:, :HG], col_right[:, :HG]], axis=1)
    last = jnp.stack([col_left[:, GROUPS - HG :], col_right[:, GROUPS - HG :]], axis=1)
    cor_bot = lax.ppermute(first, "rows", up)
    cor_top = lax.ppermute(last, "rows", down)
    ct, ctop, cbot = turn_c(cot, col_left)
    cabove = lax.ppermute(cbot, "rows", down)
    cbelow = lax.ppermute(ctop, "rows", up)

    final, h1, b1, h2 = forward_call(
        tile_mask, xt, xabove, xbelow, col_left, col_right, cor_top, cor_bot, wr, wc
    )
    map_grad, taps = backward_call(
        tile_mask, ct, cabove, cbelow, col_left, col_right, cor_top, cor_bot, wr, wc, xt, h1, b1, h2
    )
    total = tap_sum(taps) * factor
    row_grad = jnp.stack([total[3], total[1]])
    col_grad = jnp.stack([total[2], total[0]])
    return final, map_grad, row_grad, col_grad


def solution(mesh):
    placed = (P(None, "rows", "cols"), P(), P(), P(), P(None, "rows", "cols"))
    return jax.shard_map(
        on_device,
        mesh=mesh,
        in_specs=placed,
        out_specs=(P(None, "rows", "cols"), P(None, "rows", "cols"), P(), P()),
        check_vma=False,
    )
```

```python
import functools
import math

import jax
import jax.numpy as jnp
from jax import lax
from jax.experimental import pallas as pl
from jax.experimental.pallas import tpu as pltpu
from jax.sharding import Mesh, PartitionSpec as P

FIRST_SPACING = 4
SECOND_SPACING = 8
TILE = 128
C = 64
R = 32
W = 512
E = 640
XHALO = 8
HALO = 12
XEDGE = 32
CEDGE = 16
XTILES = R * XEDGE // 128
CTILES = R * CEDGE // 128
F32 = jnp.float32
BF16 = jnp.bfloat16
VMEM_LIMIT = 60 * 1024 * 1024


def dot(a, b):
    return jnp.dot(a, b, preferred_element_type=F32)


def dot_nt(a, b):
    return lax.dot_general(a, b, (((1,), (1,)), ((), ())), preferred_element_type=F32)


def turn(block):
    return jnp.swapaxes(block, 0, 1)


def lanes(first, count, channels):
    lane = lax.broadcasted_iota(jnp.int32, (channels, 128), 1)
    return ((lane >= first) & (lane < first + count)).astype(F32).astype(BF16)


def rolled(v, shift):
    shift = shift % 128
    return pltpu.roll(v, shift, 1) if shift else v


def pack(rows, width, first):
    keep = lanes(first, width, rows[0].shape[0])
    parts = [rolled(v * keep, width * k - first) for k, v in enumerate(rows)]
    return functools.reduce(jnp.add, parts)


def unpack(left, right, k, width):
    channels = left.shape[0]
    ahead = rolled(right, -width * k) * lanes(0, width, channels)
    behind = rolled(left, 128 - width - width * k) * lanes(128 - width, width, channels)
    return ahead + behind


GC = 16


def edge_kernel(x_low, x_high, c_low, c_high, to_left, to_right):
    for src, width, at in ((x_low, XEDGE, 0), (c_low, CEDGE, XTILES)):
        for i in range(2):
            rows = turn(src[:, i * 16 : (i + 1) * 16, :])
            per = 128 // width
            for g in range(16 // per):
                tile = pack([rows[g * per + k] for k in range(per)], width, 0)
                to_left[at + (i * 16) // per + g] = tile
    for src, width, at in ((x_high, XEDGE, 0), (c_high, CEDGE, XTILES)):
        for i in range(2):
            rows = turn(src[:, i * 16 : (i + 1) * 16, :])
            per = 128 // width
            for g in range(16 // per):
                tile = pack([rows[g * per + k] for k in range(per)], width, 128 - width)
                to_right[at + (i * 16) // per + g] = tile


def pack_edges(x, c):
    low = pl.BlockSpec((GC, R, 128), lambda g: (g, 0, 0))
    high = pl.BlockSpec((GC, R, 128), lambda g: (g, 0, W // 128 - 1))
    out = pl.BlockSpec((XTILES + CTILES, GC, 128), lambda g: (0, g, 0))
    return pl.pallas_call(
        edge_kernel,
        grid=(C // GC,),
        in_specs=[low, high, low, high],
        out_specs=[out, out],
        out_shape=[jax.ShapeDtypeStruct((XTILES + CTILES, C, 128), BF16)] * 2,
        compiler_params=pltpu.CompilerParams(vmem_limit_bytes=VMEM_LIMIT),
        name="pack_edges",
    )(x, x, c, c)


def turn_block(src, dst):
    for i in range(R // 16):
        for t in range(W // 128):
            at = slice(t * 128, (t + 1) * 128)
            dst[i * 16 : (i + 1) * 16, :, at] = turn(src[:, i * 16 : (i + 1) * 16, at])


def turn_x_kernel(x_ref, xt, up, down):
    turn_block(x_ref, xt)
    up[0:XHALO] = xt[0:XHALO]
    down[0:XHALO] = xt[R - XHALO : R]


def turn_c_kernel(c_ref, left, right, ct, up, down):
    turn_block(c_ref, ct)
    up[0:HALO] = ct[0:HALO]
    down[0:HALO] = ct[R - HALO : R]
    for out, first in ((up, XTILES), (down, XTILES + CTILES - 2)):
        tiles = [left[first], left[first + 1], right[first], right[first + 1]]
        out[HALO] = jnp.concatenate(tiles, axis=1)


NATIVE = pl.BlockSpec((GC, R, W), lambda g: (g, 0, 0))
TURNED = pl.BlockSpec((R, GC, W), lambda g: (0, g, 0))


def message(rows):
    return (
        pl.BlockSpec((rows + 1, GC, W), lambda g: (0, g, 0)),
        jax.ShapeDtypeStruct((rows + 1, C, W), BF16),
    )


def turn_x(x):
    spec, shape = message(XHALO)
    return pl.pallas_call(
        turn_x_kernel,
        grid=(C // GC,),
        in_specs=[NATIVE],
        out_specs=[TURNED, spec, spec],
        out_shape=[jax.ShapeDtypeStruct((R, C, W), BF16), shape, shape],
        compiler_params=pltpu.CompilerParams(vmem_limit_bytes=VMEM_LIMIT),
        name="turn_x",
    )(x)


def turn_c(c, left, right):
    spec, shape = message(HALO)
    edges = pl.BlockSpec((XTILES + CTILES, GC, 128), lambda g: (0, g, 0))
    return pl.pallas_call(
        turn_c_kernel,
        grid=(C // GC,),
        in_specs=[NATIVE, edges, edges],
        out_specs=[TURNED, spec, spec],
        out_shape=[jax.ShapeDtypeStruct((R, C, W), BF16), shape, shape],
        compiler_params=pltpu.CompilerParams(vmem_limit_bytes=VMEM_LIMIT),
        name="turn_c",
    )(c, left, right)


def fill_kernel(up_in, down_in, left, right, up, down, rows, sems):
    copies = []
    for q, (out, first) in enumerate(((up, 0), (down, XTILES - 2))):
        tiles = [left[first], left[first + 1], right[first], right[first + 1]]
        rows[q] = jnp.concatenate(tiles, axis=1)
        copies.append(pltpu.make_async_copy(rows.at[q], out.at[XHALO], sems.at[q]))
        copies[-1].start()
    for copy in copies:
        copy.wait()


def fill_x(up, down, left, right):
    shape = jax.ShapeDtypeStruct(up.shape, BF16)
    return pl.pallas_call(
        fill_kernel,
        in_specs=[ANY, ANY, VM, VM],
        out_specs=[ANY, ANY],
        out_shape=[shape, shape],
        input_output_aliases={0: 0, 1: 1},
        scratch_shapes=[pltpu.VMEM((2, C, W), BF16), pltpu.SemaphoreType.DMA((2,))],
        name="fill_x",
    )(up, down, left, right)


ANY = pl.BlockSpec(memory_space=pl.ANY)
VM = pl.BlockSpec(memory_space=pltpu.VMEM)
SM = pl.BlockSpec(memory_space=pltpu.SMEM)
STEP = 8


def build_mask(tiles, mask):
    row_dev, col_dev = lax.axis_index("rows"), lax.axis_index("cols")
    n_rows, n_cols = tiles.shape
    first_row, first_tile = row_dev * R, col_dev * (W // TILE)
    lane = lax.broadcasted_iota(jnp.int32, (16, 128), 1)

    def value(p, ct):
        cell = first_row + (-1, 0, R)[p]
        inside = (cell >= 0) & (cell < n_rows * TILE) & (ct >= 0) & (ct < n_cols)
        rt = jnp.clip(cell, 0, n_rows * TILE - 1) // TILE
        return jnp.where(inside, tiles[rt, jnp.clip(ct, 0, n_cols - 1)], 0)

    for p in range(3):
        for t in range(W // 128):
            cell = jnp.full((16, 128), value(p, first_tile + t), jnp.int32)
            mask[p, :, t * 128 : (t + 1) * 128] = cell.astype(F32).astype(BF16)
        right = jnp.full((16, 128), value(p, first_tile + W // TILE), jnp.int32)
        left = jnp.full((16, 128), value(p, first_tile - 1), jnp.int32)
        mask[p, :, W:E] = jnp.where(lane < 64, right, left).astype(F32).astype(BF16)


def masked(v, mask, r, at):
    if isinstance(r, int):
        p = int(r >= 0) + int(r >= R)
    else:
        p = (r >= 0).astype(jnp.int32) + (r >= R).astype(jnp.int32)
    m = mask[p, :, at]
    return v * jnp.concatenate([m] * (C // 16), axis=0)


def shifted(v, d):
    return pltpu.roll(v, (-d) % v.shape[1], 1)


def row_stack(v, d, reverse):
    ahead, behind = shifted(v, d), shifted(v, -d)
    parts = [ahead, v, behind] if reverse else [behind, v, ahead]
    return jnp.concatenate(parts, axis=0)


def col_stack(ref, r, d, at):
    return jnp.concatenate([ref[r + d, :, at], ref[r, :, at], ref[r - d, :, at]], axis=0)


def forward_matrix(w):
    return jnp.concatenate([w[j].astype(F32).T for j in range(3)], axis=0).T.astype(BF16)


def backward_matrix(w, order=(0, 1, 2)):
    return jnp.concatenate([w[j].astype(F32) for j in order], axis=0).T.astype(BF16)


def two_rows(matrix):
    none = jnp.zeros((C, C), BF16)
    return jnp.concatenate(
        [jnp.concatenate([matrix, none], axis=1), jnp.concatenate([none, matrix], axis=1)], axis=0
    )


MAIN = (slice(0, 256), slice(256, 512))
TAIL = slice(W, E)


def loop(count, step, body):
    def one(i, _):
        body(i * step)
        return 0

    lax.fori_loop(0, count // step, one, 0)


def conv_columns(ref, rows, d, matrix, post, tail=True):
    def window(r, at):
        return jnp.concatenate([ref[r + k * d, :, at] for k in (-1, 0, 1, 2)], axis=0)

    for r in rows:
        for at in MAIN:
            both = dot(matrix, window(r, at))
            post(r, at, both[:C])
            post(r + d, at, both[C:])
    if tail:
        for r, s in zip(rows[::2], rows[1::2]):
            both = dot(matrix, jnp.concatenate([window(r, TAIL), window(s, TAIL)], axis=1))
            for row, half in ((r, both[:, :128]), (s, both[:, 128:])):
                post(row, TAIL, half[:C])
                post(row + d, TAIL, half[C:])


def conv_columns_single(ref, rows, d, matrix, post):
    def window(r, at):
        return jnp.concatenate([ref[r + k * d, :, at] for k in (-1, 0, 1)], axis=0)

    for r in rows:
        for at in MAIN:
            post(r, at, dot(matrix, window(r, at)))
    for r, s in zip(rows[::2], rows[1::2]):
        both = dot(matrix, jnp.concatenate([window(r, TAIL), window(s, TAIL)], axis=1))
        post(r, TAIL, both[:, :128])
        post(s, TAIL, both[:, 128:])


def conv_rows(ref, rows, d, reverse, matrix, post, tail=True):
    stacks = []
    for r in rows:
        stack = row_stack(ref[r], d, reverse)
        stacks.append(stack)
        for at in MAIN:
            post(r, at, dot(matrix, stack[:, at]))
    if tail:
        for q in range(0, len(rows), 2):
            both = dot(matrix, jnp.concatenate([stacks[q][:, TAIL], stacks[q + 1][:, TAIL]], axis=1))
            post(rows[q], TAIL, both[:, :128])
            post(rows[q + 1], TAIL, both[:, 128:])
    return stacks


def elu(p):
    return jnp.where(p > 0, p, jnp.exp(p) - 1.0)


def turn_out(src, out):
    for i in range(R // 16):
        for t in range(W // 128):
            at = slice(t * 128, (t + 1) * 128)
            out[:, i * 16 : (i + 1) * 16, at] = turn(src[i * 16 : (i + 1) * 16, :, at])


def call(kernel, name, in_specs, outs, scratch, cost, *args):
    return pl.pallas_call(
        kernel,
        in_specs=in_specs,
        out_specs=[spec for spec, _, _ in outs],
        out_shape=[jax.ShapeDtypeStruct(shape, dtype) for _, shape, dtype in outs],
        scratch_shapes=scratch,
        compiler_params=pltpu.CompilerParams(vmem_limit_bytes=VMEM_LIMIT),
        cost_estimate=pl.CostEstimate(flops=cost * 500_000_000, bytes_accessed=cost * 1_000_000, transcendentals=0),
        name=name,
    )(*args)


INNER = R - 2 * FIRST_SPACING


def inner_kernel(
    tiles, x, left, right, wr, wc,
    x_out, h1_out, b1_out, h2_out, up_out, down_out,
    xe, h1, b1, h2, mask, sems,
):
    d1, d2 = FIRST_SPACING, SECOND_SPACING
    load = pltpu.make_async_copy(x, xe.at[:, :, 0:W], sems.at[0])
    load.start()
    build_mask(tiles, mask)
    per = 128 // XEDGE

    def edges(g, _):
        for k in range(per):
            xe[g * per + k, :, TAIL] = unpack(left[g], right[g], k, XEDGE)
        return 0

    lax.fori_loop(0, XTILES, edges, 0)
    wr1, wr2 = forward_matrix(wr[0]), forward_matrix(wr[1])
    wc1 = two_rows(forward_matrix(wc[0]))
    load.wait()
    saves = [
        pltpu.make_async_copy(xe.at[0 : 2 * d1], x_out.at[0], sems.at[1]),
        pltpu.make_async_copy(xe.at[R - 2 * d1 : R], x_out.at[1], sems.at[2]),
    ]
    for save in saves:
        save.start()

    def hidden_one(r):
        def post(row, at, pre):
            h1[row, :, at] = masked(elu(pre).astype(BF16), mask, row, at)

        conv_rows(xe, [r + q for q in range(STEP)], d1, False, wr1, post)

    loop(R, STEP, hidden_one)
    saves.append(pltpu.make_async_copy(h1, h1_out, sems.at[3]))
    saves[-1].start()

    def block_one(r):
        def post(row, at, col):
            b1[row - d1, :, at] = xe[row, :, at] + masked(col.astype(BF16), mask, row, at)

        conv_columns(h1, [r + d1 + q for q in range(d1)], d1, wc1, post)

    loop(INNER, 2 * d1, block_one)
    saves.append(pltpu.make_async_copy(b1, b1_out, sems.at[4]))
    saves[-1].start()

    def hidden_two(r):
        def post(row, at, pre):
            h2[row, :, at] = masked(elu(pre).astype(BF16), mask, row + d1, at)

        conv_rows(b1, [r + q for q in range(STEP)], d2, False, wr2, post)

    loop(INNER, STEP, hidden_two)
    saves.append(pltpu.make_async_copy(h2, h2_out, sems.at[5]))
    saves.append(pltpu.make_async_copy(h2.at[0 : d2 - d1, :, 0:W], up_out, sems.at[6]))
    saves.append(pltpu.make_async_copy(h2.at[INNER - (d2 - d1) : INNER, :, 0:W], down_out, sems.at[7]))
    for save in saves[-3:]:
        save.start()
    for save in saves:
        save.wait()


def forward_inner(*args):
    d1, d2 = FIRST_SPACING, SECOND_SPACING
    return call(
        inner_kernel, "forward_inner", [SM, ANY, VM, VM, VM, VM],
        [
            (ANY, (2, 2 * d1, C, E), BF16),
            (ANY, (R, C, E), BF16),
            (ANY, (INNER, C, E), BF16),
            (ANY, (INNER, C, E), BF16),
            (ANY, (d2 - d1, C, W), BF16),
            (ANY, (d2 - d1, C, W), BF16),
        ],
        [
            pltpu.VMEM((R, C, E), BF16),
            pltpu.VMEM((R, C, E), BF16),
            pltpu.VMEM((INNER, C, E), BF16),
            pltpu.VMEM((INNER, C, E), BF16),
            pltpu.VMEM((3, 16, E), BF16),
            pltpu.SemaphoreType.DMA((8,)),
        ],
        10, *args,
    )


def outer_kernel(
    tiles, above, below, x_in, h1_in, wr, wc,
    b1_out, h2_out,
    x, h1, b1, h2, mask, sems,
):
    d1, d2 = FIRST_SPACING, SECOND_SPACING
    n = 2 * d1
    loads = [
        pltpu.make_async_copy(above.at[0:XHALO], x.at[0, 0:n, :, 0:W], sems.at[0]),
        pltpu.make_async_copy(below.at[0:XHALO], x.at[1, n : 2 * n, :, 0:W], sems.at[1]),
        pltpu.make_async_copy(x_in.at[0], x.at[0, n : 2 * n], sems.at[2]),
        pltpu.make_async_copy(x_in.at[1], x.at[1, 0:n], sems.at[3]),
        pltpu.make_async_copy(h1_in.at[0:n], h1.at[0, n : 2 * n], sems.at[4]),
        pltpu.make_async_copy(h1_in.at[R - n : R], h1.at[1, 0:n], sems.at[5]),
    ]
    edge_rows = pltpu.VMEM((2, C, W), BF16)
    for load in loads:
        load.start()
    build_mask(tiles, mask)

    def with_edges(packed, sem):
        gets = [
            pltpu.make_async_copy(above.at[XHALO], packed.at[0], sem.at[0]),
            pltpu.make_async_copy(below.at[XHALO], packed.at[1], sem.at[1]),
        ]
        for get in gets:
            get.start()
        for get in gets:
            get.wait()
        per = 128 // XEDGE
        for side in range(2):
            tile = [packed[side, :, t * 128 : (t + 1) * 128] for t in range(4)]
            for q in range(XHALO):
                x[side, side * n + q, :, TAIL] = unpack(tile[q // per], tile[2 + q // per], q % per, XEDGE)

    pl.run_scoped(with_edges, edge_rows, pltpu.SemaphoreType.DMA((2,)))
    wr1, wr2 = forward_matrix(wr[0]), forward_matrix(wr[1])
    wc1 = two_rows(forward_matrix(wc[0]))
    for load in loads:
        load.wait()

    def side_step(side, _):
        first = side * R - n

        def post_h1(row, at, pre):
            h1[side, row, :, at] = masked(elu(pre).astype(BF16), mask, row + first, at)

        conv_rows(x.at[side], [side * n + q for q in range(n)], d1, False, wr1, post_h1)
        return 0

    def side_next(side, _):
        first = side * R - n

        def post_b1(row, at, col):
            kept = masked(col.astype(BF16), mask, row + first, at)
            b1[side, row - d1, :, at] = x[side, row, :, at] + kept

        conv_columns(h1.at[side], [d1 + q for q in range(d1)], d1, wc1, post_b1)
        return 0

    def side_last(side, _):
        first = side * R - d1

        def post_h2(row, at, pre):
            h2[side, row, :, at] = masked(elu(pre).astype(BF16), mask, row + first, at)

        conv_rows(b1.at[side], [q for q in range(n)], d2, False, wr2, post_h2)
        return 0

    lax.fori_loop(0, 2, side_step, 0)
    lax.fori_loop(0, 2, side_next, 0)
    lax.fori_loop(0, 2, side_last, 0)
    saves = [pltpu.make_async_copy(b1, b1_out, sems.at[6]), pltpu.make_async_copy(h2, h2_out, sems.at[7])]
    for save in saves:
        save.start()
    for save in saves:
        save.wait()


def forward_outer(*args):
    n = 2 * FIRST_SPACING
    return call(
        outer_kernel, "forward_outer", [SM, ANY, ANY, ANY, ANY, VM, VM],
        [(ANY, (2, n, C, E), BF16), (ANY, (2, n, C, E), BF16)],
        [
            pltpu.VMEM((2, 2 * n, C, E), BF16),
            pltpu.VMEM((2, 2 * n, C, E), BF16),
            pltpu.VMEM((2, n, C, E), BF16),
            pltpu.VMEM((2, n, C, E), BF16),
            pltpu.VMEM((3, 16, E), BF16),
            pltpu.SemaphoreType.DMA((8,)),
        ],
        7, *args,
    )


def final_kernel(
    tiles, above, below, b1_in, b1_side, h2_in, h2_side, wc,
    out,
    b1, h2, flat, mask, sems,
):
    d1, d2 = FIRST_SPACING, SECOND_SPACING
    n, far, own = 2 * d1, d2 - d1, slice(0, W)
    loads = [
        pltpu.make_async_copy(above, h2.at[0:far], sems.at[0]),
        pltpu.make_async_copy(h2_side.at[0, :, :, own], h2.at[far : far + n], sems.at[1]),
        pltpu.make_async_copy(h2_in.at[:, :, own], h2.at[far + n : far + n + INNER], sems.at[2]),
        pltpu.make_async_copy(h2_side.at[1, :, :, own], h2.at[far + n + INNER : R + 2 * d2 - far], sems.at[3]),
        pltpu.make_async_copy(below, h2.at[R + 2 * d2 - far : R + 2 * d2], sems.at[4]),
        pltpu.make_async_copy(b1_side.at[0, d1:n, :, own], b1.at[0:d1], sems.at[5]),
        pltpu.make_async_copy(b1_in.at[:, :, own], b1.at[d1 : R - d1], sems.at[6]),
        pltpu.make_async_copy(b1_side.at[1, 0:d1, :, own], b1.at[R - d1 : R], sems.at[7]),
    ]
    for load in loads:
        load.start()
    build_mask(tiles, mask)
    wc2 = two_rows(forward_matrix(wc[1]))
    for load in loads:
        load.wait()

    def last(i):
        r = (i // d2) * 2 * d2 + i % d2

        def post(row, at, col):
            flat[row - d2, :, at] = b1[row - d2, :, at] + masked(col.astype(BF16), mask, row - d2, at)

        conv_columns(h2, [r + d2 + q for q in range(4)], d2, wc2, post, tail=False)

    loop(R // 2, 4, last)
    turn_out(flat, out)


def forward_final(*args):
    return call(
        final_kernel, "forward_final", [SM, ANY, ANY, ANY, ANY, ANY, ANY, VM],
        [(VM, (C, R, W), BF16)],
        [
            pltpu.VMEM((R, C, W), BF16),
            pltpu.VMEM((R + 2 * SECOND_SPACING, C, W), BF16),
            pltpu.VMEM((R, C, W), BF16),
            pltpu.VMEM((3, 16, E), BF16),
            pltpu.SemaphoreType.DMA((8,)),
        ],
        4, *args,
    )[0]


def backward_kernel(
    tiles, c, above, below, left, right, wr, wc, x_in, h1_in, b1_in, b1_side, h2_in, h2_side,
    out, taps,
    packed, ce, cm, h1, b1, h2, x, a2, cg1, g1, a1, flat, mask, sems,
):
    d1, d2 = FIRST_SPACING, SECOND_SPACING
    n = 2 * d1
    loads = [
        pltpu.make_async_copy(c, ce.at[HALO : HALO + R, :, 0:W], sems.at[0]),
        pltpu.make_async_copy(above.at[0:HALO], ce.at[0:HALO, :, 0:W], sems.at[1]),
        pltpu.make_async_copy(below.at[0:HALO], ce.at[HALO + R :, :, 0:W], sems.at[2]),
        pltpu.make_async_copy(above.at[HALO], packed.at[0], sems.at[7]),
        pltpu.make_async_copy(below.at[HALO], packed.at[1], sems.at[8]),
    ]
    late = [
        pltpu.make_async_copy(h2_side.at[0], h2.at[0:n], sems.at[3]),
        pltpu.make_async_copy(h2_in, h2.at[n : n + INNER], sems.at[9]),
        pltpu.make_async_copy(h2_side.at[1], h2.at[n + INNER : R + n], sems.at[10]),
        pltpu.make_async_copy(b1_side.at[0, d1:n], b1.at[0:d1], sems.at[4]),
        pltpu.make_async_copy(b1_in, b1.at[d1 : R - d1], sems.at[11]),
        pltpu.make_async_copy(b1_side.at[1, 0:d1], b1.at[R - d1 : R], sems.at[12]),
        pltpu.make_async_copy(h1_in, h1, sems.at[5]),
        pltpu.make_async_copy(x_in, x, sems.at[6]),
    ]
    for load in loads + late:
        load.start()
    build_mask(tiles, mask)
    per = 128 // CEDGE

    def edges(g, _):
        for k in range(per):
            ce[HALO + g * per + k, :, TAIL] = unpack(left[XTILES + g], right[XTILES + g], k, CEDGE)
        return 0

    lax.fori_loop(0, CTILES, edges, 0)
    wr1, wr2 = backward_matrix(wr[0]), backward_matrix(wr[1])
    wc1, wc2 = backward_matrix(wc[0], (2, 1, 0)), backward_matrix(wc[1], (2, 1, 0))
    wc1w, wc2w = two_rows(wc1), two_rows(wc2)
    taps[...] = jnp.zeros_like(taps)
    for load in loads:
        load.wait()
    for side, first, skip in ((0, 0, 2 * per - HALO), (1, HALO + R, 0)):
        tile = [packed[side, :, t * 128 : (t + 1) * 128] for t in range(4)]
        for q in range(HALO):
            g, k = divmod(q + skip, per)
            ce[first + q, :, TAIL] = unpack(tile[g], tile[2 + g], k, CEDGE)

    def mask_cot(r):
        for q in range(4):
            cm[r + q] = masked(ce[r + q], mask, r + q - HALO, slice(0, E))

    loop(R + 2 * HALO, 4, mask_cot)
    for load in late[0:3]:
        load.wait()

    up = HALO - d1

    def post_two(row, at, hid):
        slope = 1.0 + jnp.minimum(h2[row - up, :, at], 0).astype(F32)
        a2[row - up, :, at] = masked((hid * slope).astype(BF16), mask, row - HALO, at)

    def act_two(i):
        r = (i // d2) * 2 * d2 + i % d2
        conv_columns(cm, [r + up + q for q in range(4)], d2, wc2w, post_two)

    loop(R // 2, 4, act_two)
    conv_columns_single(cm, [R + up + q for q in range(2 * d1)], d2, wc2, post_two)
    for load in late[3:6]:
        load.wait()

    def add_taps(k, left, right):
        taps[k] += dot_nt(jnp.concatenate(left, axis=1), jnp.concatenate(right, axis=1))

    own = slice(0, W)

    def col_taps_two(r):
        rows = [r + q for q in range(4)]
        add_taps(0, [col_stack(cm, s + HALO, d2, own) for s in rows], [h2[s + d1, :, own] for s in rows])

    loop(R, 4, col_taps_two)

    def post_one(row, at, mixed):
        g = ce[row + up, :, at].astype(F32) + mixed
        cg1[row, :, at] = masked(g.astype(BF16), mask, row - d1, at)
        if at != TAIL:
            g1[row, :, at] = g

    def grad_one(r):
        rows = [r + q + d1 for q in range(4)]
        stacks = conv_rows(a2, rows, d2, True, wr2, post_one)
        add_taps(1, [s[:, own] for s in stacks], [b1[s - d1, :, own] for s in rows])

    for first in (0, R + d1):
        conv_rows(a2, [first + q for q in range(d1)], d2, True, wr2, post_one)
    loop(R, 4, grad_one)
    for load in late[6:8]:
        load.wait()

    def act_one(r):
        def post(row, at, hid):
            slope = 1.0 + jnp.minimum(h1[row - d1, :, at], 0).astype(F32)
            a1[row - d1, :, at] = masked((hid * slope).astype(BF16), mask, row - d1, at)

        rows = [r + q for q in range(2 * d1)]
        conv_columns(cg1, [s + d1 for s in rows[:d1]], d1, wc1w, post)
        add_taps(2, [col_stack(cg1, s + d1, d1, own) for s in rows], [h1[s, :, own] for s in rows])

    loop(R, 2 * d1, act_one)

    def last(r):
        def post(row, at, mixed):
            flat[row, :, at] = (g1[row + d1, :, at] + mixed).astype(BF16)

        rows = [r + q for q in range(4)]
        stacks = conv_rows(a1, rows, d1, True, wr1, post, tail=False)
        add_taps(3, [s[:, own] for s in stacks], [x[s] for s in rows])

    loop(R, 4, last)
    turn_out(flat, out)


def backward(*args):
    n = 2 * FIRST_SPACING
    return call(
        backward_kernel, "backward", [SM, ANY, ANY, ANY, VM, VM, VM, VM] + [ANY] * 6,
        [(VM, (C, R, W), BF16), (VM, (4, 3 * C, C), F32)],
        [
            pltpu.VMEM((2, C, W), BF16),
            pltpu.VMEM((R + 2 * HALO, C, E), BF16),
            pltpu.VMEM((R + 2 * HALO, C, E), BF16),
            pltpu.VMEM((R, C, E), BF16),
            pltpu.VMEM((R, C, E), BF16),
            pltpu.VMEM((R + n, C, E), BF16),
            pltpu.VMEM((R, C, W), BF16),
            pltpu.VMEM((R + n, C, E), BF16),
            pltpu.VMEM((R + n, C, E), BF16),
            pltpu.VMEM((R + n, C, W), F32),
            pltpu.VMEM((R, C, E), BF16),
            pltpu.VMEM((R, C, W), BF16),
            pltpu.VMEM((3, 16, E), BF16),
            pltpu.SemaphoreType.DMA((13,)),
        ],
        25, *args,
    )


def tap_sum(taps):
    flat = taps.reshape(-1, 128)
    wide = lax.axis_size("rows")
    part = lax.all_to_all(flat, "rows", 0, 0, tiled=True).reshape(wide, -1, 128).sum(0)
    cols = lax.axis_size("cols")
    spread = jnp.broadcast_to(part[None], (cols,) + part.shape).reshape(-1, 128)
    part = lax.all_to_all(spread, "cols", 0, 0, tiled=True).reshape(cols, -1, 128).sum(0)
    spread = jnp.broadcast_to(part[None], (wide,) + part.shape).reshape(-1, 128)
    whole = lax.all_to_all(spread, "rows", 0, 0, tiled=True)
    return whole.reshape(4, 3, C, C)


def on_device(x, tile_mask, wr, wc, cot):
    n_rows, n_cols = lax.axis_size("rows"), lax.axis_size("cols")
    factor = 1.0 / math.sqrt(R * n_rows * W * n_cols)
    down = [(i, i + 1) for i in range(n_rows - 1)]
    up = [(i + 1, i) for i in range(n_rows - 1)]
    right = [(i, i + 1) for i in range(n_cols - 1)]
    left = [(i + 1, i) for i in range(n_cols - 1)]

    to_left, to_right = pack_edges(x, cot)
    from_right = lax.ppermute(to_left, "cols", left)
    from_left = lax.ppermute(to_right, "cols", right)
    xt, x_up, x_down = turn_x(x)
    x_up, x_down = fill_x(x_up, x_down, from_left, from_right)
    x_above = lax.ppermute(x_down, "rows", down)
    x_below = lax.ppermute(x_up, "rows", up)
    ct, c_up, c_down = turn_c(cot, from_left, from_right)
    c_above = lax.ppermute(c_down, "rows", down)
    c_below = lax.ppermute(c_up, "rows", up)

    x_side, h1, b1, h2, h2_up, h2_down = forward_inner(tile_mask, xt, from_left, from_right, wr, wc)
    h2_above = lax.ppermute(h2_down, "rows", down)
    h2_below = lax.ppermute(h2_up, "rows", up)
    b1_side, h2_side = forward_outer(tile_mask, x_above, x_below, x_side, h1, wr, wc)
    map_grad, taps = backward(
        tile_mask, ct, c_above, c_below, from_left, from_right, wr, wc, xt, h1, b1, b1_side, h2, h2_side
    )
    final = forward_final(tile_mask, h2_above, h2_below, b1, b1_side, h2, h2_side, wc)
    total = tap_sum(taps) * factor
    row_grad = jnp.stack([total[3], total[1]])
    col_grad = jnp.stack([total[2], total[0]])
    return final, map_grad, row_grad, col_grad


def solution(mesh):
    placed = (P(None, "rows", "cols"), P(), P(), P(), P(None, "rows", "cols"))
    return jax.shard_map(
        on_device,
        mesh=mesh,
        in_specs=placed,
        out_specs=(P(None, "rows", "cols"), P(None, "rows", "cols"), P(), P()),
        check_vma=False,
    )
```

```python
import functools
import math

import jax
import jax.numpy as jnp
from jax import lax
from jax.experimental import pallas as pl
from jax.experimental.pallas import tpu as pltpu
from jax.sharding import Mesh, PartitionSpec as P

FIRST_SPACING = 4
SECOND_SPACING = 8
TILE = 128
C = 64
R = 32
W = 512
E = 640
XHALO = 8
HALO = 12
XEDGE = 32
CEDGE = 16
XTILES = R * XEDGE // 128
CTILES = R * CEDGE // 128
F32 = jnp.float32
BF16 = jnp.bfloat16
VMEM_LIMIT = 60 * 1024 * 1024


def dot(a, b):
    return jnp.dot(a, b, preferred_element_type=F32)


def dot_nt(a, b):
    return lax.dot_general(a, b, (((1,), (1,)), ((), ())), preferred_element_type=F32)


def turn(block):
    return jnp.swapaxes(block, 0, 1)


def lanes(first, count, channels):
    lane = lax.broadcasted_iota(jnp.int32, (channels, 128), 1)
    return ((lane >= first) & (lane < first + count)).astype(F32).astype(BF16)


def rolled(v, shift):
    shift = shift % 128
    return pltpu.roll(v, shift, 1) if shift else v


def pack(rows, width, first):
    keep = lanes(first, width, rows[0].shape[0])
    parts = [rolled(v * keep, width * k - first) for k, v in enumerate(rows)]
    return functools.reduce(jnp.add, parts)


def unpack(left, right, k, width):
    channels = left.shape[0]
    ahead = rolled(right, -width * k) * lanes(0, width, channels)
    behind = rolled(left, 128 - width - width * k) * lanes(128 - width, width, channels)
    return ahead + behind


GC = 16


def edge_kernel(x_low, x_high, c_low, c_high, to_left, to_right):
    for src, width, at in ((x_low, XEDGE, 0), (c_low, CEDGE, XTILES)):
        for i in range(2):
            rows = turn(src[:, i * 16 : (i + 1) * 16, :])
            per = 128 // width
            for g in range(16 // per):
                tile = pack([rows[g * per + k] for k in range(per)], width, 0)
                to_left[at + (i * 16) // per + g] = tile
    for src, width, at in ((x_high, XEDGE, 0), (c_high, CEDGE, XTILES)):
        for i in range(2):
            rows = turn(src[:, i * 16 : (i + 1) * 16, :])
            per = 128 // width
            for g in range(16 // per):
                tile = pack([rows[g * per + k] for k in range(per)], width, 128 - width)
                to_right[at + (i * 16) // per + g] = tile


def pack_edges(x, c):
    low = pl.BlockSpec((GC, R, 128), lambda g: (g, 0, 0))
    high = pl.BlockSpec((GC, R, 128), lambda g: (g, 0, W // 128 - 1))
    out = pl.BlockSpec((XTILES + CTILES, GC, 128), lambda g: (0, g, 0))
    return pl.pallas_call(
        edge_kernel,
        grid=(C // GC,),
        in_specs=[low, high, low, high],
        out_specs=[out, out],
        out_shape=[jax.ShapeDtypeStruct((XTILES + CTILES, C, 128), BF16)] * 2,
        compiler_params=pltpu.CompilerParams(vmem_limit_bytes=VMEM_LIMIT),
        name="pack_edges",
    )(x, x, c, c)


def turn_block(src, dst):
    for i in range(R // 16):
        for t in range(W // 128):
            at = slice(t * 128, (t + 1) * 128)
            dst[i * 16 : (i + 1) * 16, :, at] = turn(src[:, i * 16 : (i + 1) * 16, at])


def turn_kernel(x_ref, c_ref, xt, x_up, x_down, ct, c_up, c_down):
    for src, dst, up, down, halo in ((x_ref, xt, x_up, x_down, XHALO), (c_ref, ct, c_up, c_down, HALO)):
        turn_block(src, dst)
        up[0:halo] = dst[0:halo]
        down[0:halo] = dst[R - halo : R]


def message(rows):
    return (
        pl.BlockSpec((rows + 1, GC, W), lambda g: (0, g, 0)),
        jax.ShapeDtypeStruct((rows + 1, C, W), BF16),
    )


def turn_both(x, c):
    native = pl.BlockSpec((GC, R, W), lambda g: (g, 0, 0))
    turned = pl.BlockSpec((R, GC, W), lambda g: (0, g, 0))
    block = jax.ShapeDtypeStruct((R, C, W), BF16)
    (xs, x_shape), (cs, c_shape) = message(XHALO), message(HALO)
    return pl.pallas_call(
        turn_kernel,
        grid=(C // GC,),
        in_specs=[native, native],
        out_specs=[turned, xs, xs, turned, cs, cs],
        out_shape=[block, x_shape, x_shape, block, c_shape, c_shape],
        compiler_params=pltpu.CompilerParams(vmem_limit_bytes=VMEM_LIMIT),
        name="turn_both",
    )(x, c)


def fill_kernel(x_up_in, x_down_in, c_up_in, c_down_in, left, right, x_up, x_down, c_up, c_down, rows, sems):
    copies = []
    for q, (out, first, at) in enumerate((
        (x_up, 0, XHALO),
        (x_down, XTILES - 2, XHALO),
        (c_up, XTILES, HALO),
        (c_down, XTILES + CTILES - 2, HALO),
    )):
        tiles = [left[first], left[first + 1], right[first], right[first + 1]]
        rows[q] = jnp.concatenate(tiles, axis=1)
        copies.append(pltpu.make_async_copy(rows.at[q], out.at[at], sems.at[q]))
        copies[-1].start()
    for copy in copies:
        copy.wait()


def fill(messages, left, right):
    return pl.pallas_call(
        fill_kernel,
        in_specs=[ANY] * 4 + [VM, VM],
        out_specs=[ANY] * 4,
        out_shape=[jax.ShapeDtypeStruct(m.shape, BF16) for m in messages],
        input_output_aliases={q: q for q in range(4)},
        scratch_shapes=[pltpu.VMEM((4, C, W), BF16), pltpu.SemaphoreType.DMA((4,))],
        name="fill_messages",
    )(*messages, left, right)


ANY = pl.BlockSpec(memory_space=pl.ANY)
VM = pl.BlockSpec(memory_space=pltpu.VMEM)
SM = pl.BlockSpec(memory_space=pltpu.SMEM)
STEP = 8


def build_mask(tiles, mask):
    row_dev, col_dev = lax.axis_index("rows"), lax.axis_index(COLS)
    n_rows, n_cols = tiles.shape
    first_row, first_tile = row_dev * R, col_dev * (W // TILE)
    lane = lax.broadcasted_iota(jnp.int32, (16, 128), 1)

    def value(p, ct):
        cell = first_row + (-1, 0, R)[p]
        inside = (cell >= 0) & (cell < n_rows * TILE) & (ct >= 0) & (ct < n_cols)
        rt = jnp.clip(cell, 0, n_rows * TILE - 1) // TILE
        return jnp.where(inside, tiles[rt, jnp.clip(ct, 0, n_cols - 1)], 0)

    for p in range(3):
        for t in range(W // 128):
            cell = jnp.full((16, 128), value(p, first_tile + t), jnp.int32)
            mask[p, :, t * 128 : (t + 1) * 128] = cell.astype(F32).astype(BF16)
        right = jnp.full((16, 128), value(p, first_tile + W // TILE), jnp.int32)
        left = jnp.full((16, 128), value(p, first_tile - 1), jnp.int32)
        mask[p, :, W:E] = jnp.where(lane < 64, right, left).astype(F32).astype(BF16)


def masked(v, mask, r, at):
    if isinstance(r, int):
        p = int(r >= 0) + int(r >= R)
    else:
        p = (r >= 0).astype(jnp.int32) + (r >= R).astype(jnp.int32)
    m = mask[p, :, at]
    return v * jnp.concatenate([m] * (C // 16), axis=0)


def shifted(v, d):
    return pltpu.roll(v, (-d) % v.shape[1], 1)


def row_stack(v, d, reverse):
    ahead, behind = shifted(v, d), shifted(v, -d)
    parts = [ahead, v, behind] if reverse else [behind, v, ahead]
    return jnp.concatenate(parts, axis=0)


def forward_matrix(w):
    return jnp.concatenate([w[j].astype(F32).T for j in range(3)], axis=0).T.astype(BF16)


def backward_matrix(w, order=(0, 1, 2)):
    return jnp.concatenate([w[j].astype(F32) for j in order], axis=0).T.astype(BF16)


def two_rows(matrix):
    none = jnp.zeros((C, C), BF16)
    return jnp.concatenate(
        [jnp.concatenate([matrix, none], axis=1), jnp.concatenate([none, matrix], axis=1)], axis=0
    )


MAIN = (slice(0, 256), slice(256, 512))
TAIL = slice(W, E)


def loop(count, step, body):
    def one(i, _):
        body(i * step)
        return 0

    lax.fori_loop(0, count // step, one, 0)


def conv_columns(ref, rows, d, matrix, post, tail=True):
    def window(r, at):
        return jnp.concatenate([ref[r + k * d, :, at] for k in (-1, 0, 1, 2)], axis=0)

    for r in rows:
        for at in MAIN:
            both = dot(matrix, window(r, at))
            post(r, at, both[:C])
            post(r + d, at, both[C:])
    if tail:
        for r, s in zip(rows[::2], rows[1::2]):
            both = dot(matrix, jnp.concatenate([window(r, TAIL), window(s, TAIL)], axis=1))
            for row, half in ((r, both[:, :128]), (s, both[:, 128:])):
                post(row, TAIL, half[:C])
                post(row + d, TAIL, half[C:])


def conv_columns_single(ref, rows, d, matrix, post):
    def window(r, at):
        return jnp.concatenate([ref[r + k * d, :, at] for k in (-1, 0, 1)], axis=0)

    for r in rows:
        for at in MAIN:
            post(r, at, dot(matrix, window(r, at)))
    for r, s in zip(rows[::2], rows[1::2]):
        both = dot(matrix, jnp.concatenate([window(r, TAIL), window(s, TAIL)], axis=1))
        post(r, TAIL, both[:, :128])
        post(s, TAIL, both[:, 128:])


def conv_rows(ref, rows, d, reverse, matrix, post, tail=True):
    stacks = []
    for r in rows:
        stack = row_stack(ref[r], d, reverse)
        stacks.append(stack)
        for at in MAIN:
            post(r, at, dot(matrix, stack[:, at]))
    if tail:
        for q in range(0, len(rows), 2):
            both = dot(matrix, jnp.concatenate([stacks[q][:, TAIL], stacks[q + 1][:, TAIL]], axis=1))
            post(rows[q], TAIL, both[:, :128])
            post(rows[q + 1], TAIL, both[:, 128:])
    return stacks


def elu(p):
    return jnp.where(p > 0, p, jnp.exp(p) - 1.0)


def turn_out(src, out):
    for i in range(R // 16):
        for t in range(W // 128):
            at = slice(t * 128, (t + 1) * 128)
            out[:, i * 16 : (i + 1) * 16, at] = turn(src[i * 16 : (i + 1) * 16, :, at])


def call(kernel, name, in_specs, outs, scratch, cost, *args):
    return pl.pallas_call(
        kernel,
        in_specs=in_specs,
        out_specs=[spec for spec, _, _ in outs],
        out_shape=[jax.ShapeDtypeStruct(shape, dtype) for _, shape, dtype in outs],
        scratch_shapes=scratch,
        compiler_params=pltpu.CompilerParams(vmem_limit_bytes=VMEM_LIMIT),
        cost_estimate=pl.CostEstimate(flops=cost * 500_000_000, bytes_accessed=cost * 1_000_000, transcendentals=0),
        name=name,
    )(*args)


INNER = R - 2 * FIRST_SPACING


def inner_kernel(
    tiles, x, left, right, wr, wc,
    x_out, h1_out, b1_out, h2_out, up_out, down_out,
    xe, h1, b1, h2, mask, sems,
):
    d1, d2 = FIRST_SPACING, SECOND_SPACING
    load = pltpu.make_async_copy(x, xe.at[:, :, 0:W], sems.at[0])
    load.start()
    build_mask(tiles, mask)
    per = 128 // XEDGE

    def edges(g, _):
        for k in range(per):
            xe[g * per + k, :, TAIL] = unpack(left[g], right[g], k, XEDGE)
        return 0

    lax.fori_loop(0, XTILES, edges, 0)
    wr1, wr2 = forward_matrix(wr[0]), forward_matrix(wr[1])
    wc1 = two_rows(forward_matrix(wc[0]))
    load.wait()
    saves = [
        pltpu.make_async_copy(xe.at[0 : 2 * d1], x_out.at[0], sems.at[1]),
        pltpu.make_async_copy(xe.at[R - 2 * d1 : R], x_out.at[1], sems.at[2]),
    ]
    for save in saves:
        save.start()

    def hidden_one(r):
        def post(row, at, pre):
            h1[row, :, at] = masked(elu(pre).astype(BF16), mask, row, at)

        conv_rows(xe, [r + q for q in range(16)], d1, False, wr1, post)

    loop(R, 16, hidden_one)
    saves.append(pltpu.make_async_copy(h1, h1_out, sems.at[3]))
    saves[-1].start()

    def block_one(r):
        def post(row, at, col):
            b1[row - d1, :, at] = xe[row, :, at] + masked(col.astype(BF16), mask, row, at)

        conv_columns(h1, [r + d1 + q for q in range(d1)], d1, wc1, post)

    loop(INNER, 2 * d1, block_one)
    saves.append(pltpu.make_async_copy(b1, b1_out, sems.at[4]))
    saves[-1].start()

    def hidden_two(r):
        def post(row, at, pre):
            h2[row, :, at] = masked(elu(pre).astype(BF16), mask, row + d1, at)

        conv_rows(b1, [r + q for q in range(12)], d2, False, wr2, post)

    loop(INNER, 12, hidden_two)
    saves.append(pltpu.make_async_copy(h2, h2_out, sems.at[5]))
    saves.append(pltpu.make_async_copy(h2.at[0 : d2 - d1, :, 0:W], up_out, sems.at[6]))
    saves.append(pltpu.make_async_copy(h2.at[INNER - (d2 - d1) : INNER, :, 0:W], down_out, sems.at[7]))
    for save in saves[-3:]:
        save.start()
    for save in saves:
        save.wait()


def forward_inner(*args):
    d1, d2 = FIRST_SPACING, SECOND_SPACING
    return call(
        inner_kernel, "forward_inner", [SM, ANY, VM, VM, VM, VM],
        [
            (ANY, (2, 2 * d1, C, E), BF16),
            (ANY, (R, C, E), BF16),
            (ANY, (INNER, C, E), BF16),
            (ANY, (INNER, C, E), BF16),
            (ANY, (d2 - d1, C, W), BF16),
            (ANY, (d2 - d1, C, W), BF16),
        ],
        [
            pltpu.VMEM((R, C, E), BF16),
            pltpu.VMEM((R, C, E), BF16),
            pltpu.VMEM((INNER, C, E), BF16),
            pltpu.VMEM((INNER, C, E), BF16),
            pltpu.VMEM((3, 16, E), BF16),
            pltpu.SemaphoreType.DMA((8,)),
        ],
        10, *args,
    )


def outer_kernel(
    tiles, above, below, x_in, h1_in, wr, wc,
    b1_out, h2_out,
    x, h1, b1, h2, mask, sems,
):
    d1, d2 = FIRST_SPACING, SECOND_SPACING
    n = 2 * d1
    loads = [
        pltpu.make_async_copy(above.at[0:XHALO], x.at[0, 0:n, :, 0:W], sems.at[0]),
        pltpu.make_async_copy(below.at[0:XHALO], x.at[1, n : 2 * n, :, 0:W], sems.at[1]),
        pltpu.make_async_copy(x_in.at[0], x.at[0, n : 2 * n], sems.at[2]),
        pltpu.make_async_copy(x_in.at[1], x.at[1, 0:n], sems.at[3]),
        pltpu.make_async_copy(h1_in.at[0:n], h1.at[0, n : 2 * n], sems.at[4]),
        pltpu.make_async_copy(h1_in.at[R - n : R], h1.at[1, 0:n], sems.at[5]),
    ]
    edge_rows = pltpu.VMEM((2, C, W), BF16)
    for load in loads:
        load.start()
    build_mask(tiles, mask)

    def with_edges(packed, sem):
        gets = [
            pltpu.make_async_copy(above.at[XHALO], packed.at[0], sem.at[0]),
            pltpu.make_async_copy(below.at[XHALO], packed.at[1], sem.at[1]),
        ]
        for get in gets:
            get.start()
        for get in gets:
            get.wait()
        per = 128 // XEDGE
        for side in range(2):
            tile = [packed[side, :, t * 128 : (t + 1) * 128] for t in range(4)]
            for q in range(XHALO):
                x[side, side * n + q, :, TAIL] = unpack(tile[q // per], tile[2 + q // per], q % per, XEDGE)

    pl.run_scoped(with_edges, edge_rows, pltpu.SemaphoreType.DMA((2,)))
    wr1, wr2 = forward_matrix(wr[0]), forward_matrix(wr[1])
    wc1 = two_rows(forward_matrix(wc[0]))
    for load in loads:
        load.wait()

    for side in range(2):
        first = side * R - n

        def post_h1(row, at, pre):
            h1[side, row, :, at] = masked(elu(pre).astype(BF16), mask, row + first, at)

        conv_rows(x.at[side], [side * n + q for q in range(n)], d1, False, wr1, post_h1)
    for side in range(2):
        first = side * R - n

        def post_b1(row, at, col):
            kept = masked(col.astype(BF16), mask, row + first, at)
            b1[side, row - d1, :, at] = x[side, row, :, at] + kept

        conv_columns(h1.at[side], [d1 + q for q in range(d1)], d1, wc1, post_b1)
    for side in range(2):
        first = side * R - d1

        def post_h2(row, at, pre):
            h2[side, row, :, at] = masked(elu(pre).astype(BF16), mask, row + first, at)

        conv_rows(b1.at[side], [q for q in range(n)], d2, False, wr2, post_h2)
    saves = [pltpu.make_async_copy(b1, b1_out, sems.at[6]), pltpu.make_async_copy(h2, h2_out, sems.at[7])]
    for save in saves:
        save.start()
    for save in saves:
        save.wait()


def forward_outer(*args):
    n = 2 * FIRST_SPACING
    return call(
        outer_kernel, "forward_outer", [SM, ANY, ANY, ANY, ANY, VM, VM],
        [(ANY, (2, n, C, E), BF16), (ANY, (2, n, C, E), BF16)],
        [
            pltpu.VMEM((2, 2 * n, C, E), BF16),
            pltpu.VMEM((2, 2 * n, C, E), BF16),
            pltpu.VMEM((2, n, C, E), BF16),
            pltpu.VMEM((2, n, C, E), BF16),
            pltpu.VMEM((3, 16, E), BF16),
            pltpu.SemaphoreType.DMA((8,)),
        ],
        7, *args,
    )


def final_kernel(
    tiles, above, below, b1_in, b1_side, h2_in, h2_side, wc,
    out,
    b1, h2, flat, mask, sems,
):
    d1, d2 = FIRST_SPACING, SECOND_SPACING
    n, far, own = 2 * d1, d2 - d1, slice(0, W)
    loads = [
        pltpu.make_async_copy(above, h2.at[0:far], sems.at[0]),
        pltpu.make_async_copy(h2_side.at[0, :, :, own], h2.at[far : far + n], sems.at[1]),
        pltpu.make_async_copy(h2_in.at[:, :, own], h2.at[far + n : far + n + INNER], sems.at[2]),
        pltpu.make_async_copy(h2_side.at[1, :, :, own], h2.at[far + n + INNER : R + 2 * d2 - far], sems.at[3]),
        pltpu.make_async_copy(below, h2.at[R + 2 * d2 - far : R + 2 * d2], sems.at[4]),
        pltpu.make_async_copy(b1_side.at[0, d1:n, :, own], b1.at[0:d1], sems.at[5]),
        pltpu.make_async_copy(b1_in.at[:, :, own], b1.at[d1 : R - d1], sems.at[6]),
        pltpu.make_async_copy(b1_side.at[1, 0:d1, :, own], b1.at[R - d1 : R], sems.at[7]),
    ]
    for load in loads:
        load.start()
    build_mask(tiles, mask)
    wc2 = two_rows(forward_matrix(wc[1]))
    for load in loads:
        load.wait()

    def last(i):
        r = (i // d2) * 2 * d2 + i % d2

        def post(row, at, col):
            flat[row - d2, :, at] = b1[row - d2, :, at] + masked(col.astype(BF16), mask, row - d2, at)

        conv_columns(h2, [r + d2 + q for q in range(4)], d2, wc2, post, tail=False)

    loop(R // 2, 4, last)
    turn_out(flat, out)


def forward_final(*args):
    return call(
        final_kernel, "forward_final", [SM, ANY, ANY, ANY, ANY, ANY, ANY, VM],
        [(VM, (C, R, W), BF16)],
        [
            pltpu.VMEM((R, C, W), BF16),
            pltpu.VMEM((R + 2 * SECOND_SPACING, C, W), BF16),
            pltpu.VMEM((R, C, W), BF16),
            pltpu.VMEM((3, 16, E), BF16),
            pltpu.SemaphoreType.DMA((8,)),
        ],
        4, *args,
    )[0]


def backward_kernel(
    tiles, c, above, below, left, right, wr, wc, x_in, h1_in, b1_in, b1_side, h2_in, h2_side,
    taps, a1_out, g1_out,
    packed, ce, cm, h1, b1, h2, x, a2, cg1, g1, a1, col_acc, row_acc, mask, sems,
):
    d1, d2 = FIRST_SPACING, SECOND_SPACING
    n = 2 * d1
    loads = [
        pltpu.make_async_copy(c, ce.at[HALO : HALO + R, :, 0:W], sems.at[0]),
        pltpu.make_async_copy(above.at[0:HALO], ce.at[0:HALO, :, 0:W], sems.at[1]),
        pltpu.make_async_copy(below.at[0:HALO], ce.at[HALO + R :, :, 0:W], sems.at[2]),
        pltpu.make_async_copy(above.at[HALO], packed.at[0], sems.at[7]),
        pltpu.make_async_copy(below.at[HALO], packed.at[1], sems.at[8]),
    ]
    late = [
        pltpu.make_async_copy(h2_side.at[0], h2.at[0:n], sems.at[3]),
        pltpu.make_async_copy(h2_in, h2.at[n : n + INNER], sems.at[9]),
        pltpu.make_async_copy(h2_side.at[1], h2.at[n + INNER : R + n], sems.at[10]),
        pltpu.make_async_copy(b1_side.at[0, d1:n], b1.at[0:d1], sems.at[4]),
        pltpu.make_async_copy(b1_in, b1.at[d1 : R - d1], sems.at[11]),
        pltpu.make_async_copy(b1_side.at[1, 0:d1], b1.at[R - d1 : R], sems.at[12]),
        pltpu.make_async_copy(h1_in, h1, sems.at[5]),
        pltpu.make_async_copy(x_in, x, sems.at[6]),
    ]
    for load in loads + late:
        load.start()
    build_mask(tiles, mask)
    per = 128 // CEDGE

    def edges(g, _):
        for k in range(per):
            ce[HALO + g * per + k, :, TAIL] = unpack(left[XTILES + g], right[XTILES + g], k, CEDGE)
        return 0

    lax.fori_loop(0, CTILES, edges, 0)
    wr1, wr2 = backward_matrix(wr[0]), backward_matrix(wr[1])
    wc1, wc2 = backward_matrix(wc[0], (2, 1, 0)), backward_matrix(wc[1], (2, 1, 0))
    wc1w, wc2w = two_rows(wc1), two_rows(wc2)
    for load in loads:
        load.wait()
    for side, first, skip in ((0, 0, 2 * per - HALO), (1, HALO + R, 0)):
        tile = [packed[side, :, t * 128 : (t + 1) * 128] for t in range(4)]
        for q in range(HALO):
            g, k = divmod(q + skip, per)
            ce[first + q, :, TAIL] = unpack(tile[g], tile[2 + g], k, CEDGE)

    def mask_cot(r):
        for q in range(4):
            cm[r + q] = masked(ce[r + q], mask, r + q - HALO, slice(0, E))

    loop(R + 2 * HALO, 4, mask_cot)
    for load in late[0:3]:
        load.wait()

    up = HALO - d1

    def post_two(row, at, hid):
        slope = 1.0 + jnp.minimum(h2[row - up, :, at], 0).astype(F32)
        a2[row - up, :, at] = masked((hid * slope).astype(BF16), mask, row - HALO, at)

    def act_two(i):
        r = (i // d2) * 2 * d2 + i % d2
        conv_columns(cm, [r + up + q for q in range(4)], d2, wc2w, post_two)

    loop(R // 2, 4, act_two)
    conv_columns_single(cm, [R + up + q for q in range(2 * d1)], d2, wc2, post_two)
    for load in late[3:6]:
        load.wait()

    col_acc[...] = jnp.zeros_like(col_acc)
    row_acc[...] = jnp.zeros_like(row_acc)

    def add_col_taps(k, grads, g, hidden, h, d, rows):
        acc = col_acc[k]
        for r in rows:
            for at in MAIN:
                left = jnp.concatenate([hidden[r + h + q * d, :, at] for q in (0, 1)], axis=0)
                right = jnp.concatenate([grads[r + g + q * d, :, at] for q in (-1, 0, 1, 2)], axis=0)
                acc += dot_nt(left, right)
        col_acc[k] = acc

    def add_row_taps(k, values, stacks):
        acc = row_acc[k]
        for value, stack in zip(values, stacks):
            for at in MAIN:
                acc += dot_nt(value[:, at], stack[:, at])
        row_acc[k] = acc

    def col_taps_two(i):
        r = (i // d2) * 2 * d2 + i % d2
        add_col_taps(0, cm, HALO, h2, d1, d2, [r + q for q in range(4)])

    loop(R // 2, 4, col_taps_two)

    def post_one(row, at, mixed):
        g = ce[row + up, :, at].astype(F32) + mixed
        cg1[row, :, at] = masked(g.astype(BF16), mask, row - d1, at)
        if at != TAIL:
            g1[row, :, at] = g

    def grad_one(r):
        rows = [r + q + d1 for q in range(STEP)]
        stacks = conv_rows(a2, rows, d2, True, wr2, post_one)
        add_row_taps(0, [b1[s - d1] for s in rows], stacks)

    for first in (0, R + d1):
        conv_rows(a2, [first + q for q in range(d1)], d2, True, wr2, post_one)
    loop(R, STEP, grad_one)
    save_g1 = pltpu.make_async_copy(g1.at[d1 : R + d1], g1_out, sems.at[13])
    save_g1.start()
    for load in late[6:8]:
        load.wait()

    def act_one(r):
        def post(row, at, hid):
            slope = 1.0 + jnp.minimum(h1[row - d1, :, at], 0).astype(F32)
            a1[row - d1, :, at] = masked((hid * slope).astype(BF16), mask, row - d1, at)

        rows = [r + q for q in range(2 * d1)]
        conv_columns(cg1, [s + d1 for s in rows[:d1]], d1, wc1w, post)
        add_col_taps(1, cg1, d1, h1, 0, d1, rows[:d1])

    loop(R, 2 * d1, act_one)

    save_a1 = pltpu.make_async_copy(a1, a1_out, sems.at[14])
    save_a1.start()

    def last(r):
        rows = [r + q for q in range(STEP)]
        add_row_taps(1, [x[s] for s in rows], [row_stack(a1[s], d1, True) for s in rows])

    loop(R, STEP, last)
    save_a1.wait()
    save_g1.wait()
    for k in range(2):
        acc = col_acc[k]
        low, high = acc[:C].T, acc[C:].T
        col = [low[(2 - q) * C : (3 - q) * C] + high[(3 - q) * C : (4 - q) * C] for q in range(3)]
        both = jnp.concatenate([jnp.concatenate(col, axis=0), row_acc[k].T], axis=1)
        for q in range(PIECES // 2):
            taps[k * PIECES // 2 + q] = both[q * PIECE : (q + 1) * PIECE]


PIECES = 32
PIECE = 6 * C // PIECES


def backward(*args):
    n = 2 * FIRST_SPACING
    return call(
        backward_kernel, "backward", [SM, ANY, ANY, ANY, VM, VM, VM, VM] + [ANY] * 6,
        [(VM, (PIECES, PIECE, 2 * C), F32), (ANY, (R, C, E), BF16), (ANY, (R, C, W), F32)],
        [
            pltpu.VMEM((2, C, W), BF16),
            pltpu.VMEM((R + 2 * HALO, C, E), BF16),
            pltpu.VMEM((R + 2 * HALO, C, E), BF16),
            pltpu.VMEM((R, C, E), BF16),
            pltpu.VMEM((R, C, E), BF16),
            pltpu.VMEM((R + n, C, E), BF16),
            pltpu.VMEM((R, C, W), BF16),
            pltpu.VMEM((R + n, C, E), BF16),
            pltpu.VMEM((R + n, C, E), BF16),
            pltpu.VMEM((R + n, C, W), F32),
            pltpu.VMEM((R, C, E), BF16),
            pltpu.VMEM((2, 2 * C, 4 * C), F32),
            pltpu.VMEM((2, C, 3 * C), F32),
            pltpu.VMEM((3, 16, E), BF16),
            pltpu.SemaphoreType.DMA((15,)),
        ],
        25, *args,
    )


def map_kernel(a1_in, g1_in, wr, out, a1, g1, flat, sems):
    half = R // 2
    loads = []
    for q in range(2):
        at = pl.ds(q * half, half)
        loads.append(pltpu.make_async_copy(a1_in.at[at], a1.at[at], sems.at[2 * q]))
        loads.append(pltpu.make_async_copy(g1_in.at[at], g1.at[at], sems.at[2 * q + 1]))
    for load in loads:
        load.start()
    wr1 = backward_matrix(wr[0])

    def last(r):
        def post(row, at, mixed):
            flat[row, :, at] = (g1[row, :, at] + mixed).astype(BF16)

        conv_rows(a1, [r + q for q in range(STEP)], FIRST_SPACING, True, wr1, post, tail=False)

    for q in range(2):
        loads[2 * q].wait()
        loads[2 * q + 1].wait()
        loop(half, STEP, lambda r, q=q: last(q * half + r))
    turn_out(flat, out)


def backward_map(*args):
    return call(
        map_kernel, "backward_map", [ANY, ANY, VM],
        [(VM, (C, R, W), BF16)],
        [
            pltpu.VMEM((R, C, E), BF16),
            pltpu.VMEM((R, C, W), F32),
            pltpu.VMEM((R, C, W), BF16),
            pltpu.SemaphoreType.DMA((4,)),
        ],
        4, *args,
    )[0]


def tap_sum(taps, beside):
    part = lax.all_to_all(taps, "rows", 0, 0, tiled=True)
    part, beside = lax.optimization_barrier((part, beside))
    part = lax.all_gather(part.sum(0), COLS).sum(0)
    spread = jnp.broadcast_to(part[None], taps.shape)
    whole = lax.all_to_all(spread, "rows", 0, 0, tiled=True)
    return whole.reshape(2, 3, C, 2 * C), beside


COLS = ("y_hi", "core")


def on_device(x, tile_mask, wr, wc, cot):
    n_rows, n_cols = lax.axis_size("rows"), lax.axis_size(COLS)
    factor = 1.0 / math.sqrt(R * n_rows * W * n_cols)
    down = [(i, i + 1) for i in range(n_rows - 1)]
    up = [(i + 1, i) for i in range(n_rows - 1)]
    right = [(i, i + 1) for i in range(n_cols - 1)]
    left = [(i + 1, i) for i in range(n_cols - 1)]

    to_left, to_right = pack_edges(x, cot)
    from_right = lax.ppermute(to_left, COLS, left)
    from_left = lax.ppermute(to_right, COLS, right)
    xt, x_up, x_down, ct, c_up, c_down = turn_both(x, cot)
    x_up, x_down, c_up, c_down = fill((x_up, x_down, c_up, c_down), from_left, from_right)
    x_above = lax.ppermute(x_down, "rows", down)
    x_below = lax.ppermute(x_up, "rows", up)
    c_above = lax.ppermute(c_down, "rows", down)
    c_below = lax.ppermute(c_up, "rows", up)

    x_side, h1, b1, h2, h2_up, h2_down = forward_inner(tile_mask, xt, from_left, from_right, wr, wc)
    h2_above = lax.ppermute(h2_down, "rows", down)
    h2_below = lax.ppermute(h2_up, "rows", up)
    b1_side, h2_side = forward_outer(tile_mask, x_above, x_below, x_side, h1, wr, wc)
    taps, a1, g1 = backward(
        tile_mask, ct, c_above, c_below, from_left, from_right, wr, wc, xt, h1, b1, b1_side, h2, h2_side
    )
    taps, h2_above, h2_below = lax.optimization_barrier((taps, h2_above, h2_below))
    final = forward_final(tile_mask, h2_above, h2_below, b1, b1_side, h2, h2_side, wc)
    total, map_grad = tap_sum(taps, backward_map(a1, g1, wr))
    total = total[::-1] * factor
    return final, map_grad, total[..., C:], total[..., :C]


def solution(mesh):
    n_rows, n_cols = mesh.devices.shape
    inner = Mesh(mesh.devices.reshape(n_rows, n_cols // 2, 2), ("rows",) + COLS)
    blocks = P(None, "rows", COLS)
    return jax.shard_map(
        on_device,
        mesh=inner,
        in_specs=(blocks, P(), P(), P(), blocks),
        out_specs=(blocks, blocks, P(), P()),
        check_vma=False,
    )
```

```python
import functools
import math

import jax
import jax.numpy as jnp
from jax import lax
from jax.experimental import pallas as pl
from jax.experimental.pallas import tpu as pltpu
from jax.sharding import Mesh, PartitionSpec as P

FIRST_SPACING = 4
SECOND_SPACING = 8
TILE = 128
C = 64
R = 32
W = 512
E = 640
HALO = 12
XEDGE = 32
CEDGE = 16
XTILES = R * XEDGE // 128
CTILES = R * CEDGE // 128
F32 = jnp.float32
BF16 = jnp.bfloat16
MIB = 1024 * 1024
VM_INNER, VM_OUTER, VM_BACK, VM_TURN = 59, 59, 59, 59


def dot(a, b):
    return jnp.dot(a, b, preferred_element_type=F32)


def dot_nt(a, b):
    return lax.dot_general(a, b, (((1,), (1,)), ((), ())), preferred_element_type=F32)


def turn(block):
    return jnp.swapaxes(block, 0, 1)


def lanes(first, count, channels):
    lane = lax.broadcasted_iota(jnp.int32, (channels, 128), 1)
    return ((lane >= first) & (lane < first + count)).astype(F32).astype(BF16)


def rolled(v, shift):
    shift = shift % 128
    return pltpu.roll(v, shift, 1) if shift else v


def pack(rows, width, first):
    keep = lanes(first, width, rows[0].shape[0])
    parts = [rolled(v * keep, width * k - first) for k, v in enumerate(rows)]
    return functools.reduce(jnp.add, parts)


def unpack(left, right, k, width):
    channels = left.shape[0]
    ahead = rolled(right, -width * k) * lanes(0, width, channels)
    behind = rolled(left, 128 - width - width * k) * lanes(128 - width, width, channels)
    return ahead + behind


GC = 16


def edge_kernel(x_low, x_high, c_low, c_high, to_left, to_right):
    for src, width, at in ((x_low, XEDGE, 0), (c_low, CEDGE, XTILES)):
        for i in range(2):
            rows = turn(src[:, i * 16 : (i + 1) * 16, :])
            per = 128 // width
            for g in range(16 // per):
                tile = pack([rows[g * per + k] for k in range(per)], width, 0)
                to_left[at + (i * 16) // per + g] = tile
    for src, width, at in ((x_high, XEDGE, 0), (c_high, CEDGE, XTILES)):
        for i in range(2):
            rows = turn(src[:, i * 16 : (i + 1) * 16, :])
            per = 128 // width
            for g in range(16 // per):
                tile = pack([rows[g * per + k] for k in range(per)], width, 128 - width)
                to_right[at + (i * 16) // per + g] = tile


def pack_edges(x, c):
    low = pl.BlockSpec((GC, R, 128), lambda g: (g, 0, 0))
    high = pl.BlockSpec((GC, R, 128), lambda g: (g, 0, W // 128 - 1))
    out = pl.BlockSpec((XTILES + CTILES, GC, 128), lambda g: (0, g, 0))
    return pl.pallas_call(
        edge_kernel,
        grid=(C // GC,),
        in_specs=[low, high, low, high],
        out_specs=[out, out],
        out_shape=[jax.ShapeDtypeStruct((XTILES + CTILES, C, 128), BF16)] * 2,
        compiler_params=pltpu.CompilerParams(vmem_limit_bytes=16 * MIB),
        name="pack_edges",
    )(x, x, c, c)


def turn_block(src, dst):
    for i in range(R // 16):
        for t in range(W // 128):
            at = slice(t * 128, (t + 1) * 128)
            dst[i * 16 : (i + 1) * 16, :, at] = turn(src[:, i * 16 : (i + 1) * 16, at])


XROWS = 2 * HALO + 3
CROWS = HALO + 1


def turn_kernel(x_ref, c_ref, xt, x_up, x_down, ct, c_up, c_down):
    turn_block(x_ref, xt)
    for out, rows in ((x_up, slice(0, HALO)), (x_down, slice(R - HALO, R))):
        out[0:HALO] = xt[rows, :, MAIN[0]]
        out[HALO : 2 * HALO] = xt[rows, :, MAIN[1]]
    turn_block(c_ref, ct)
    c_up[0:HALO] = ct[0:HALO]
    c_down[0:HALO] = ct[R - HALO : R]


def message(rows, width):
    return (
        pl.BlockSpec((rows, GC, width), lambda g: (0, g, 0)),
        jax.ShapeDtypeStruct((rows, C, width), BF16),
    )


def turn_both(x, c):
    native = pl.BlockSpec((GC, R, W), lambda g: (g, 0, 0))
    turned = pl.BlockSpec((R, GC, W), lambda g: (0, g, 0))
    block = jax.ShapeDtypeStruct((R, C, W), BF16)
    (xs, x_shape), (cs, c_shape) = message(XROWS, W // 2), message(CROWS, W)
    return pl.pallas_call(
        turn_kernel,
        grid=(C // GC,),
        in_specs=[native, native],
        out_specs=[turned, xs, xs, turned, cs, cs],
        out_shape=[block, x_shape, x_shape, block, c_shape, c_shape],
        compiler_params=pltpu.CompilerParams(vmem_limit_bytes=VM_TURN * MIB),
        name="turn_both",
    )(x, c)


def fill_kernel(
    x_up_in, x_down_in, c_up_in, c_down_in, left, right, x_up, x_down, c_up, c_down, x_rows, c_rows, sems
):
    copies = []
    for q, (out, first) in enumerate(((x_up, 0), (x_down, XTILES - 3))):
        tiles = [left[first + k] for k in range(3)] + [right[first + k] for k in range(3)]
        for k in range(3):
            x_rows[q, k] = jnp.concatenate(tiles[2 * k : 2 * k + 2], axis=1)
        copies.append(pltpu.make_async_copy(x_rows.at[q], out.at[2 * HALO : XROWS], sems.at[q]))
    for q, (out, first) in enumerate(((c_up, XTILES), (c_down, XTILES + CTILES - 2))):
        tiles = [left[first], left[first + 1], right[first], right[first + 1]]
        c_rows[q] = jnp.concatenate(tiles, axis=1)
        copies.append(pltpu.make_async_copy(c_rows.at[q], out.at[HALO], sems.at[2 + q]))
    for copy in copies:
        copy.start()
    for copy in copies:
        copy.wait()


def fill(messages, left, right):
    return pl.pallas_call(
        fill_kernel,
        in_specs=[ANY] * 4 + [VM, VM],
        out_specs=[ANY] * 4,
        out_shape=[jax.ShapeDtypeStruct(m.shape, BF16) for m in messages],
        input_output_aliases={q: q for q in range(4)},
        scratch_shapes=[
            pltpu.VMEM((2, 3, C, W // 2), BF16),
            pltpu.VMEM((2, C, W), BF16),
            pltpu.SemaphoreType.DMA((4,)),
        ],
        name="fill_messages",
    )(*messages, left, right)


ANY = pl.BlockSpec(memory_space=pl.ANY)
VM = pl.BlockSpec(memory_space=pltpu.VMEM)
SM = pl.BlockSpec(memory_space=pltpu.SMEM)
STEP = 8
LONG = 16


def build_mask(tiles, mask):
    row_dev, col_dev = lax.axis_index("rows"), lax.axis_index(COLS)
    n_rows, n_cols = tiles.shape
    first_row, first_tile = row_dev * R, col_dev * (W // TILE)
    lane = lax.broadcasted_iota(jnp.int32, (16, 128), 1)

    def value(p, ct):
        cell = first_row + (-1, 0, R)[p]
        inside = (cell >= 0) & (cell < n_rows * TILE) & (ct >= 0) & (ct < n_cols)
        rt = jnp.clip(cell, 0, n_rows * TILE - 1) // TILE
        return jnp.where(inside, tiles[rt, jnp.clip(ct, 0, n_cols - 1)], 0)

    for p in range(3):
        for t in range(W // 128):
            cell = jnp.full((16, 128), value(p, first_tile + t), jnp.int32)
            mask[p, :, t * 128 : (t + 1) * 128] = cell.astype(F32).astype(BF16)
        right = jnp.full((16, 128), value(p, first_tile + W // TILE), jnp.int32)
        left = jnp.full((16, 128), value(p, first_tile - 1), jnp.int32)
        mask[p, :, W:E] = jnp.where(lane < 64, right, left).astype(F32).astype(BF16)


def masked(v, mask, r, at):
    if isinstance(r, int):
        p = int(r >= 0) + int(r >= R)
    else:
        p = (r >= 0).astype(jnp.int32) + (r >= R).astype(jnp.int32)
    m = mask[p, :, at]
    return v * jnp.concatenate([m] * (C // 16), axis=0)


def shifted(v, d):
    return pltpu.roll(v, (-d) % v.shape[1], 1)


def row_stack(v, d, reverse):
    ahead, behind = shifted(v, d), shifted(v, -d)
    parts = [ahead, v, behind] if reverse else [behind, v, ahead]
    return jnp.concatenate(parts, axis=0)


def forward_matrix(w):
    return jnp.concatenate([w[j].astype(F32).T for j in range(3)], axis=0).T.astype(BF16)


def backward_matrix(w, order=(0, 1, 2)):
    return jnp.concatenate([w[j].astype(F32) for j in order], axis=0).T.astype(BF16)


def two_rows(matrix):
    none = jnp.zeros((C, C), BF16)
    return jnp.concatenate(
        [jnp.concatenate([matrix, none], axis=1), jnp.concatenate([none, matrix], axis=1)], axis=0
    )


MAIN = (slice(0, 256), slice(256, 512))
TAIL = slice(W, E)


def loop(count, step, body):
    def one(i, _):
        body(i * step)
        return 0

    lax.fori_loop(0, count // step, one, 0)


def conv_columns(ref, rows, d, matrix, post, tail=True):
    def window(r, at):
        return jnp.concatenate([ref[r + k * d, :, at] for k in (-1, 0, 1, 2)], axis=0)

    for r in rows:
        for at in MAIN:
            both = dot(matrix, window(r, at))
            post(r, at, both[:C])
            post(r + d, at, both[C:])
    if tail:
        for r, s in zip(rows[::2], rows[1::2]):
            both = dot(matrix, jnp.concatenate([window(r, TAIL), window(s, TAIL)], axis=1))
            for row, half in ((r, both[:, :128]), (s, both[:, 128:])):
                post(row, TAIL, half[:C])
                post(row + d, TAIL, half[C:])


def conv_columns_single(ref, rows, d, matrix, post):
    def window(r, at):
        return jnp.concatenate([ref[r + k * d, :, at] for k in (-1, 0, 1)], axis=0)

    for r in rows:
        for at in MAIN:
            post(r, at, dot(matrix, window(r, at)))
    for r, s in zip(rows[::2], rows[1::2]):
        both = dot(matrix, jnp.concatenate([window(r, TAIL), window(s, TAIL)], axis=1))
        post(r, TAIL, both[:, :128])
        post(s, TAIL, both[:, 128:])


def conv_rows(ref, rows, d, reverse, matrix, post, tail=True):
    stacks = []
    for r in rows:
        stack = row_stack(ref[r], d, reverse)
        stacks.append(stack)
        for at in MAIN:
            post(r, at, dot(matrix, stack[:, at]))
    if tail:
        for q in range(0, len(rows), 2):
            both = dot(matrix, jnp.concatenate([stacks[q][:, TAIL], stacks[q + 1][:, TAIL]], axis=1))
            post(rows[q], TAIL, both[:, :128])
            post(rows[q + 1], TAIL, both[:, 128:])
    return stacks


def add_col_taps(acc_ref, grads, g, hidden, h, d, rows):
    acc = acc_ref[...]
    for r in rows:
        for at in MAIN:
            left = jnp.concatenate([hidden[r + h + q * d, :, at] for q in (0, 1)], axis=0)
            right = jnp.concatenate([grads[r + g + q * d, :, at] for q in (-1, 0, 1, 2)], axis=0)
            acc += dot_nt(left, right)
    acc_ref[...] = acc


def add_col_taps_single(acc_ref, grads, g, hidden, h, d, rows):
    acc = acc_ref[0:C, 0 : 3 * C]
    for r in rows:
        for at in MAIN:
            right = jnp.concatenate([grads[r + g + q * d, :, at] for q in (-1, 0, 1)], axis=0)
            acc += dot_nt(hidden[r + h, :, at], right)
    acc_ref[0:C, 0 : 3 * C] = acc


def add_row_taps(acc_ref, values, stacks):
    acc = acc_ref[...]
    for value, stack in zip(values, stacks):
        for at in MAIN:
            acc += dot_nt(value[:, at], stack[:, at])
    acc_ref[...] = acc


def elu(p):
    return jnp.where(p > 0, p, jnp.exp(p) - 1.0)


def turn_out(src, out):
    for i in range(R // 16):
        for t in range(W // 128):
            at = slice(t * 128, (t + 1) * 128)
            out[:, i * 16 : (i + 1) * 16, at] = turn(src[i * 16 : (i + 1) * 16, :, at])


def call(kernel, name, in_specs, outs, scratch, cost, vmem, *args):
    return pl.pallas_call(
        kernel,
        in_specs=in_specs,
        out_specs=[spec for spec, _, _ in outs],
        out_shape=[jax.ShapeDtypeStruct(shape, dtype) for _, shape, dtype in outs],
        scratch_shapes=scratch,
        compiler_params=pltpu.CompilerParams(vmem_limit_bytes=vmem * MIB),
        cost_estimate=pl.CostEstimate(flops=cost * 500_000_000, bytes_accessed=cost * 1_000_000, transcendentals=0),
        name=name,
    )(*args)


INNER = R - 2 * FIRST_SPACING


def inner_kernel(
    tiles, x, c, left, right, wr, wc,
    x_out, h1_out, b1_out, h2_out, c_out, a2_out, cg1_out, g1_out, col_acc, row_acc,
    xe, h1, b1, h2, ce, cm, a2, cg1, g1, mask, sems,
):
    d1, d2 = FIRST_SPACING, SECOND_SPACING
    load = pltpu.make_async_copy(x, xe.at[:, :, 0:W], sems.at[0])
    load.start()
    load_c = pltpu.make_async_copy(c, ce.at[:, :, 0:W], sems.at[6])
    load_c.start()
    build_mask(tiles, mask)
    for dst, width, first, count in ((xe, XEDGE, 0, XTILES), (ce, CEDGE, XTILES, CTILES)):
        per = 128 // width

        def edges(g, _):
            for k in range(per):
                dst[g * per + k, :, TAIL] = unpack(left[first + g], right[first + g], k, width)
            return 0

        lax.fori_loop(0, count, edges, 0)
    wr1, wr2 = forward_matrix(wr[0]), forward_matrix(wr[1])
    wc1 = two_rows(forward_matrix(wc[0]))
    load.wait()
    saves = [
        pltpu.make_async_copy(xe.at[0 : 2 * d1], x_out.at[0], sems.at[1]),
        pltpu.make_async_copy(xe.at[R - 2 * d1 : R], x_out.at[1], sems.at[2]),
    ]
    for save in saves:
        save.start()

    def hidden_one(r):
        def post(row, at, pre):
            h1[row, :, at] = masked(elu(pre).astype(BF16), mask, row, at)

        conv_rows(xe, [r + q for q in range(16)], d1, False, wr1, post)

    loop(R, 16, hidden_one)
    saves.append(pltpu.make_async_copy(h1, h1_out, sems.at[3]))
    saves[-1].start()

    def block_one(r):
        def post(row, at, col):
            b1[row - d1, :, at] = xe[row, :, at] + masked(col.astype(BF16), mask, row, at)

        conv_columns(h1, [r + d1 + q for q in range(d1)], d1, wc1, post)

    loop(INNER, 2 * d1, block_one)
    saves.append(pltpu.make_async_copy(b1, b1_out, sems.at[4]))
    saves[-1].start()

    def hidden_two(r):
        def post(row, at, pre):
            h2[row, :, at] = masked(elu(pre).astype(BF16), mask, row + d1, at)

        conv_rows(b1, [r + q for q in range(12)], d2, False, wr2, post)

    loop(INNER, 12, hidden_two)
    saves.append(pltpu.make_async_copy(h2, h2_out, sems.at[5]))
    saves[-1].start()

    wr2b = backward_matrix(wr[1])
    wc2b = two_rows(backward_matrix(wc[1], (2, 1, 0)))
    col_acc[...] = jnp.zeros_like(col_acc)
    row_acc[...] = jnp.zeros_like(row_acc)
    load_c.wait()
    saves.append(pltpu.make_async_copy(ce, c_out, sems.at[7]))
    saves[-1].start()

    def mask_cot(r):
        for q in range(4):
            cm[r + q] = masked(ce[r + q], mask, r + q, slice(0, E))

    loop(R, 4, mask_cot)

    def post_two(row, at, hid):
        slope = 1.0 + jnp.minimum(h2[row - d1, :, at], 0).astype(F32)
        a2[row - d2, :, at] = masked((hid * slope).astype(BF16), mask, row, at)

    rows = [d2 + q for q in range(d2)]
    conv_columns(cm, rows, d2, wc2b, post_two)
    add_col_taps(col_acc, cm, 0, h2, -d1, d2, rows)

    def post_one(row, at, mixed):
        g = ce[row + d2, :, at].astype(F32) + mixed
        cg1[row, :, at] = masked(g.astype(BF16), mask, row + d2, at)
        if at != TAIL:
            g1[row, :, at] = g

    rows = list(range(MIDDLE))
    stacks = conv_rows(a2, rows, d2, True, wr2b, post_one)
    add_row_taps(row_acc, [b1[r + d2 - d1, :, 0:W] for r in rows], stacks)
    late = [
        pltpu.make_async_copy(a2, a2_out, sems.at[8]),
        pltpu.make_async_copy(cg1, cg1_out, sems.at[9]),
        pltpu.make_async_copy(g1, g1_out, sems.at[10]),
    ]
    for save in late:
        save.start()
    for save in saves + late:
        save.wait()


MIDDLE = R - 2 * SECOND_SPACING


def forward_inner(*args):
    d1 = FIRST_SPACING
    return call(
        inner_kernel, "forward_inner", [SM, ANY, ANY, VM, VM, VM, VM],
        [
            (ANY, (2, 2 * d1, C, E), BF16),
            (ANY, (R, C, E), BF16),
            (ANY, (INNER, C, E), BF16),
            (ANY, (INNER, C, E), BF16),
            (ANY, (R, C, E), BF16),
            (ANY, (MIDDLE, C, E), BF16),
            (ANY, (MIDDLE, C, E), BF16),
            (ANY, (MIDDLE, C, W), F32),
            (VM, (2 * C, 4 * C), F32),
            (VM, (C, 3 * C), F32),
        ],
        [
            pltpu.VMEM((R, C, E), BF16),
            pltpu.VMEM((R, C, E), BF16),
            pltpu.VMEM((INNER, C, E), BF16),
            pltpu.VMEM((INNER, C, E), BF16),
            pltpu.VMEM((R, C, E), BF16),
            pltpu.VMEM((R, C, E), BF16),
            pltpu.VMEM((MIDDLE, C, E), BF16),
            pltpu.VMEM((MIDDLE, C, E), BF16),
            pltpu.VMEM((MIDDLE, C, W), F32),
            pltpu.VMEM((3, 16, E), BF16),
            pltpu.SemaphoreType.DMA((11,)),
        ],
        14, VM_INNER, *args,
    )


OUTER = HALO


def outer_kernel(
    tiles, above, below, x_in, h1_in, b1_in, h2_in, wr, wc,
    out, b1_out, h2_out,
    x, h1, b1s, h2s, b1, h2, packed, flat, mask, sems,
):
    d1, d2 = FIRST_SPACING, SECOND_SPACING
    n, own = 2 * d1, slice(0, W)
    size = HALO + n
    halo_at, own_at = (slice(0, HALO), slice(n, size)), (slice(HALO, size), slice(0, n))
    first_row = (-HALO, R - n)
    loads = []

    def load(src, dst):
        loads.append(pltpu.make_async_copy(src, dst, sems.at[len(loads)]))
        loads[-1].start()

    for side, src in enumerate((above, below)):
        load(src.at[2 * HALO : XROWS], packed.at[side])
        load(src.at[0:HALO], x.at[side, halo_at[side], :, MAIN[0]])
        load(src.at[HALO : 2 * HALO], x.at[side, halo_at[side], :, MAIN[1]])
        load(x_in.at[side], x.at[side, own_at[side]])
        load(h1_in.at[side * (R - n) : side * (R - n) + n], h1.at[side, own_at[side]])
    load(b1_in.at[:, :, own], b1.at[d1 : R - d1])
    load(h2_in.at[:, :, own], h2.at[OUTER : OUTER + INNER])
    build_mask(tiles, mask)
    wr1, wr2 = forward_matrix(wr[0]), forward_matrix(wr[1])
    wc1s = forward_matrix(wc[0])
    wc1, wc2 = two_rows(wc1s), two_rows(forward_matrix(wc[1]))
    for copy in loads:
        copy.wait()
    per = 128 // XEDGE
    for side in range(2):
        tile = [packed[side, k // 2, :, (k % 2) * 128 : (k % 2 + 1) * 128] for k in range(6)]
        for q in range(HALO):
            x[side, halo_at[side].start + q, :, TAIL] = unpack(tile[q // per], tile[3 + q // per], q % per, XEDGE)

    for side in range(2):

        def post_h1(row, at, pre):
            h1[side, row, :, at] = masked(elu(pre).astype(BF16), mask, row + first_row[side], at)

        conv_rows(x.at[side], [halo_at[side].start + q for q in range(HALO)], d1, False, wr1, post_h1)
    for side in range(2):

        def post_b1(row, at, col):
            kept = masked(col.astype(BF16), mask, row + first_row[side], at)
            b1s[side, row - d1, :, at] = x[side, row, :, at] + kept

        conv_columns(h1.at[side], [d1 + q for q in range(d1)], d1, wc1, post_b1)
        conv_columns_single(h1.at[side], [3 * d1 + q for q in range(d1)], d1, wc1s, post_b1)
    saves = [pltpu.make_async_copy(b1s, b1_out, sems.at[len(loads)])]
    saves[0].start()
    for side in range(2):

        def post_h2(row, at, pre):
            h2s[side, row, :, at] = masked(elu(pre).astype(BF16), mask, row + first_row[side] + d1, at)

        conv_rows(b1s.at[side], list(range(OUTER)), d2, False, wr2, post_h2)
    saves.append(pltpu.make_async_copy(h2s, h2_out, sems.at[len(loads) + 1]))
    saves[1].start()
    h2[0:OUTER] = h2s[0, :, :, own]
    h2[OUTER + INNER : 2 * OUTER + INNER] = h2s[1, :, :, own]
    b1[0:d1] = b1s[0, d2:OUTER, :, own]
    b1[R - d1 : R] = b1s[1, 0:d1, :, own]

    def last(i):
        r = (i // d2) * 2 * d2 + i % d2

        def post(row, at, col):
            flat[row - d2, :, at] = b1[row - d2, :, at] + masked(col.astype(BF16), mask, row - d2, at)

        conv_columns(h2, [r + d2 + q for q in range(4)], d2, wc2, post, tail=False)

    loop(R // 2, 4, last)
    turn_out(flat, out)
    for save in saves:
        save.wait()


def forward_outer(*args):
    size = HALO + 2 * FIRST_SPACING
    return call(
        outer_kernel, "forward_outer", [SM, VM, VM] + [ANY] * 4 + [VM, VM],
        [(VM, (C, R, W), BF16), (ANY, (2, OUTER, C, E), BF16), (ANY, (2, OUTER, C, E), BF16)],
        [
            pltpu.VMEM((2, size, C, E), BF16),
            pltpu.VMEM((2, size, C, E), BF16),
            pltpu.VMEM((2, OUTER, C, E), BF16),
            pltpu.VMEM((2, OUTER, C, E), BF16),
            pltpu.VMEM((R, C, W), BF16),
            pltpu.VMEM((R + 2 * SECOND_SPACING, C, W), BF16),
            pltpu.VMEM((2, 3, C, W // 2), BF16),
            pltpu.VMEM((R, C, W), BF16),
            pltpu.VMEM((3, 16, E), BF16),
            pltpu.SemaphoreType.DMA((14,)),
        ],
        14, VM_OUTER, *args,
    )


def backward_kernel(
    tiles, above, below, wr, wc, c, a2_in, cg1_in, g1_in, col_in, row_in,
    x_in, h1_in, b1_in, b1_side, h2_in, h2_side,
    taps, a1_out, g1_out,
    packed, ce, cm, h1, b1, h2, x, a2, cg1, g1, a1, col_acc, row_acc, mask, sems,
):
    d1, d2 = FIRST_SPACING, SECOND_SPACING
    n = 2 * d1
    loads = [
        pltpu.make_async_copy(c, ce.at[HALO : HALO + R], sems.at[0]),
        pltpu.make_async_copy(above.at[0:HALO], ce.at[0:HALO, :, 0:W], sems.at[1]),
        pltpu.make_async_copy(below.at[0:HALO], ce.at[HALO + R :, :, 0:W], sems.at[2]),
        pltpu.make_async_copy(above.at[HALO], packed.at[0], sems.at[7]),
        pltpu.make_async_copy(below.at[HALO], packed.at[1], sems.at[8]),
    ]
    late = [
        pltpu.make_async_copy(h2_side.at[0, OUTER - n : OUTER], h2.at[0:n], sems.at[3]),
        pltpu.make_async_copy(h2_in, h2.at[n : n + INNER], sems.at[9]),
        pltpu.make_async_copy(h2_side.at[1, 0:n], h2.at[n + INNER : R + n], sems.at[10]),
        pltpu.make_async_copy(b1_side.at[0, d2:OUTER], b1.at[0:d1], sems.at[4]),
        pltpu.make_async_copy(b1_in, b1.at[d1 : R - d1], sems.at[11]),
        pltpu.make_async_copy(b1_side.at[1, 0:d1], b1.at[R - d1 : R], sems.at[12]),
        pltpu.make_async_copy(a2_in, a2.at[d1 + d2 : d1 + d2 + MIDDLE], sems.at[15]),
        pltpu.make_async_copy(cg1_in, cg1.at[d1 + d2 : d1 + d2 + MIDDLE], sems.at[16]),
        pltpu.make_async_copy(g1_in, g1.at[d1 + d2 : d1 + d2 + MIDDLE], sems.at[17]),
        pltpu.make_async_copy(h1_in, h1, sems.at[5]),
        pltpu.make_async_copy(x_in, x, sems.at[6]),
    ]
    for load in loads + late:
        load.start()
    build_mask(tiles, mask)
    per = 128 // CEDGE

    wr1, wr2 = backward_matrix(wr[0]), backward_matrix(wr[1])
    wc1, wc2 = backward_matrix(wc[0], (2, 1, 0)), backward_matrix(wc[1], (2, 1, 0))
    wc1w, wc2w = two_rows(wc1), two_rows(wc2)
    for load in loads:
        load.wait()
    for side, first, skip in ((0, 0, 2 * per - HALO), (1, HALO + R, 0)):
        tile = [packed[side, :, t * 128 : (t + 1) * 128] for t in range(4)]
        for q in range(HALO):
            g, k = divmod(q + skip, per)
            ce[first + q, :, TAIL] = unpack(tile[g], tile[2 + g], k, CEDGE)

    def mask_cot(r):
        for q in range(4):
            cm[r + q] = masked(ce[r + q], mask, r + q - HALO, slice(0, E))

    loop(R + 2 * HALO, 4, mask_cot)
    for load in late[0:3]:
        load.wait()

    up = HALO - d1

    def post_two(row, at, hid):
        slope = 1.0 + jnp.minimum(h2[row - up, :, at], 0).astype(F32)
        a2[row - up, :, at] = masked((hid * slope).astype(BF16), mask, row - HALO, at)

    for first in (0, d2 + MIDDLE + d1):
        conv_columns(cm, [first + up + q for q in range(d1)], d2, wc2w, post_two)
        conv_columns_single(cm, [first + up + d1 + q for q in range(d1)], d2, wc2, post_two)
    col_acc[0] = col_in[...]
    row_acc[0] = row_in[...]
    col_acc[1] = jnp.zeros_like(col_in)
    row_acc[1] = jnp.zeros_like(row_in)
    edge_rows = [*range(d2), *range(R - d2, R)]
    add_col_taps_single(col_acc.at[0], cm, HALO, h2, d1, d2, edge_rows)
    for load in late[3:9]:
        load.wait()

    def post_one(row, at, mixed):
        g = ce[row + up, :, at].astype(F32) + mixed
        cg1[row, :, at] = masked(g.astype(BF16), mask, row - d1, at)
        if at != TAIL:
            g1[row, :, at] = g

    rows = [*range(d1 + d2), *range(d1 + d2 + MIDDLE, 2 * d1 + R)]
    stacks = conv_rows(a2, rows, d2, True, wr2, post_one)
    pairs = [(b1[r - d1], stack) for r, stack in zip(rows, stacks) if d1 <= r < R + d1]
    add_row_taps(row_acc.at[0], [p[0] for p in pairs], [p[1] for p in pairs])
    save_g1 = pltpu.make_async_copy(g1.at[d1 : R + d1], g1_out, sems.at[13])
    save_g1.start()
    for load in late[9:11]:
        load.wait()

    def act_one(r):
        def post(row, at, hid):
            slope = 1.0 + jnp.minimum(h1[row - d1, :, at], 0).astype(F32)
            a1[row - d1, :, at] = masked((hid * slope).astype(BF16), mask, row - d1, at)

        rows = [r + q for q in (*range(d1), *range(2 * d1, 3 * d1))]
        conv_columns(cg1, [s + d1 for s in rows], d1, wc1w, post)
        add_col_taps(col_acc.at[1], cg1, d1, h1, 0, d1, rows)

    loop(R, 4 * d1, act_one)

    save_a1 = pltpu.make_async_copy(a1, a1_out, sems.at[14])
    save_a1.start()

    def last(r):
        rows = [r + q for q in range(LONG)]
        add_row_taps(row_acc.at[1], [x[s] for s in rows], [row_stack(a1[s], d1, True) for s in rows])

    loop(R, LONG, last)
    save_a1.wait()
    save_g1.wait()
    for k in range(2):
        acc = col_acc[k]
        low, high = acc[:C].T, acc[C:].T
        col = [low[(2 - q) * C : (3 - q) * C] + high[(3 - q) * C : (4 - q) * C] for q in range(3)]
        both = jnp.concatenate([jnp.concatenate(col, axis=0), row_acc[k].T], axis=1)
        for q in range(PIECES // 2):
            taps[k * PIECES // 2 + q] = both[q * PIECE : (q + 1) * PIECE]


PIECES = 32
PIECE = 6 * C // PIECES


def backward(*args):
    n = 2 * FIRST_SPACING
    return call(
        backward_kernel, "backward", [SM, VM, VM, VM, VM] + [ANY] * 4 + [VM, VM] + [ANY] * 6,
        [(VM, (PIECES, PIECE, 2 * C), F32), (ANY, (R, C, E), BF16), (ANY, (R, C, W), F32)],
        [
            pltpu.VMEM((2, C, W), BF16),
            pltpu.VMEM((R + 2 * HALO, C, E), BF16),
            pltpu.VMEM((R + 2 * HALO, C, E), BF16),
            pltpu.VMEM((R, C, E), BF16),
            pltpu.VMEM((R, C, E), BF16),
            pltpu.VMEM((R + n, C, E), BF16),
            pltpu.VMEM((R, C, W), BF16),
            pltpu.VMEM((R + n, C, E), BF16),
            pltpu.VMEM((R + n, C, E), BF16),
            pltpu.VMEM((R + n, C, W), F32),
            pltpu.VMEM((R, C, E), BF16),
            pltpu.VMEM((2, 2 * C, 4 * C), F32),
            pltpu.VMEM((2, C, 3 * C), F32),
            pltpu.VMEM((3, 16, E), BF16),
            pltpu.SemaphoreType.DMA((18,)),
        ],
        20, VM_BACK, *args,
    )


def map_kernel(a1_in, g1_in, wr, out, a1, g1, flat, sems):
    half = R // 2
    loads = []
    for q in range(2):
        at = pl.ds(q * half, half)
        loads.append(pltpu.make_async_copy(a1_in.at[at], a1.at[at], sems.at[2 * q]))
        loads.append(pltpu.make_async_copy(g1_in.at[at], g1.at[at], sems.at[2 * q + 1]))
    for load in loads:
        load.start()
    wr1 = backward_matrix(wr[0])

    def last(r):
        def post(row, at, mixed):
            flat[row, :, at] = (g1[row, :, at] + mixed).astype(BF16)

        conv_rows(a1, [r + q for q in range(STEP)], FIRST_SPACING, True, wr1, post, tail=False)

    for q in range(2):
        loads[2 * q].wait()
        loads[2 * q + 1].wait()
        loop(half, STEP, lambda r, q=q: last(q * half + r))
    turn_out(flat, out)


def backward_map(*args):
    return call(
        map_kernel, "backward_map", [ANY, ANY, VM],
        [(VM, (C, R, W), BF16)],
        [
            pltpu.VMEM((R, C, E), BF16),
            pltpu.VMEM((R, C, W), F32),
            pltpu.VMEM((R, C, W), BF16),
            pltpu.SemaphoreType.DMA((4,)),
        ],
        4, 24, *args,
    )[0]


def tap_sum(taps, beside):
    part = lax.all_to_all(taps, "rows", 0, 0, tiled=True)
    part, beside = lax.optimization_barrier((part, beside))
    part = lax.all_gather(part.sum(0), COLS).sum(0)
    spread = jnp.broadcast_to(part[None], taps.shape)
    whole = lax.all_to_all(spread, "rows", 0, 0, tiled=True)
    return whole.reshape(2, 3, C, 2 * C), beside


COLS = ("y_hi", "core")


def in_hbm(array):
    return pltpu.with_memory_space_constraint(array, pltpu.HBM)


def in_vmem(array):
    return pltpu.with_memory_space_constraint(array, pltpu.VMEM)


def on_device(x, tile_mask, wr, wc, cot):
    n_rows, n_cols = lax.axis_size("rows"), lax.axis_size(COLS)
    factor = 1.0 / math.sqrt(R * n_rows * W * n_cols)
    down = [(i, i + 1) for i in range(n_rows - 1)]
    up = [(i + 1, i) for i in range(n_rows - 1)]
    right = [(i, i + 1) for i in range(n_cols - 1)]
    left = [(i + 1, i) for i in range(n_cols - 1)]

    to_left, to_right = pack_edges(x, cot)
    from_right = in_vmem(lax.ppermute(to_left, COLS, left))
    from_left = in_vmem(lax.ppermute(to_right, COLS, right))
    xt, x_up, x_down, ct, c_up, c_down = turn_both(x, cot)
    x_up, x_down, c_up, c_down = fill((x_up, x_down, c_up, c_down), from_left, from_right)
    x_above = in_vmem(lax.ppermute(x_down, "rows", down))
    x_below = in_vmem(lax.ppermute(x_up, "rows", up))
    c_above = in_vmem(lax.ppermute(c_down, "rows", down))
    c_below = in_vmem(lax.ppermute(c_up, "rows", up))

    x_side, h1, b1, h2, ce, a2, cg1, g1, col_taps, row_taps = forward_inner(
        tile_mask, xt, ct, from_left, from_right, wr, wc
    )
    final, b1_side, h2_side = forward_outer(tile_mask, x_above, x_below, x_side, h1, b1, h2, wr, wc)
    taps, a1, g1 = backward(
        tile_mask, c_above, c_below, wr, wc, ce, a2, cg1, g1, col_taps, row_taps,
        xt, h1, b1, b1_side, h2, h2_side,
    )
    a1, g1 = in_hbm(a1), in_hbm(g1)
    total, map_grad = tap_sum(taps, backward_map(a1, g1, wr))
    total = total[::-1] * factor
    return final, map_grad, total[..., C:], total[..., :C]


def solution(mesh):
    n_rows, n_cols = mesh.devices.shape
    inner = Mesh(mesh.devices.reshape(n_rows, n_cols // 2, 2), ("rows",) + COLS)
    blocks = P(None, "rows", COLS)
    return jax.shard_map(
        on_device,
        mesh=inner,
        in_specs=(blocks, P(), P(), P(), blocks),
        out_specs=(blocks, blocks, P(), P()),
        check_vma=False,
    )
```

```python
import functools
import math

import jax
import jax.numpy as jnp
from jax import lax
from jax.experimental import pallas as pl
from jax.experimental.pallas import tpu as pltpu
from jax.sharding import Mesh, PartitionSpec as P

FIRST_SPACING = 4
SECOND_SPACING = 8
TILE = 128
C = 64
R = 32
W = 512
E = 640
HALO = 12
XEDGE = 32
CEDGE = 16
XTILES = R * XEDGE // 128
CTILES = R * CEDGE // 128
F32 = jnp.float32
BF16 = jnp.bfloat16
MIB = 1024 * 1024


def dot(a, b):
    return jnp.dot(a, b, preferred_element_type=F32)


def dot_nt(a, b):
    return lax.dot_general(a, b, (((1,), (1,)), ((), ())), preferred_element_type=F32)


def turn(block):
    return jnp.swapaxes(block, 0, 1)


def lanes(first, count, channels):
    lane = lax.broadcasted_iota(jnp.int32, (channels, 128), 1)
    return ((lane >= first) & (lane < first + count)).astype(F32).astype(BF16)


def rolled(v, shift):
    shift = shift % 128
    return pltpu.roll(v, shift, 1) if shift else v


def pack(rows, width, first):
    keep = lanes(first, width, rows[0].shape[0])
    parts = [rolled(v * keep, width * k - first) for k, v in enumerate(rows)]
    return functools.reduce(jnp.add, parts)


def unpack(left, right, k, width):
    channels = left.shape[0]
    ahead = rolled(right, -width * k) * lanes(0, width, channels)
    behind = rolled(left, 128 - width - width * k) * lanes(128 - width, width, channels)
    return ahead + behind


GC = 16


def edge_kernel(x_low, x_high, c_low, c_high, to_left, to_right):
    for src, width, at in ((x_low, XEDGE, 0), (c_low, CEDGE, XTILES)):
        for i in range(2):
            rows = turn(src[:, i * 16 : (i + 1) * 16, :])
            per = 128 // width
            for g in range(16 // per):
                tile = pack([rows[g * per + k] for k in range(per)], width, 0)
                to_left[at + (i * 16) // per + g] = tile
    for src, width, at in ((x_high, XEDGE, 0), (c_high, CEDGE, XTILES)):
        for i in range(2):
            rows = turn(src[:, i * 16 : (i + 1) * 16, :])
            per = 128 // width
            for g in range(16 // per):
                tile = pack([rows[g * per + k] for k in range(per)], width, 128 - width)
                to_right[at + (i * 16) // per + g] = tile


def pack_edges(x, c):
    low = pl.BlockSpec((GC, R, 128), lambda g: (g, 0, 0))
    high = pl.BlockSpec((GC, R, 128), lambda g: (g, 0, W // 128 - 1))
    out = pl.BlockSpec((XTILES + CTILES, GC, 128), lambda g: (0, g, 0))
    return pl.pallas_call(
        edge_kernel,
        grid=(C // GC,),
        in_specs=[low, high, low, high],
        out_specs=[out, out],
        out_shape=[jax.ShapeDtypeStruct((XTILES + CTILES, C, 128), BF16)] * 2,
        compiler_params=pltpu.CompilerParams(vmem_limit_bytes=16 * MIB),
        name="pack_edges",
    )(x, x, c, c)


def turn_block(src, dst):
    for i in range(R // 16):
        for t in range(W // 128):
            at = slice(t * 128, (t + 1) * 128)
            dst[i * 16 : (i + 1) * 16, :, at] = turn(src[:, i * 16 : (i + 1) * 16, at])


XROWS = 2 * HALO + 3
CROWS = HALO + 1


def turn_kernel(x_ref, c_ref, xt, x_up, x_down, ct, c_up, c_down):
    turn_block(x_ref, xt)
    for out, rows in ((x_up, slice(0, HALO)), (x_down, slice(R - HALO, R))):
        out[0:HALO] = xt[rows, :, MAIN[0]]
        out[HALO : 2 * HALO] = xt[rows, :, MAIN[1]]
    turn_block(c_ref, ct)
    c_up[0:HALO] = ct[0:HALO]
    c_down[0:HALO] = ct[R - HALO : R]


def message(rows, width):
    return (
        pl.BlockSpec((rows, GC, width), lambda g: (0, g, 0)),
        pltpu.HBM((rows, C, width), BF16),
    )


def turn_both(x, c):
    native = pl.BlockSpec((GC, R, W), lambda g: (g, 0, 0))
    turned = pl.BlockSpec((R, GC, W), lambda g: (0, g, 0))
    block = pltpu.VMEM((R, C, W), BF16)
    (xs, x_shape), (cs, c_shape) = message(XROWS, W // 2), message(CROWS, W)
    return pl.pallas_call(
        turn_kernel,
        grid=(C // GC,),
        in_specs=[native, native],
        out_specs=[turned, xs, xs, turned, cs, cs],
        out_shape=[block, x_shape, x_shape, block, c_shape, c_shape],
        compiler_params=pltpu.CompilerParams(vmem_limit_bytes=16 * MIB),
        name="turn_both",
    )(x, c)


def fill_kernel(
    x_up_in, x_down_in, c_up_in, c_down_in, left, right, x_up, x_down, c_up, c_down, x_rows, c_rows, sems
):
    copies = []
    for q, (out, first) in enumerate(((x_up, 0), (x_down, XTILES - 3))):
        tiles = [left[first + k] for k in range(3)] + [right[first + k] for k in range(3)]
        for k in range(3):
            x_rows[q, k] = jnp.concatenate(tiles[2 * k : 2 * k + 2], axis=1)
        copies.append(pltpu.make_async_copy(x_rows.at[q], out.at[2 * HALO : XROWS], sems.at[q]))
    for q, (out, first) in enumerate(((c_up, XTILES), (c_down, XTILES + CTILES - 2))):
        tiles = [left[first], left[first + 1], right[first], right[first + 1]]
        c_rows[q] = jnp.concatenate(tiles, axis=1)
        copies.append(pltpu.make_async_copy(c_rows.at[q], out.at[HALO], sems.at[2 + q]))
    for copy in copies:
        copy.start()
    for copy in copies:
        copy.wait()


def fill(messages, left, right):
    return pl.pallas_call(
        fill_kernel,
        in_specs=[ANY] * 4 + [VM, VM],
        out_specs=[ANY] * 4,
        out_shape=[pltpu.HBM(m.shape, BF16) for m in messages],
        input_output_aliases={q: q for q in range(4)},
        scratch_shapes=[
            pltpu.VMEM((2, 3, C, W // 2), BF16),
            pltpu.VMEM((2, C, W), BF16),
            pltpu.SemaphoreType.DMA((4,)),
        ],
        name="fill_messages",
    )(*map(in_hbm, messages), left, right)


ANY = pl.BlockSpec(memory_space=pl.ANY)
VM = pl.BlockSpec(memory_space=pltpu.VMEM)
SM = pl.BlockSpec(memory_space=pltpu.SMEM)
STEP = 8
LONG = 16


def build_mask(tiles, mask):
    row_dev, col_dev = lax.axis_index("rows"), lax.axis_index(COLS)
    n_rows, n_cols = tiles.shape
    first_row, first_tile = row_dev * R, col_dev * (W // TILE)
    lane = lax.broadcasted_iota(jnp.int32, (16, 128), 1)

    def value(p, ct):
        cell = first_row + (-1, 0, R)[p]
        inside = (cell >= 0) & (cell < n_rows * TILE) & (ct >= 0) & (ct < n_cols)
        rt = jnp.clip(cell, 0, n_rows * TILE - 1) // TILE
        return jnp.where(inside, tiles[rt, jnp.clip(ct, 0, n_cols - 1)], 0)

    for p in range(3):
        for t in range(W // 128):
            cell = jnp.full((16, 128), value(p, first_tile + t), jnp.int32)
            mask[p, :, t * 128 : (t + 1) * 128] = cell.astype(F32).astype(BF16)
        right = jnp.full((16, 128), value(p, first_tile + W // TILE), jnp.int32)
        left = jnp.full((16, 128), value(p, first_tile - 1), jnp.int32)
        mask[p, :, W:E] = jnp.where(lane < 64, right, left).astype(F32).astype(BF16)


def masked(v, mask, r, at):
    if isinstance(r, int):
        p = int(r >= 0) + int(r >= R)
    else:
        p = (r >= 0).astype(jnp.int32) + (r >= R).astype(jnp.int32)
    m = mask[p, :, at]
    return v * jnp.concatenate([m] * (C // 16), axis=0)


def shifted(v, d):
    return pltpu.roll(v, (-d) % v.shape[1], 1)


def row_stack(v, d, reverse):
    ahead, behind = shifted(v, d), shifted(v, -d)
    parts = [ahead, v, behind] if reverse else [behind, v, ahead]
    return jnp.concatenate(parts, axis=0)


def forward_matrix(w):
    return jnp.concatenate([w[j].astype(F32).T for j in range(3)], axis=0).T.astype(BF16)


def backward_matrix(w, order=(0, 1, 2)):
    return jnp.concatenate([w[j].astype(F32) for j in order], axis=0).T.astype(BF16)


def two_rows(matrix):
    none = jnp.zeros((C, C), BF16)
    return jnp.concatenate(
        [jnp.concatenate([matrix, none], axis=1), jnp.concatenate([none, matrix], axis=1)], axis=0
    )


MAIN = (slice(0, 256), slice(256, 512))
TAIL = slice(W, E)


class Rows:
    def __init__(self, *parts):
        self.parts = parts

    def __call__(self, r, at):
        for first, count, get in self.parts:
            if first <= r < first + count:
                return get(r - first, at)
        raise IndexError(r)

    def row(self, r):
        return jnp.concatenate([self(r, at) for at in (*MAIN, TAIL)], axis=1)


def held(ref, *index):
    return lambda q, at: ref[(*index, q, slice(None), at)]


def with_tail(main, tail):
    return lambda q, at: tail[q] if at == TAIL else main[q, :, at]


def conv_columns(get, rows, d, matrix, post, tail=True, taps=(-1, 0, 1, 2)):
    def window(r, at):
        return jnp.concatenate([get(r + k * d, at) for k in taps], axis=0)

    def put(r, at, both):
        post(r, at, both[:C])
        if len(taps) == 4:
            post(r + d, at, both[C:])

    for r in rows:
        for at in MAIN:
            put(r, at, dot(matrix, window(r, at)))
    if tail:
        for r, s in zip(rows[::2], rows[1::2]):
            both = dot(matrix, jnp.concatenate([window(r, TAIL), window(s, TAIL)], axis=1))
            put(r, TAIL, both[:, :128])
            put(s, TAIL, both[:, 128:])


SINGLE = (-1, 0, 1)


def conv_rows(get, rows, d, reverse, matrix, post, tail=True):
    stacks = []
    for r in rows:
        stack = row_stack(get.row(r), d, reverse)
        stacks.append(stack)
        for at in MAIN:
            post(r, at, dot(matrix, stack[:, at]))
    if tail:
        for q in range(0, len(rows), 2):
            both = dot(matrix, jnp.concatenate([stacks[q][:, TAIL], stacks[q + 1][:, TAIL]], axis=1))
            post(rows[q], TAIL, both[:, :128])
            post(rows[q + 1], TAIL, both[:, 128:])
    return stacks


def add_col_taps(acc_ref, grads, hidden, d, rows):
    acc = acc_ref[...]
    for r in rows:
        for at in MAIN:
            left = jnp.concatenate([hidden(r + q * d, at) for q in (0, 1)], axis=0)
            right = jnp.concatenate([grads(r + q * d, at) for q in (-1, 0, 1, 2)], axis=0)
            acc += dot_nt(left, right)
    acc_ref[...] = acc


def add_col_taps_single(acc_ref, grads, hidden, d, rows):
    acc = acc_ref[0:C, 0 : 3 * C]
    for r in rows:
        for at in MAIN:
            right = jnp.concatenate([grads(r + q * d, at) for q in (-1, 0, 1)], axis=0)
            acc += dot_nt(hidden(r, at), right)
    acc_ref[0:C, 0 : 3 * C] = acc


def add_row_taps(acc_ref, values, rows, stacks):
    acc = acc_ref[...]
    for r, stack in zip(rows, stacks):
        for at in MAIN:
            acc += dot_nt(values(r, at), stack[:, at])
    acc_ref[...] = acc


def elu(p):
    return jnp.where(p > 0, p, jnp.exp(p) - 1.0)


def turn_out(src, out):
    for i in range(R // 16):
        for t in range(W // 128):
            at = slice(t * 128, (t + 1) * 128)
            out[:, i * 16 : (i + 1) * 16, at] = turn(src[i * 16 : (i + 1) * 16, :, at])


def call(kernel, name, in_specs, outs, scratch, cost, vmem, *args):
    return pl.pallas_call(
        kernel,
        in_specs=in_specs,
        out_specs=[VM for _ in outs],
        out_shape=outs,
        scratch_shapes=scratch,
        compiler_params=pltpu.CompilerParams(vmem_limit_bytes=vmem * MIB),
        cost_estimate=pl.CostEstimate(flops=cost * 500_000_000, bytes_accessed=cost * 1_000_000, transcendentals=0),
        name=name,
    )(*args)


INNER = R - 2 * FIRST_SPACING
MIDDLE = R - 2 * SECOND_SPACING
OUTER = HALO
D1, D2 = FIRST_SPACING, SECOND_SPACING


def inner_kernel(
    tiles, x, c, left, right, wr, wc,
    xt, h1, b1, h2, ct, cm, a2, cg1, g1, col_acc, row_acc,
    mask,
):
    build_mask(tiles, mask)
    for dst, width, first, count in ((xt, XEDGE, 0, XTILES), (ct, CEDGE, XTILES, CTILES)):
        per = 128 // width

        def edges(g, _):
            for k in range(per):
                dst[g * per + k] = unpack(left[first + g], right[first + g], k, width)
            return 0

        lax.fori_loop(0, count, edges, 0)
    wr1, wr2 = forward_matrix(wr[0]), forward_matrix(wr[1])
    wc1 = two_rows(forward_matrix(wc[0]))
    wr2b = backward_matrix(wr[1])
    wc2b = two_rows(backward_matrix(wc[1], (2, 1, 0)))
    get_x = Rows((0, R, with_tail(x, xt)))
    get_c = Rows((0, R, with_tail(c, ct)))
    get_h1 = Rows((0, R, held(h1)))
    get_b1 = Rows((D1, INNER, held(b1)))
    get_h2 = Rows((D1, INNER, held(h2)))
    get_cm = Rows((0, R, held(cm)))
    get_a2 = Rows((D2, MIDDLE, held(a2)))

    def hidden_one(first):
        def post(row, at, pre):
            h1[row, :, at] = masked(elu(pre).astype(BF16), mask, row, at)

        conv_rows(get_x, [first + q for q in range(8)], D1, False, wr1, post)

    def block_one(first):
        def post(row, at, col):
            b1[row - D1, :, at] = get_x(row, at) + masked(col.astype(BF16), mask, row, at)

        conv_columns(get_h1, [first + q for q in range(D1)], D1, wc1, post)

    def hidden_two(first):
        def post(row, at, pre):
            h2[row - D1, :, at] = masked(elu(pre).astype(BF16), mask, row, at)

        conv_rows(get_b1, [first + q for q in range(8)], D2, False, wr2, post)

    def mask_cot(first):
        for r in range(first, first + 8):
            for at in (*MAIN, TAIL):
                cm[r, :, at] = masked(get_c(r, at), mask, r, at)

    hidden_one(0)
    mask_cot(0)
    hidden_one(8)
    mask_cot(8)
    block_one(4)
    hidden_one(16)
    mask_cot(16)
    block_one(12)
    hidden_two(4)
    hidden_one(24)
    mask_cot(24)
    block_one(20)
    hidden_two(12)
    hidden_two(20)

    def post_two(row, at, hid):
        slope = 1.0 + jnp.minimum(get_h2(row, at), 0).astype(F32)
        a2[row - D2, :, at] = masked((hid * slope).astype(BF16), mask, row, at)

    rows = [D2 + q for q in range(D2)]
    conv_columns(get_cm, rows, D2, wc2b, post_two)
    col_acc[...] = jnp.zeros_like(col_acc)
    row_acc[...] = jnp.zeros_like(row_acc)
    add_col_taps(col_acc, get_cm, get_h2, D2, rows)

    def post_one(row, at, mixed):
        g = get_c(row, at).astype(F32) + mixed
        cg1[row - D2, :, at] = masked(g.astype(BF16), mask, row, at)
        if at != TAIL:
            g1[row - D2, :, at] = g

    for first in range(D2, R - D2, 8):
        rows = list(range(first, first + 8))
        stacks = conv_rows(get_a2, rows, D2, True, wr2b, post_one)
        add_row_taps(row_acc, get_b1, rows, stacks)


def forward_inner(*args):
    return call(
        inner_kernel, "forward_inner", [SM] + [VM] * 6,
        [
            pltpu.VMEM((R, C, 128), BF16),
            pltpu.VMEM((R, C, E), BF16),
            pltpu.VMEM((INNER, C, E), BF16),
            pltpu.VMEM((INNER, C, E), BF16),
            pltpu.VMEM((R, C, 128), BF16),
            pltpu.VMEM((R, C, E), BF16),
            pltpu.VMEM((MIDDLE, C, E), BF16),
            pltpu.VMEM((MIDDLE, C, E), BF16),
            pltpu.VMEM((MIDDLE, C, W), F32),
            pltpu.VMEM((2 * C, 4 * C), F32),
            pltpu.VMEM((C, 3 * C), F32),
        ],
        [pltpu.VMEM((3, 16, E), BF16)],
        14, 8, *args,
    )


def outer_kernel(
    tiles, above, below, x, xt, h1, b1, h2, wr, wc,
    out, b1s, h2s,
    xe, h1e, flat, mask,
):
    build_mask(tiles, mask)
    wr1, wr2 = forward_matrix(wr[0]), forward_matrix(wr[1])
    wc1s = forward_matrix(wc[0])
    wc1, wc2 = two_rows(wc1s), two_rows(forward_matrix(wc[1]))
    per = 128 // XEDGE

    def message(side, ref):
        def get(q, at):
            if at == TAIL:
                return xe[side, q]
            return ref[q if at == MAIN[0] else HALO + q]

        return get

    for side, ref in enumerate((above, below)):
        tile = [ref[2 * HALO + k // 2, :, (k % 2) * 128 : (k % 2 + 1) * 128] for k in range(6)]
        for q in range(HALO):
            xe[side, q] = unpack(tile[q // per], tile[3 + q // per], q % per, XEDGE)
    get_x = Rows((-HALO, HALO, message(0, above)), (0, R, with_tail(x, xt)), (R, HALO, message(1, below)))
    get_h1 = Rows((-HALO, HALO, held(h1e, 0)), (0, R, held(h1)), (R, HALO, held(h1e, 1)))
    get_b1 = Rows((-D2, OUTER, held(b1s, 0)), (D1, INNER, held(b1)), (R - D1, OUTER, held(b1s, 1)))
    get_h2 = Rows((-D2, OUTER, held(h2s, 0)), (D1, INNER, held(h2)), (R - D1, OUTER, held(h2s, 1)))

    def hidden_one(side):
        first = (-HALO, R)[side]

        def post(row, at, pre):
            h1e[side, row - first, :, at] = masked(elu(pre).astype(BF16), mask, row, at)

        conv_rows(get_x, [first + q for q in range(HALO)], D1, False, wr1, post)

    def block_one(side):
        first = (-D2, R - D1)[side]

        def post(row, at, col):
            b1s[side, row - first, :, at] = get_x(row, at) + masked(col.astype(BF16), mask, row, at)

        conv_columns(get_h1, [first + q for q in range(D1)], D1, wc1, post)
        conv_columns(get_h1, [first + 2 * D1 + q for q in range(D1)], D1, wc1s, post, taps=SINGLE)

    def hidden_two(side):
        first = (-D2, R - D1)[side]

        def post(row, at, pre):
            h2s[side, row - first, :, at] = masked(elu(pre).astype(BF16), mask, row, at)

        conv_rows(get_b1, [first + q for q in range(OUTER)], D2, False, wr2, post)

    def last(first):
        def post(row, at, col):
            flat[row, :, at] = get_b1(row, at) + masked(col.astype(BF16), mask, row, at)

        conv_columns(get_h2, [first + q for q in range(D2)], D2, wc2, post, tail=False)

    hidden_one(0)
    block_one(0)
    hidden_one(1)
    hidden_two(0)
    block_one(1)
    last(0)
    hidden_two(1)
    last(2 * D2)
    turn_out(flat, out)


def forward_outer(*args):
    return call(
        outer_kernel, "forward_outer", [SM] + [VM] * 9,
        [
            jax.ShapeDtypeStruct((C, R, W), BF16),
            pltpu.VMEM((2, OUTER, C, E), BF16),
            pltpu.VMEM((2, OUTER, C, E), BF16),
        ],
        [
            pltpu.VMEM((2, HALO, C, 128), BF16),
            pltpu.VMEM((2, HALO, C, E), BF16),
            pltpu.VMEM((R, C, W), BF16),
            pltpu.VMEM((3, 16, E), BF16),
        ],
        14, 16, *args,
    )


PIECES = 32
PIECE = 6 * C // PIECES
REST = D1 + D2


def backward_kernel(
    tiles, above, below, wr, wc, c, ct, cm, a2, cg1, col_in, row_in, x, h1, b1, b1s, h2, h2s,
    taps, a1, g1s,
    cmh, a2s, cg1s, col_acc, row_acc, mask,
):
    build_mask(tiles, mask)
    wr1, wr2 = backward_matrix(wr[0]), backward_matrix(wr[1])
    wc1, wc2 = backward_matrix(wc[0], (2, 1, 0)), backward_matrix(wc[1], (2, 1, 0))
    wc1w, wc2w = two_rows(wc1), two_rows(wc2)
    per = 128 // CEDGE
    for side, ref, skip in ((0, above, 2 * per - HALO), (1, below, 0)):
        first = (-HALO, R)[side]
        tile = [ref[HALO, :, t * 128 : (t + 1) * 128] for t in range(4)]
        for q in range(HALO):
            g, k = divmod(q + skip, per)
            for at in MAIN:
                cmh[side, q, :, at] = masked(ref[q, :, at], mask, first + q, at)
            cmh[side, q, :, TAIL] = masked(unpack(tile[g], tile[2 + g], k, CEDGE), mask, first + q, TAIL)
    get_c = Rows((-HALO, HALO, held(cmh, 0)), (0, R, with_tail(c, ct)), (R, HALO, held(cmh, 1)))
    get_cm = Rows((-HALO, HALO, held(cmh, 0)), (0, R, held(cm)), (R, HALO, held(cmh, 1)))
    get_b1 = Rows((-D2, OUTER, held(b1s, 0)), (D1, INNER, held(b1)), (R - D1, OUTER, held(b1s, 1)))
    get_h2 = Rows((-D2, OUTER, held(h2s, 0)), (D1, INNER, held(h2)), (R - D1, OUTER, held(h2s, 1)))
    get_a2 = Rows((-D1, REST, held(a2s, 0)), (D2, MIDDLE, held(a2)), (R - D2, REST, held(a2s, 1)))
    get_cg1 = Rows((-D1, REST, held(cg1s, 0)), (D2, MIDDLE, held(cg1)), (R - D2, REST, held(cg1s, 1)))
    get_h1 = Rows((0, R, held(h1)))
    get_a1 = Rows((0, R, held(a1)))
    get_x = Rows((0, R, held(x)))
    firsts = (-D1, R - D2)

    col_acc[0] = col_in[...]
    row_acc[0] = row_in[...]
    col_acc[1] = jnp.zeros_like(col_in)
    row_acc[1] = jnp.zeros_like(row_in)
    for side, first in enumerate(firsts):

        def post_two(row, at, hid):
            slope = 1.0 + jnp.minimum(get_h2(row, at), 0).astype(F32)
            a2s[side, row - first, :, at] = masked((hid * slope).astype(BF16), mask, row, at)

        conv_columns(get_cm, [first + q for q in range(D1)], D2, wc2w, post_two)
        conv_columns(get_cm, [first + D1 + q for q in range(D1)], D2, wc2, post_two, taps=SINGLE)
    for side, first in enumerate(firsts):
        own = [r for r in range(first, first + REST) if 0 <= r < R]
        add_col_taps_single(col_acc.at[0], get_cm, get_h2, D2, own)

        def post_one(row, at, mixed):
            g = get_c(row, at).astype(F32) + mixed
            cg1s[side, row - first, :, at] = masked(g.astype(BF16), mask, row, at)
            if at != TAIL and row in own:
                g1s[side, row - own[0], :, at] = g

        rows = list(range(first, first + REST))
        stacks = conv_rows(get_a2, rows, D2, True, wr2, post_one)
        kept = [(r, stack) for r, stack in zip(rows, stacks) if r in own]
        add_row_taps(row_acc.at[0], get_b1, [k[0] for k in kept], [k[1] for k in kept])

    for first in range(0, R, 2 * D1):

        def post(row, at, hid):
            slope = 1.0 + jnp.minimum(h1[row, :, at], 0).astype(F32)
            a1[row, :, at] = masked((hid * slope).astype(BF16), mask, row, at)

        rows = [first + q for q in range(D1)]
        conv_columns(get_cg1, rows, D1, wc1w, post)
        add_col_taps(col_acc.at[1], get_cg1, get_h1, D1, rows)
        rows = list(range(first, first + 2 * D1))
        add_row_taps(row_acc.at[1], get_x, rows, [row_stack(get_a1.row(r), D1, True) for r in rows])

    for k in range(2):
        acc = col_acc[k]
        low, high = acc[:C].T, acc[C:].T
        col = [low[(2 - q) * C : (3 - q) * C] + high[(3 - q) * C : (4 - q) * C] for q in range(3)]
        both = jnp.concatenate([jnp.concatenate(col, axis=0), row_acc[k].T], axis=1)
        for q in range(PIECES // 2):
            taps[k * PIECES // 2 + q] = both[q * PIECE : (q + 1) * PIECE]


def backward(*args):
    return call(
        backward_kernel, "backward", [SM] + [VM] * 17,
        [
            jax.ShapeDtypeStruct((PIECES, PIECE, 2 * C), F32),
            pltpu.VMEM((R, C, E), BF16),
            pltpu.VMEM((2, D2, C, W), F32),
        ],
        [
            pltpu.VMEM((2, HALO, C, E), BF16),
            pltpu.VMEM((2, REST, C, E), BF16),
            pltpu.VMEM((2, REST, C, E), BF16),
            pltpu.VMEM((2, 2 * C, 4 * C), F32),
            pltpu.VMEM((2, C, 3 * C), F32),
            pltpu.VMEM((3, 16, E), BF16),
        ],
        16, 20, *args,
    )


def map_kernel(a1, g1, g1s, wr, out, flat):
    wr1 = backward_matrix(wr[0])
    get_a1 = Rows((0, R, held(a1)))
    get_g1 = Rows((0, D2, held(g1s, 0)), (D2, MIDDLE, held(g1)), (R - D2, D2, held(g1s, 1)))

    def post(row, at, mixed):
        flat[row, :, at] = (get_g1(row, at) + mixed).astype(BF16)

    for first in range(0, R, 8):
        conv_rows(get_a1, [first + q for q in range(8)], D1, True, wr1, post, tail=False)
    turn_out(flat, out)


def backward_map(*args):
    return call(
        map_kernel, "backward_map", [VM] * 4,
        [jax.ShapeDtypeStruct((C, R, W), BF16)],
        [pltpu.VMEM((R, C, W), BF16)],
        4, 10, *args,
    )[0]


def tap_sum(taps, beside):
    part = lax.all_to_all(taps, "rows", 0, 0, tiled=True)
    part = lax.all_gather(part.sum(0), COLS).sum(0)
    spread = jnp.broadcast_to(part[None], taps.shape)
    whole = lax.all_to_all(spread, "rows", 0, 0, tiled=True)
    return whole.reshape(2, 3, C, 2 * C), beside


COLS = ("y_hi", "core")


def in_hbm(array):
    return pltpu.with_memory_space_constraint(array, pltpu.HBM)


def in_vmem(array):
    return pltpu.with_memory_space_constraint(array, pltpu.VMEM)


def on_device(x, tile_mask, wr, wc, cot):
    n_rows, n_cols = lax.axis_size("rows"), lax.axis_size(COLS)
    factor = 1.0 / math.sqrt(R * n_rows * W * n_cols)
    down = [(i, i + 1) for i in range(n_rows - 1)]
    up = [(i + 1, i) for i in range(n_rows - 1)]
    right = [(i, i + 1) for i in range(n_cols - 1)]
    left = [(i + 1, i) for i in range(n_cols - 1)]

    to_left, to_right = pack_edges(x, cot)
    from_right = in_vmem(lax.ppermute(to_left, COLS, left))
    from_left = in_vmem(lax.ppermute(to_right, COLS, right))
    xt, x_up, x_down, ct, c_up, c_down = turn_both(x, cot)
    x_up, x_down, c_up, c_down = fill((x_up, x_down, c_up, c_down), from_left, from_right)
    x_above = in_vmem(lax.ppermute(x_down, "rows", down))
    x_below = in_vmem(lax.ppermute(x_up, "rows", up))
    c_above = in_vmem(lax.ppermute(c_down, "rows", down))
    c_below = in_vmem(lax.ppermute(c_up, "rows", up))

    xt, ct = in_vmem(xt), in_vmem(ct)
    x_tail, h1, b1, h2, c_tail, cm, a2, cg1, g1, col_taps, row_taps = map(
        in_vmem, forward_inner(tile_mask, xt, ct, from_left, from_right, wr, wc)
    )
    final, b1s, h2s = forward_outer(tile_mask, x_above, x_below, xt, x_tail, h1, b1, h2, wr, wc)
    b1s, h2s = in_vmem(b1s), in_vmem(h2s)
    taps, a1, g1s = backward(
        tile_mask, c_above, c_below, wr, wc, ct, c_tail, cm, a2, cg1, col_taps, row_taps,
        xt, h1, b1, b1s, h2, h2s,
    )
    total, map_grad = tap_sum(taps, backward_map(in_vmem(a1), g1, in_vmem(g1s), wr))
    total = total[::-1] * factor
    return final, map_grad, total[..., C:], total[..., :C]


def solution(mesh):
    n_rows, n_cols = mesh.devices.shape
    inner = Mesh(mesh.devices.reshape(n_rows, n_cols // 2, 2), ("rows",) + COLS)
    blocks = P(None, "rows", COLS)
    return jax.shard_map(
        on_device,
        mesh=inner,
        in_specs=(blocks, P(), P(), P(), blocks),
        out_specs=(blocks, blocks, P(), P()),
        check_vma=False,
    )
```

```python
import functools
import math

import jax
import jax.numpy as jnp
from jax import lax
from jax.experimental import pallas as pl
from jax.experimental.pallas import tpu as pltpu
from jax.sharding import Mesh, PartitionSpec as P

FIRST_SPACING = 4
SECOND_SPACING = 8
TILE = 128
C = 64
R = 32
W = 512
E = 640
HALO = 12
XEDGE = 32
CEDGE = 16
XTILES = R * XEDGE // 128
CTILES = R * CEDGE // 128
F32 = jnp.float32
BF16 = jnp.bfloat16
MIB = 1024 * 1024


def dot(a, b):
    return jnp.dot(a, b, preferred_element_type=F32)


def dot_nt(a, b):
    return lax.dot_general(a, b, (((1,), (1,)), ((), ())), preferred_element_type=F32)


def turn(block):
    return jnp.swapaxes(block, 0, 1)


def lanes(first, count, channels):
    lane = lax.broadcasted_iota(jnp.int32, (channels, 128), 1)
    return ((lane >= first) & (lane < first + count)).astype(F32).astype(BF16)


def rolled(v, shift):
    shift = shift % 128
    return pltpu.roll(v, shift, 1) if shift else v


def pack(rows, width, first):
    keep = lanes(first, width, rows[0].shape[0])
    parts = [rolled(v * keep, width * k - first) for k, v in enumerate(rows)]
    return functools.reduce(jnp.add, parts)


def unpack(left, right, k, width):
    channels = left.shape[0]
    ahead = rolled(right, -width * k) * lanes(0, width, channels)
    behind = rolled(left, 128 - width - width * k) * lanes(128 - width, width, channels)
    return ahead + behind


GC = 16


def edge_kernel(x_low, x_high, c_low, c_high, to_left, to_right):
    for src, width, at in ((x_low, XEDGE, 0), (c_low, CEDGE, XTILES)):
        for i in range(2):
            rows = turn(src[:, i * 16 : (i + 1) * 16, :])
            per = 128 // width
            for g in range(16 // per):
                tile = pack([rows[g * per + k] for k in range(per)], width, 0)
                to_left[at + (i * 16) // per + g] = tile
    for src, width, at in ((x_high, XEDGE, 0), (c_high, CEDGE, XTILES)):
        for i in range(2):
            rows = turn(src[:, i * 16 : (i + 1) * 16, :])
            per = 128 // width
            for g in range(16 // per):
                tile = pack([rows[g * per + k] for k in range(per)], width, 128 - width)
                to_right[at + (i * 16) // per + g] = tile


def pack_edges(x, c):
    low = pl.BlockSpec((GC, R, 128), lambda g: (g, 0, 0))
    high = pl.BlockSpec((GC, R, 128), lambda g: (g, 0, W // 128 - 1))
    out = pl.BlockSpec((XTILES + CTILES, GC, 128), lambda g: (0, g, 0))
    return pl.pallas_call(
        edge_kernel,
        grid=(C // GC,),
        in_specs=[low, high, low, high],
        out_specs=[out, out],
        out_shape=[jax.ShapeDtypeStruct((XTILES + CTILES, C, 128), BF16)] * 2,
        compiler_params=pltpu.CompilerParams(vmem_limit_bytes=16 * MIB),
        name="pack_edges",
    )(x, x, c, c)


def turn_block(src, dst):
    for i in range(R // 16):
        for t in range(W // 128):
            at = slice(t * 128, (t + 1) * 128)
            dst[i * 16 : (i + 1) * 16, :, at] = turn(src[:, i * 16 : (i + 1) * 16, at])


XROWS = 2 * HALO + 3
CROWS = HALO + 1


def turn_kernel(x_ref, c_ref, xt, x_up, x_down, ct, c_up, c_down):
    turn_block(x_ref, xt)
    for out, rows in ((x_up, slice(0, HALO)), (x_down, slice(R - HALO, R))):
        out[0:HALO] = xt[rows, :, MAIN[0]]
        out[HALO : 2 * HALO] = xt[rows, :, MAIN[1]]
    turn_block(c_ref, ct)
    c_up[0:HALO] = ct[0:HALO]
    c_down[0:HALO] = ct[R - HALO : R]


def message(rows, width):
    return (
        pl.BlockSpec((rows, GC, width), lambda g: (0, g, 0)),
        pltpu.HBM((rows, C, width), BF16),
    )


def turn_both(x, c):
    native = pl.BlockSpec((GC, R, W), lambda g: (g, 0, 0))
    turned = pl.BlockSpec((R, GC, W), lambda g: (0, g, 0))
    block = pltpu.VMEM((R, C, W), BF16)
    (xs, x_shape), (cs, c_shape) = message(XROWS, W // 2), message(CROWS, W)
    return pl.pallas_call(
        turn_kernel,
        grid=(C // GC,),
        in_specs=[native, native],
        out_specs=[turned, xs, xs, turned, cs, cs],
        out_shape=[block, x_shape, x_shape, block, c_shape, c_shape],
        compiler_params=pltpu.CompilerParams(vmem_limit_bytes=16 * MIB),
        name="turn_both",
    )(x, c)


def fill_kernel(
    x_up_in, x_down_in, c_up_in, c_down_in, left, right, x_up, x_down, c_up, c_down, x_rows, c_rows, sems
):
    copies = []
    for q, (out, first) in enumerate(((x_up, 0), (x_down, XTILES - 3))):
        tiles = [left[first + k] for k in range(3)] + [right[first + k] for k in range(3)]
        for k in range(3):
            x_rows[q, k] = jnp.concatenate(tiles[2 * k : 2 * k + 2], axis=1)
        copies.append(pltpu.make_async_copy(x_rows.at[q], out.at[2 * HALO : XROWS], sems.at[q]))
    for q, (out, first) in enumerate(((c_up, XTILES), (c_down, XTILES + CTILES - 2))):
        tiles = [left[first], left[first + 1], right[first], right[first + 1]]
        c_rows[q] = jnp.concatenate(tiles, axis=1)
        copies.append(pltpu.make_async_copy(c_rows.at[q], out.at[HALO], sems.at[2 + q]))
    for copy in copies:
        copy.start()
    for copy in copies:
        copy.wait()


def fill(messages, left, right):
    return pl.pallas_call(
        fill_kernel,
        in_specs=[ANY] * 4 + [VM, VM],
        out_specs=[ANY] * 4,
        out_shape=[pltpu.HBM(m.shape, BF16) for m in messages],
        input_output_aliases={q: q for q in range(4)},
        scratch_shapes=[
            pltpu.VMEM((2, 3, C, W // 2), BF16),
            pltpu.VMEM((2, C, W), BF16),
            pltpu.SemaphoreType.DMA((4,)),
        ],
        compiler_params=pltpu.CompilerParams(vmem_limit_bytes=8 * MIB),
        name="fill_messages",
    )(*map(in_hbm, messages), left, right)


ANY = pl.BlockSpec(memory_space=pl.ANY)
VM = pl.BlockSpec(memory_space=pltpu.VMEM)
SM = pl.BlockSpec(memory_space=pltpu.SMEM)
STEP = 8
LONG = 16


def build_mask(tiles, mask):
    row_dev, col_dev = lax.axis_index("rows"), lax.axis_index(COLS)
    n_rows, n_cols = tiles.shape
    first_row, first_tile = row_dev * R, col_dev * (W // TILE)
    lane = lax.broadcasted_iota(jnp.int32, (16, 128), 1)

    def value(p, ct):
        cell = first_row + (-1, 0, R)[p]
        inside = (cell >= 0) & (cell < n_rows * TILE) & (ct >= 0) & (ct < n_cols)
        rt = jnp.clip(cell, 0, n_rows * TILE - 1) // TILE
        return jnp.where(inside, tiles[rt, jnp.clip(ct, 0, n_cols - 1)], 0)

    for p in range(3):
        for t in range(W // 128):
            cell = jnp.full((16, 128), value(p, first_tile + t), jnp.int32)
            mask[p, :, t * 128 : (t + 1) * 128] = cell.astype(F32).astype(BF16)
        right = jnp.full((16, 128), value(p, first_tile + W // TILE), jnp.int32)
        left = jnp.full((16, 128), value(p, first_tile - 1), jnp.int32)
        mask[p, :, W:E] = jnp.where(lane < 64, right, left).astype(F32).astype(BF16)


def masked(v, mask, r, at):
    if isinstance(r, int):
        p = int(r >= 0) + int(r >= R)
    else:
        p = (r >= 0).astype(jnp.int32) + (r >= R).astype(jnp.int32)
    m = mask[p, :, at]
    return v * jnp.concatenate([m] * (C // 16), axis=0)


def shifted(v, d):
    return pltpu.roll(v, (-d) % v.shape[1], 1)


def row_stack(v, d, reverse):
    ahead, behind = shifted(v, d), shifted(v, -d)
    parts = [ahead, v, behind] if reverse else [behind, v, ahead]
    return jnp.concatenate(parts, axis=0)


def forward_matrix(w):
    return jnp.concatenate([w[j].astype(F32).T for j in range(3)], axis=0).T.astype(BF16)


def backward_matrix(w, order=(0, 1, 2)):
    return jnp.concatenate([w[j].astype(F32) for j in order], axis=0).T.astype(BF16)


def two_rows(matrix):
    none = jnp.zeros((C, C), BF16)
    return jnp.concatenate(
        [jnp.concatenate([matrix, none], axis=1), jnp.concatenate([none, matrix], axis=1)], axis=0
    )


MAIN = (slice(0, 256), slice(256, 512))
TAIL = slice(W, E)


class Rows:
    def __init__(self, *parts):
        self.parts = parts

    def __call__(self, r, at):
        for first, count, get in self.parts:
            if first <= r < first + count:
                return get(r - first, at)
        raise IndexError(r)

    def row(self, r):
        return jnp.concatenate([self(r, at) for at in (*MAIN, TAIL)], axis=1)


def held(ref, *index):
    return lambda q, at: ref[(*index, q, slice(None), at)]


def with_tail(main, tail):
    return lambda q, at: tail[q] if at == TAIL else main[q, :, at]


def conv_columns(get, rows, d, matrix, post, tail=True, taps=(-1, 0, 1, 2)):
    def window(r, at):
        return jnp.concatenate([get(r + k * d, at) for k in taps], axis=0)

    def put(r, at, both):
        post(r, at, both[:C])
        if len(taps) == 4:
            post(r + d, at, both[C:])

    for r in rows:
        for at in MAIN:
            put(r, at, dot(matrix, window(r, at)))
    if tail:
        for r, s in zip(rows[::2], rows[1::2]):
            both = dot(matrix, jnp.concatenate([window(r, TAIL), window(s, TAIL)], axis=1))
            put(r, TAIL, both[:, :128])
            put(s, TAIL, both[:, 128:])


SINGLE = (-1, 0, 1)


def conv_rows(get, rows, d, reverse, matrix, post, tail=True):
    stacks = []
    for r in rows:
        stack = row_stack(get.row(r), d, reverse)
        stacks.append(stack)
        for at in MAIN:
            post(r, at, dot(matrix, stack[:, at]))
    if tail:
        for q in range(0, len(rows), 2):
            both = dot(matrix, jnp.concatenate([stacks[q][:, TAIL], stacks[q + 1][:, TAIL]], axis=1))
            post(rows[q], TAIL, both[:, :128])
            post(rows[q + 1], TAIL, both[:, 128:])
    return stacks


def add_col_taps(acc_ref, grads, hidden, d, rows):
    acc = acc_ref[...]
    for r in rows:
        for at in MAIN:
            left = jnp.concatenate([hidden(r + q * d, at) for q in (0, 1)], axis=0)
            right = jnp.concatenate([grads(r + q * d, at) for q in (-1, 0, 1, 2)], axis=0)
            acc += dot_nt(left, right)
    acc_ref[...] = acc


def add_col_taps_single(acc_ref, grads, hidden, d, rows):
    acc = acc_ref[0:C, 0 : 3 * C]
    for r in rows:
        for at in MAIN:
            right = jnp.concatenate([grads(r + q * d, at) for q in (-1, 0, 1)], axis=0)
            acc += dot_nt(hidden(r, at), right)
    acc_ref[0:C, 0 : 3 * C] = acc


def add_row_taps(acc_ref, values, rows, stacks):
    acc = acc_ref[...]
    for r, stack in zip(rows, stacks):
        for at in MAIN:
            acc += dot_nt(values(r, at), stack[:, at])
    acc_ref[...] = acc


def elu(p):
    return jnp.where(p > 0, p, jnp.exp(p) - 1.0)


def turn_out(src, out):
    for i in range(R // 16):
        for t in range(W // 128):
            at = slice(t * 128, (t + 1) * 128)
            out[:, i * 16 : (i + 1) * 16, at] = turn(src[i * 16 : (i + 1) * 16, :, at])


def call(kernel, name, in_specs, outs, scratch, cost, vmem, *args):
    return pl.pallas_call(
        kernel,
        in_specs=in_specs,
        out_specs=[ANY if getattr(out, "memory_space", None) == pltpu.HBM else VM for out in outs],
        out_shape=outs,
        scratch_shapes=scratch,
        compiler_params=pltpu.CompilerParams(vmem_limit_bytes=vmem * MIB),
        cost_estimate=pl.CostEstimate(flops=cost * 500_000_000, bytes_accessed=cost * 1_000_000, transcendentals=0),
        name=name,
    )(*args)


INNER = R - 2 * FIRST_SPACING
MIDDLE = R - 2 * SECOND_SPACING
OUTER = HALO
D1, D2 = FIRST_SPACING, SECOND_SPACING


def inner_kernel(
    tiles, x, c, left, right, wr, wc,
    xt, h1, b1, h2, ct, cm, a2, cg1, g1, col_acc, row_acc,
    mask,
):
    build_mask(tiles, mask)
    for dst, width, first, count in ((xt, XEDGE, 0, XTILES), (ct, CEDGE, XTILES, CTILES)):
        per = 128 // width

        def edges(g, _):
            for k in range(per):
                dst[g * per + k] = unpack(left[first + g], right[first + g], k, width)
            return 0

        lax.fori_loop(0, count, edges, 0)
    wr1, wr2 = forward_matrix(wr[0]), forward_matrix(wr[1])
    wc1 = two_rows(forward_matrix(wc[0]))
    wr2b = backward_matrix(wr[1])
    wc2b = two_rows(backward_matrix(wc[1], (2, 1, 0)))
    get_x = Rows((0, R, with_tail(x, xt)))
    get_c = Rows((0, R, with_tail(c, ct)))
    get_h1 = Rows((0, R, held(h1)))
    get_b1 = Rows((D1, INNER, held(b1)))
    get_h2 = Rows((D1, INNER, held(h2)))
    get_cm = Rows((0, R, held(cm)))
    get_a2 = Rows((D2, MIDDLE, held(a2)))

    def hidden_one(first):
        def post(row, at, pre):
            h1[row, :, at] = masked(elu(pre).astype(BF16), mask, row, at)

        conv_rows(get_x, [first + q for q in range(8)], D1, False, wr1, post)

    def block_one(first):
        def post(row, at, col):
            b1[row - D1, :, at] = get_x(row, at) + masked(col.astype(BF16), mask, row, at)

        conv_columns(get_h1, [first + q for q in range(D1)], D1, wc1, post)

    def hidden_two(first):
        def post(row, at, pre):
            h2[row - D1, :, at] = masked(elu(pre).astype(BF16), mask, row, at)

        conv_rows(get_b1, [first + q for q in range(8)], D2, False, wr2, post)

    def mask_cot(first):
        for r in range(first, first + 8):
            for at in (*MAIN, TAIL):
                cm[r, :, at] = masked(get_c(r, at), mask, r, at)

    hidden_one(0)
    mask_cot(0)
    hidden_one(8)
    mask_cot(8)
    block_one(4)
    hidden_one(16)
    mask_cot(16)
    block_one(12)
    hidden_two(4)
    hidden_one(24)
    mask_cot(24)
    block_one(20)
    hidden_two(12)
    hidden_two(20)

    def post_two(row, at, hid):
        slope = 1.0 + jnp.minimum(get_h2(row, at), 0).astype(F32)
        a2[row - D2, :, at] = masked((hid * slope).astype(BF16), mask, row, at)

    rows = [D2 + q for q in range(D2)]
    conv_columns(get_cm, rows, D2, wc2b, post_two)
    col_acc[...] = jnp.zeros_like(col_acc)
    row_acc[...] = jnp.zeros_like(row_acc)
    add_col_taps(col_acc, get_cm, get_h2, D2, rows)

    def post_one(row, at, mixed):
        g = get_c(row, at).astype(F32) + mixed
        cg1[row - D2, :, at] = masked(g.astype(BF16), mask, row, at)
        if at != TAIL:
            g1[row - D2, :, at] = g

    for first in range(D2, R - D2, 8):
        rows = list(range(first, first + 8))
        stacks = conv_rows(get_a2, rows, D2, True, wr2b, post_one)
        add_row_taps(row_acc, get_b1, rows, stacks)


def forward_inner(*args):
    return call(
        inner_kernel, "forward_inner", [SM] + [VM] * 6,
        [
            pltpu.VMEM((R, C, 128), BF16),
            pltpu.VMEM((R, C, E), BF16),
            pltpu.VMEM((INNER, C, E), BF16),
            pltpu.VMEM((INNER, C, E), BF16),
            pltpu.VMEM((R, C, 128), BF16),
            pltpu.VMEM((R, C, E), BF16),
            pltpu.VMEM((MIDDLE, C, E), BF16),
            pltpu.VMEM((MIDDLE, C, E), BF16),
            pltpu.VMEM((MIDDLE, C, W), F32),
            pltpu.VMEM((2 * C, 4 * C), F32),
            pltpu.VMEM((C, 3 * C), F32),
        ],
        [pltpu.VMEM((3, 16, E), BF16)],
        14, 8, *args,
    )


def outer_kernel(
    tiles, above, below, x, xt, h1, b1, h2, wr, wc,
    out, b1s, h2s,
    xe, h1e, flat, mask,
):
    build_mask(tiles, mask)
    wr1, wr2 = forward_matrix(wr[0]), forward_matrix(wr[1])
    wc1s = forward_matrix(wc[0])
    wc1, wc2 = two_rows(wc1s), two_rows(forward_matrix(wc[1]))
    per = 128 // XEDGE

    def message(side, ref):
        def get(q, at):
            if at == TAIL:
                return xe[side, q]
            return ref[q if at == MAIN[0] else HALO + q]

        return get

    for side, ref in enumerate((above, below)):
        tile = [ref[2 * HALO + k // 2, :, (k % 2) * 128 : (k % 2 + 1) * 128] for k in range(6)]
        for q in range(HALO):
            xe[side, q] = unpack(tile[q // per], tile[3 + q // per], q % per, XEDGE)
    get_x = Rows((-HALO, HALO, message(0, above)), (0, R, with_tail(x, xt)), (R, HALO, message(1, below)))
    get_h1 = Rows((-HALO, HALO, held(h1e, 0)), (0, R, held(h1)), (R, HALO, held(h1e, 1)))
    get_b1 = Rows((-D2, OUTER, held(b1s, 0)), (D1, INNER, held(b1)), (R - D1, OUTER, held(b1s, 1)))
    get_h2 = Rows((-D2, OUTER, held(h2s, 0)), (D1, INNER, held(h2)), (R - D1, OUTER, held(h2s, 1)))

    def hidden_one(side):
        first = (-HALO, R)[side]

        def post(row, at, pre):
            h1e[side, row - first, :, at] = masked(elu(pre).astype(BF16), mask, row, at)

        conv_rows(get_x, [first + q for q in range(HALO)], D1, False, wr1, post)

    def block_one(side):
        first = (-D2, R - D1)[side]

        def post(row, at, col):
            b1s[side, row - first, :, at] = get_x(row, at) + masked(col.astype(BF16), mask, row, at)

        conv_columns(get_h1, [first + q for q in range(D1)], D1, wc1, post)
        conv_columns(get_h1, [first + 2 * D1 + q for q in range(D1)], D1, wc1s, post, taps=SINGLE)

    def hidden_two(side):
        first = (-D2, R - D1)[side]

        def post(row, at, pre):
            h2s[side, row - first, :, at] = masked(elu(pre).astype(BF16), mask, row, at)

        conv_rows(get_b1, [first + q for q in range(OUTER)], D2, False, wr2, post)

    def last(first):
        def post(row, at, col):
            flat[row, :, at] = get_b1(row, at) + masked(col.astype(BF16), mask, row, at)

        conv_columns(get_h2, [first + q for q in range(D2)], D2, wc2, post, tail=False)

    hidden_one(0)
    block_one(0)
    hidden_one(1)
    hidden_two(0)
    block_one(1)
    last(0)
    hidden_two(1)
    last(2 * D2)
    turn_out(flat, out)


def forward_outer(*args):
    return call(
        outer_kernel, "forward_outer", [SM] + [VM] * 9,
        [
            jax.ShapeDtypeStruct((C, R, W), BF16),
            pltpu.VMEM((2, OUTER, C, E), BF16),
            pltpu.VMEM((2, OUTER, C, E), BF16),
        ],
        [
            pltpu.VMEM((2, HALO, C, 128), BF16),
            pltpu.VMEM((2, HALO, C, E), BF16),
            pltpu.VMEM((R, C, W), BF16),
            pltpu.VMEM((3, 16, E), BF16),
        ],
        14, 16, *args,
    )


PIECES = 32
PIECE = 6 * C // PIECES
REST = D1 + D2


def backward_kernel(
    tiles, above, below, wr, wc, c, ct, cm, a2, cg1, g1, col_in, row_in, x, h1, b1, b1s, h2, h2s,
    taps, a1, g1_out,
    cmh, a2s, cg1s, g1s, col_acc, row_acc, mask, sems,
):
    saves = [pltpu.make_async_copy(g1, g1_out.at[D2 : R - D2], sems.at[0])]
    saves[0].start()
    build_mask(tiles, mask)
    wr1, wr2 = backward_matrix(wr[0]), backward_matrix(wr[1])
    wc1, wc2 = backward_matrix(wc[0], (2, 1, 0)), backward_matrix(wc[1], (2, 1, 0))
    wc1w, wc2w = two_rows(wc1), two_rows(wc2)
    per = 128 // CEDGE
    for side, ref, skip in ((0, above, 2 * per - HALO), (1, below, 0)):
        first = (-HALO, R)[side]
        tile = [ref[HALO, :, t * 128 : (t + 1) * 128] for t in range(4)]
        for q in range(HALO):
            g, k = divmod(q + skip, per)
            for at in MAIN:
                cmh[side, q, :, at] = masked(ref[q, :, at], mask, first + q, at)
            cmh[side, q, :, TAIL] = masked(unpack(tile[g], tile[2 + g], k, CEDGE), mask, first + q, TAIL)
    get_c = Rows((-HALO, HALO, held(cmh, 0)), (0, R, with_tail(c, ct)), (R, HALO, held(cmh, 1)))
    get_cm = Rows((-HALO, HALO, held(cmh, 0)), (0, R, held(cm)), (R, HALO, held(cmh, 1)))
    get_b1 = Rows((-D2, OUTER, held(b1s, 0)), (D1, INNER, held(b1)), (R - D1, OUTER, held(b1s, 1)))
    get_h2 = Rows((-D2, OUTER, held(h2s, 0)), (D1, INNER, held(h2)), (R - D1, OUTER, held(h2s, 1)))
    get_a2 = Rows((-D1, REST, held(a2s, 0)), (D2, MIDDLE, held(a2)), (R - D2, REST, held(a2s, 1)))
    get_cg1 = Rows((-D1, REST, held(cg1s, 0)), (D2, MIDDLE, held(cg1)), (R - D2, REST, held(cg1s, 1)))
    get_h1 = Rows((0, R, held(h1)))
    get_a1 = Rows((0, R, held(a1)))
    get_x = Rows((0, R, held(x)))
    firsts = (-D1, R - D2)

    col_acc[0] = col_in[...]
    row_acc[0] = row_in[...]
    col_acc[1] = jnp.zeros_like(col_in)
    row_acc[1] = jnp.zeros_like(row_in)
    for side, first in enumerate(firsts):

        def post_two(row, at, hid):
            slope = 1.0 + jnp.minimum(get_h2(row, at), 0).astype(F32)
            a2s[side, row - first, :, at] = masked((hid * slope).astype(BF16), mask, row, at)

        conv_columns(get_cm, [first + q for q in range(D1)], D2, wc2w, post_two)
        conv_columns(get_cm, [first + D1 + q for q in range(D1)], D2, wc2, post_two, taps=SINGLE)
    for side, first in enumerate(firsts):
        own = [r for r in range(first, first + REST) if 0 <= r < R]
        add_col_taps_single(col_acc.at[0], get_cm, get_h2, D2, own)

        def post_one(row, at, mixed):
            g = get_c(row, at).astype(F32) + mixed
            cg1s[side, row - first, :, at] = masked(g.astype(BF16), mask, row, at)
            if at != TAIL and row in own:
                g1s[side, row - own[0], :, at] = g

        rows = list(range(first, first + REST))
        stacks = conv_rows(get_a2, rows, D2, True, wr2, post_one)
        kept = [(r, stack) for r, stack in zip(rows, stacks) if r in own]
        add_row_taps(row_acc.at[0], get_b1, [k[0] for k in kept], [k[1] for k in kept])
        saves.append(pltpu.make_async_copy(g1s.at[side], g1_out.at[own[0] : own[0] + D2], sems.at[1 + side]))
        saves[-1].start()

    for first in range(0, R, 2 * D1):

        def post(row, at, hid):
            slope = 1.0 + jnp.minimum(h1[row, :, at], 0).astype(F32)
            a1[row, :, at] = masked((hid * slope).astype(BF16), mask, row, at)

        rows = [first + q for q in range(D1)]
        conv_columns(get_cg1, rows, D1, wc1w, post)
        add_col_taps(col_acc.at[1], get_cg1, get_h1, D1, rows)
        rows = list(range(first, first + 2 * D1))
        add_row_taps(row_acc.at[1], get_x, rows, [row_stack(get_a1.row(r), D1, True) for r in rows])

    for k in range(2):
        acc = col_acc[k]
        low, high = acc[:C].T, acc[C:].T
        col = [low[(2 - q) * C : (3 - q) * C] + high[(3 - q) * C : (4 - q) * C] for q in range(3)]
        both = jnp.concatenate([jnp.concatenate(col, axis=0), row_acc[k].T], axis=1)
        for q in range(PIECES // 2):
            taps[k * PIECES // 2 + q] = both[q * PIECE : (q + 1) * PIECE]
    for save in saves:
        save.wait()


def backward(*args):
    return call(
        backward_kernel, "backward", [SM] + [VM] * 18,
        [
            jax.ShapeDtypeStruct((PIECES, PIECE, 2 * C), F32),
            pltpu.VMEM((R, C, E), BF16),
            pltpu.HBM((R, C, W), F32),
        ],
        [
            pltpu.VMEM((2, HALO, C, E), BF16),
            pltpu.VMEM((2, REST, C, E), BF16),
            pltpu.VMEM((2, REST, C, E), BF16),
            pltpu.VMEM((2, D2, C, W), F32),
            pltpu.VMEM((2, 2 * C, 4 * C), F32),
            pltpu.VMEM((2, C, 3 * C), F32),
            pltpu.VMEM((3, 16, E), BF16),
            pltpu.SemaphoreType.DMA((3,)),
        ],
        16, 20, *args,
    )


def map_kernel(a1, g1_in, wr, out, g1, flat, sems):
    loads = [pltpu.make_async_copy(g1_in.at[r : r + 8], g1.at[r : r + 8], sems.at[r // 8]) for r in range(0, R, 8)]
    for load in loads:
        load.start()
    wr1 = backward_matrix(wr[0])
    get_a1 = Rows((0, R, held(a1)))

    def post(row, at, mixed):
        flat[row, :, at] = (g1[row, :, at] + mixed).astype(BF16)

    for load, first in zip(loads, range(0, R, 8)):
        load.wait()
        conv_rows(get_a1, [first + q for q in range(8)], D1, True, wr1, post, tail=False)
    turn_out(flat, out)


def backward_map(*args):
    return call(
        map_kernel, "backward_map", [VM, ANY, VM],
        [jax.ShapeDtypeStruct((C, R, W), BF16)],
        [pltpu.VMEM((R, C, W), F32), pltpu.VMEM((R, C, W), BF16), pltpu.SemaphoreType.DMA((R // 8,))],
        4, 14, *args,
    )[0]


def tap_sum(taps, beside):
    part = lax.all_to_all(taps, "rows", 0, 0, tiled=True)
    part = lax.all_gather(part.sum(0), COLS).sum(0)
    spread = jnp.broadcast_to(part[None], taps.shape)
    whole = lax.all_to_all(spread, "rows", 0, 0, tiled=True)
    return whole.reshape(2, 3, C, 2 * C), beside


COLS = ("y_hi", "core")


def in_hbm(array):
    return pltpu.with_memory_space_constraint(array, pltpu.HBM)


def in_vmem(array):
    return pltpu.with_memory_space_constraint(array, pltpu.VMEM)


def on_device(x, tile_mask, wr, wc, cot):
    n_rows, n_cols = lax.axis_size("rows"), lax.axis_size(COLS)
    factor = 1.0 / math.sqrt(R * n_rows * W * n_cols)
    down = [(i, i + 1) for i in range(n_rows - 1)]
    up = [(i + 1, i) for i in range(n_rows - 1)]
    right = [(i, i + 1) for i in range(n_cols - 1)]
    left = [(i + 1, i) for i in range(n_cols - 1)]

    to_left, to_right = pack_edges(x, cot)
    from_right = in_vmem(lax.ppermute(to_left, COLS, left))
    from_left = in_vmem(lax.ppermute(to_right, COLS, right))
    xt, x_up, x_down, ct, c_up, c_down = turn_both(x, cot)
    x_up, x_down, c_up, c_down = fill((x_up, x_down, c_up, c_down), from_left, from_right)
    x_above = in_vmem(lax.ppermute(x_down, "rows", down))
    x_below = in_vmem(lax.ppermute(x_up, "rows", up))
    c_above = in_vmem(lax.ppermute(c_down, "rows", down))
    c_below = in_vmem(lax.ppermute(c_up, "rows", up))

    xt, ct = in_vmem(xt), in_vmem(ct)
    x_tail, h1, b1, h2, c_tail, cm, a2, cg1, g1, col_taps, row_taps = map(
        in_vmem, forward_inner(tile_mask, xt, ct, from_left, from_right, wr, wc)
    )
    final, b1s, h2s = forward_outer(tile_mask, x_above, x_below, xt, x_tail, h1, b1, h2, wr, wc)
    b1s, h2s = in_vmem(b1s), in_vmem(h2s)
    taps, a1, g1 = backward(
        tile_mask, c_above, c_below, wr, wc, ct, c_tail, cm, a2, cg1, g1, col_taps, row_taps,
        xt, h1, b1, b1s, h2, h2s,
    )
    total, map_grad = tap_sum(taps, backward_map(in_vmem(a1), in_hbm(g1), wr))
    total = total[::-1] * factor
    return final, map_grad, total[..., C:], total[..., :C]


def solution(mesh):
    n_rows, n_cols = mesh.devices.shape
    inner = Mesh(mesh.devices.reshape(n_rows, n_cols // 2, 2), ("rows",) + COLS)
    blocks = P(None, "rows", COLS)
    return jax.shard_map(
        on_device,
        mesh=inner,
        in_specs=(blocks, P(), P(), P(), blocks),
        out_specs=(blocks, blocks, P(), P()),
        check_vma=False,
    )
```

```python
import functools
import math

import jax
import jax.numpy as jnp
from jax import lax
from jax.experimental import pallas as pl
from jax.experimental.pallas import tpu as pltpu
from jax.sharding import Mesh, PartitionSpec as P

FIRST_SPACING = 4
SECOND_SPACING = 8
TILE = 128
C = 64
R = 32
W = 512
E = 640
HALO = 12
XEDGE = 32
CEDGE = 16
XTILES = R * XEDGE // 128
CTILES = R * CEDGE // 128
F32 = jnp.float32
BF16 = jnp.bfloat16
MIB = 1024 * 1024


def dot(a, b):
    return jnp.dot(a, b, preferred_element_type=F32)


def dot_nt(a, b):
    return lax.dot_general(a, b, (((1,), (1,)), ((), ())), preferred_element_type=F32)


def turn(block):
    return jnp.swapaxes(block, 0, 1)


def lanes(first, count, channels):
    lane = lax.broadcasted_iota(jnp.int32, (channels, 128), 1)
    return ((lane >= first) & (lane < first + count)).astype(F32).astype(BF16)


def rolled(v, shift):
    shift = shift % 128
    return pltpu.roll(v, shift, 1) if shift else v


def pack(rows, width, first):
    keep = lanes(first, width, rows[0].shape[0])
    parts = [rolled(v * keep, width * k - first) for k, v in enumerate(rows)]
    return functools.reduce(jnp.add, parts)


def unpack(left, right, k, width):
    channels = left.shape[0]
    ahead = rolled(right, -width * k) * lanes(0, width, channels)
    behind = rolled(left, 128 - width - width * k) * lanes(128 - width, width, channels)
    return ahead + behind


GC = 16


def edge_kernel(x_low, x_high, c_low, c_high, to_left, to_right):
    for src, width, at in ((x_low, XEDGE, 0), (c_low, CEDGE, XTILES)):
        for i in range(2):
            rows = turn(src[:, i * 16 : (i + 1) * 16, :])
            per = 128 // width
            for g in range(16 // per):
                tile = pack([rows[g * per + k] for k in range(per)], width, 0)
                to_left[at + (i * 16) // per + g] = tile
    for src, width, at in ((x_high, XEDGE, 0), (c_high, CEDGE, XTILES)):
        for i in range(2):
            rows = turn(src[:, i * 16 : (i + 1) * 16, :])
            per = 128 // width
            for g in range(16 // per):
                tile = pack([rows[g * per + k] for k in range(per)], width, 128 - width)
                to_right[at + (i * 16) // per + g] = tile


def pack_edges(x, c):
    low = pl.BlockSpec((GC, R, 128), lambda g: (g, 0, 0))
    high = pl.BlockSpec((GC, R, 128), lambda g: (g, 0, W // 128 - 1))
    out = pl.BlockSpec((XTILES + CTILES, GC, 128), lambda g: (0, g, 0))
    return pl.pallas_call(
        edge_kernel,
        grid=(C // GC,),
        in_specs=[low, high, low, high],
        out_specs=[out, out],
        out_shape=[jax.ShapeDtypeStruct((XTILES + CTILES, C, 128), BF16)] * 2,
        compiler_params=pltpu.CompilerParams(vmem_limit_bytes=16 * MIB),
        name="pack_edges",
    )(x, x, c, c)


def turn_block(src, dst):
    for i in range(R // 16):
        for t in range(W // 128):
            at = slice(t * 128, (t + 1) * 128)
            dst[i * 16 : (i + 1) * 16, :, at] = turn(src[:, i * 16 : (i + 1) * 16, at])


XROWS = 2 * HALO + 3
CROWS = HALO + 1


def turn_kernel(x_ref, c_ref, xt, x_up, x_down, ct, c_up, c_down):
    turn_block(x_ref, xt)
    for out, rows in ((x_up, slice(0, HALO)), (x_down, slice(R - HALO, R))):
        out[0:HALO] = xt[rows, :, MAIN[0]]
        out[HALO : 2 * HALO] = xt[rows, :, MAIN[1]]
    turn_block(c_ref, ct)
    c_up[0:HALO] = ct[0:HALO]
    c_down[0:HALO] = ct[R - HALO : R]


def message(rows, width):
    return (
        pl.BlockSpec((rows, GC, width), lambda g: (0, g, 0)),
        pltpu.HBM((rows, C, width), BF16),
    )


def turn_both(x, c):
    native = pl.BlockSpec((GC, R, W), lambda g: (g, 0, 0))
    turned = pl.BlockSpec((R, GC, W), lambda g: (0, g, 0))
    block = pltpu.VMEM((R, C, W), BF16)
    (xs, x_shape), (cs, c_shape) = message(XROWS, W // 2), message(CROWS, W)
    return pl.pallas_call(
        turn_kernel,
        grid=(C // GC,),
        in_specs=[native, native],
        out_specs=[turned, xs, xs, turned, cs, cs],
        out_shape=[block, x_shape, x_shape, block, c_shape, c_shape],
        compiler_params=pltpu.CompilerParams(vmem_limit_bytes=16 * MIB),
        name="turn_both",
    )(x, c)


def fill_kernel(
    x_up_in, x_down_in, c_up_in, c_down_in, left, right, x_up, x_down, c_up, c_down, x_rows, c_rows, sems
):
    copies = []
    for q, (out, first) in enumerate(((x_up, 0), (x_down, XTILES - 3))):
        tiles = [left[first + k] for k in range(3)] + [right[first + k] for k in range(3)]
        for k in range(3):
            x_rows[q, k] = jnp.concatenate(tiles[2 * k : 2 * k + 2], axis=1)
        copies.append(pltpu.make_async_copy(x_rows.at[q], out.at[2 * HALO : XROWS], sems.at[q]))
    for q, (out, first) in enumerate(((c_up, XTILES), (c_down, XTILES + CTILES - 2))):
        tiles = [left[first], left[first + 1], right[first], right[first + 1]]
        c_rows[q] = jnp.concatenate(tiles, axis=1)
        copies.append(pltpu.make_async_copy(c_rows.at[q], out.at[HALO], sems.at[2 + q]))
    for copy in copies:
        copy.start()
    for copy in copies:
        copy.wait()


def fill(messages, left, right):
    return pl.pallas_call(
        fill_kernel,
        in_specs=[ANY] * 4 + [VM, VM],
        out_specs=[ANY] * 4,
        out_shape=[pltpu.HBM(m.shape, BF16) for m in messages],
        input_output_aliases={q: q for q in range(4)},
        scratch_shapes=[
            pltpu.VMEM((2, 3, C, W // 2), BF16),
            pltpu.VMEM((2, C, W), BF16),
            pltpu.SemaphoreType.DMA((4,)),
        ],
        compiler_params=pltpu.CompilerParams(vmem_limit_bytes=8 * MIB),
        name="fill_messages",
    )(*map(in_hbm, messages), left, right)


ANY = pl.BlockSpec(memory_space=pl.ANY)
VM = pl.BlockSpec(memory_space=pltpu.VMEM)
SM = pl.BlockSpec(memory_space=pltpu.SMEM)
STEP = 8
LONG = 16


def build_mask(tiles, mask):
    row_dev, col_dev = lax.axis_index("rows"), lax.axis_index(COLS)
    n_rows, n_cols = tiles.shape
    first_row, first_tile = row_dev * R, col_dev * (W // TILE)
    lane = lax.broadcasted_iota(jnp.int32, (16, 128), 1)

    def value(p, ct):
        cell = first_row + (-1, 0, R)[p]
        inside = (cell >= 0) & (cell < n_rows * TILE) & (ct >= 0) & (ct < n_cols)
        rt = jnp.clip(cell, 0, n_rows * TILE - 1) // TILE
        return jnp.where(inside, tiles[rt, jnp.clip(ct, 0, n_cols - 1)], 0)

    for p in range(3):
        for t in range(W // 128):
            cell = jnp.full((16, 128), value(p, first_tile + t), jnp.int32)
            mask[p, :, t * 128 : (t + 1) * 128] = cell.astype(F32).astype(BF16)
        right = jnp.full((16, 128), value(p, first_tile + W // TILE), jnp.int32)
        left = jnp.full((16, 128), value(p, first_tile - 1), jnp.int32)
        mask[p, :, W:E] = jnp.where(lane < 64, right, left).astype(F32).astype(BF16)


def masked(v, mask, r, at):
    if isinstance(r, int):
        p = int(r >= 0) + int(r >= R)
    else:
        p = (r >= 0).astype(jnp.int32) + (r >= R).astype(jnp.int32)
    m = mask[p, :, at]
    return v * jnp.concatenate([m] * (C // 16), axis=0)


def shifted(v, d):
    return pltpu.roll(v, (-d) % v.shape[1], 1)


def row_stack(v, d, reverse):
    ahead, behind = shifted(v, d), shifted(v, -d)
    parts = [ahead, v, behind] if reverse else [behind, v, ahead]
    return jnp.concatenate(parts, axis=0)


def forward_matrix(w):
    return jnp.concatenate([w[j].astype(F32).T for j in range(3)], axis=0).T.astype(BF16)


def backward_matrix(w, order=(0, 1, 2)):
    return jnp.concatenate([w[j].astype(F32) for j in order], axis=0).T.astype(BF16)


def two_rows(matrix):
    none = jnp.zeros((C, C), BF16)
    return jnp.concatenate(
        [jnp.concatenate([matrix, none], axis=1), jnp.concatenate([none, matrix], axis=1)], axis=0
    )


MAIN = (slice(0, 256), slice(256, 512))
TAIL = slice(W, E)


class Rows:
    def __init__(self, *parts):
        self.parts = parts

    def __call__(self, r, at):
        for first, count, get in self.parts:
            if first <= r < first + count:
                return get(r - first, at)
        raise IndexError(r)

    def row(self, r):
        return jnp.concatenate([self(r, at) for at in (*MAIN, TAIL)], axis=1)


def held(ref, *index):
    return lambda q, at: ref[(*index, q, slice(None), at)]


def with_tail(main, tail):
    return lambda q, at: tail[q] if at == TAIL else main[q, :, at]


def conv_columns(get, rows, d, matrix, post, tail=True, taps=(-1, 0, 1, 2)):
    def window(r, at):
        return jnp.concatenate([get(r + k * d, at) for k in taps], axis=0)

    def put(r, at, both):
        post(r, at, both[:C])
        if len(taps) == 4:
            post(r + d, at, both[C:])

    for r in rows:
        for at in MAIN:
            put(r, at, dot(matrix, window(r, at)))
    if tail:
        for r, s in zip(rows[::2], rows[1::2]):
            both = dot(matrix, jnp.concatenate([window(r, TAIL), window(s, TAIL)], axis=1))
            put(r, TAIL, both[:, :128])
            put(s, TAIL, both[:, 128:])


SINGLE = (-1, 0, 1)


def conv_rows(get, rows, d, reverse, matrix, post, tail=True):
    stacks = []
    for r in rows:
        stack = row_stack(get.row(r), d, reverse)
        stacks.append(stack)
        for at in MAIN:
            post(r, at, dot(matrix, stack[:, at]))
    if tail:
        for q in range(0, len(rows), 2):
            both = dot(matrix, jnp.concatenate([stacks[q][:, TAIL], stacks[q + 1][:, TAIL]], axis=1))
            post(rows[q], TAIL, both[:, :128])
            post(rows[q + 1], TAIL, both[:, 128:])
    return stacks


def add_col_taps(acc_ref, grads, hidden, d, rows):
    acc = acc_ref[...]
    for r in rows:
        for at in MAIN:
            left = jnp.concatenate([hidden(r + q * d, at) for q in (0, 1)], axis=0)
            right = jnp.concatenate([grads(r + q * d, at) for q in (-1, 0, 1, 2)], axis=0)
            acc += dot_nt(left, right)
    acc_ref[...] = acc


def add_col_taps_single(acc_ref, grads, hidden, d, rows):
    acc = acc_ref[0:C, 0 : 3 * C]
    for r in rows:
        for at in MAIN:
            right = jnp.concatenate([grads(r + q * d, at) for q in (-1, 0, 1)], axis=0)
            acc += dot_nt(hidden(r, at), right)
    acc_ref[0:C, 0 : 3 * C] = acc


def add_row_taps(acc_ref, values, rows, stacks):
    acc = acc_ref[...]
    for r, stack in zip(rows, stacks):
        for at in MAIN:
            acc += dot_nt(values(r, at), stack[:, at])
    acc_ref[...] = acc


def elu(p):
    return jnp.where(p > 0, p, jnp.exp(p) - 1.0)


def turn_out(src, out):
    for i in range(R // 16):
        for t in range(W // 128):
            at = slice(t * 128, (t + 1) * 128)
            out[:, i * 16 : (i + 1) * 16, at] = turn(src[i * 16 : (i + 1) * 16, :, at])


def call(kernel, name, in_specs, outs, scratch, cost, vmem, *args):
    return pl.pallas_call(
        kernel,
        in_specs=in_specs,
        out_specs=[ANY if getattr(out, "memory_space", None) == pltpu.HBM else VM for out in outs],
        out_shape=outs,
        scratch_shapes=scratch,
        compiler_params=pltpu.CompilerParams(vmem_limit_bytes=vmem * MIB),
        cost_estimate=pl.CostEstimate(flops=cost * 500_000_000, bytes_accessed=cost * 1_000_000, transcendentals=0),
        name=name,
    )(*args)


INNER = R - 2 * FIRST_SPACING
MIDDLE = R - 2 * SECOND_SPACING
OUTER = HALO
D1, D2 = FIRST_SPACING, SECOND_SPACING


def inner_kernel(
    tiles, x, c, left, right, wr, wc,
    xt, h1, b1, h2, ct, cm, a2, cg1, g1, col_acc, row_acc,
    mask,
):
    build_mask(tiles, mask)
    for dst, width, first, count in ((xt, XEDGE, 0, XTILES), (ct, CEDGE, XTILES, CTILES)):
        per = 128 // width

        def edges(g, _):
            for k in range(per):
                dst[g * per + k] = unpack(left[first + g], right[first + g], k, width)
            return 0

        lax.fori_loop(0, count, edges, 0)
    wr1, wr2 = forward_matrix(wr[0]), forward_matrix(wr[1])
    wc1 = two_rows(forward_matrix(wc[0]))
    wr2b = backward_matrix(wr[1])
    wc2b = two_rows(backward_matrix(wc[1], (2, 1, 0)))
    get_x = Rows((0, R, with_tail(x, xt)))
    get_c = Rows((0, R, with_tail(c, ct)))
    get_h1 = Rows((0, R, held(h1)))
    get_b1 = Rows((D1, INNER, held(b1)))
    get_h2 = Rows((D1, INNER, held(h2)))
    get_cm = Rows((0, R, held(cm)))
    get_a2 = Rows((D2, MIDDLE, held(a2)))

    def hidden_one(first):
        def post(row, at, pre):
            h1[row, :, at] = masked(elu(pre).astype(BF16), mask, row, at)

        conv_rows(get_x, [first + q for q in range(8)], D1, False, wr1, post)

    def block_one(first):
        def post(row, at, col):
            b1[row - D1, :, at] = get_x(row, at) + masked(col.astype(BF16), mask, row, at)

        conv_columns(get_h1, [first + q for q in range(D1)], D1, wc1, post)

    def hidden_two(first):
        def post(row, at, pre):
            h2[row - D1, :, at] = masked(elu(pre).astype(BF16), mask, row, at)

        conv_rows(get_b1, [first + q for q in range(8)], D2, False, wr2, post)

    def mask_cot(first):
        for r in range(first, first + 8):
            for at in (*MAIN, TAIL):
                cm[r, :, at] = masked(get_c(r, at), mask, r, at)

    hidden_one(0)
    mask_cot(0)
    hidden_one(8)
    mask_cot(8)
    block_one(4)
    hidden_one(16)
    mask_cot(16)
    block_one(12)
    hidden_two(4)
    hidden_one(24)
    mask_cot(24)
    block_one(20)
    hidden_two(12)
    hidden_two(20)

    def post_two(row, at, hid):
        slope = 1.0 + jnp.minimum(get_h2(row, at), 0).astype(F32)
        a2[row - D2, :, at] = masked((hid * slope).astype(BF16), mask, row, at)

    rows = [D2 + q for q in range(D2)]
    conv_columns(get_cm, rows, D2, wc2b, post_two)
    col_acc[...] = jnp.zeros_like(col_acc)
    row_acc[...] = jnp.zeros_like(row_acc)
    add_col_taps(col_acc, get_cm, get_h2, D2, rows)

    def post_one(row, at, mixed):
        g = get_c(row, at).astype(F32) + mixed
        cg1[row - D2, :, at] = masked(g.astype(BF16), mask, row, at)
        if at != TAIL:
            g1[row - D2, :, at] = g

    for first in range(D2, R - D2, 8):
        rows = list(range(first, first + 8))
        stacks = conv_rows(get_a2, rows, D2, True, wr2b, post_one)
        add_row_taps(row_acc, get_b1, rows, stacks)


def forward_inner(*args):
    return call(
        inner_kernel, "forward_inner", [SM] + [VM] * 6,
        [
            pltpu.VMEM((R, C, 128), BF16),
            pltpu.VMEM((R, C, E), BF16),
            pltpu.VMEM((INNER, C, E), BF16),
            pltpu.VMEM((INNER, C, E), BF16),
            pltpu.VMEM((R, C, 128), BF16),
            pltpu.VMEM((R, C, E), BF16),
            pltpu.VMEM((MIDDLE, C, E), BF16),
            pltpu.VMEM((MIDDLE, C, E), BF16),
            pltpu.VMEM((MIDDLE, C, W), F32),
            pltpu.VMEM((2 * C, 4 * C), F32),
            pltpu.VMEM((C, 3 * C), F32),
        ],
        [pltpu.VMEM((3, 16, E), BF16)],
        14, 8, *args,
    )


def outer_kernel(
    tiles, above, below, x, xt, h1, b1, h2, wr, wc,
    out, b1s, h2s,
    xe, h1e, flat, mask,
):
    build_mask(tiles, mask)
    wr1, wr2 = forward_matrix(wr[0]), forward_matrix(wr[1])
    wc1s = forward_matrix(wc[0])
    wc1, wc2 = two_rows(wc1s), two_rows(forward_matrix(wc[1]))
    per = 128 // XEDGE

    def message(side, ref):
        def get(q, at):
            if at == TAIL:
                return xe[side, q]
            return ref[q if at == MAIN[0] else HALO + q]

        return get

    for side, ref in enumerate((above, below)):
        tile = [ref[2 * HALO + k // 2, :, (k % 2) * 128 : (k % 2 + 1) * 128] for k in range(6)]
        for q in range(HALO):
            xe[side, q] = unpack(tile[q // per], tile[3 + q // per], q % per, XEDGE)
    get_x = Rows((-HALO, HALO, message(0, above)), (0, R, with_tail(x, xt)), (R, HALO, message(1, below)))
    get_h1 = Rows((-HALO, HALO, held(h1e, 0)), (0, R, held(h1)), (R, HALO, held(h1e, 1)))
    get_b1 = Rows((-D2, OUTER, held(b1s, 0)), (D1, INNER, held(b1)), (R - D1, OUTER, held(b1s, 1)))
    get_h2 = Rows((-D2, OUTER, held(h2s, 0)), (D1, INNER, held(h2)), (R - D1, OUTER, held(h2s, 1)))

    def hidden_one(side):
        first = (-HALO, R)[side]

        def post(row, at, pre):
            h1e[side, row - first, :, at] = masked(elu(pre).astype(BF16), mask, row, at)

        conv_rows(get_x, [first + q for q in range(HALO)], D1, False, wr1, post)

    def block_one(side):
        first = (-D2, R - D1)[side]

        def post(row, at, col):
            b1s[side, row - first, :, at] = get_x(row, at) + masked(col.astype(BF16), mask, row, at)

        conv_columns(get_h1, [first + q for q in range(D1)], D1, wc1, post)
        conv_columns(get_h1, [first + 2 * D1 + q for q in range(D1)], D1, wc1s, post, taps=SINGLE)

    def hidden_two(side):
        first = (-D2, R - D1)[side]

        def post(row, at, pre):
            h2s[side, row - first, :, at] = masked(elu(pre).astype(BF16), mask, row, at)

        conv_rows(get_b1, [first + q for q in range(OUTER)], D2, False, wr2, post)

    def last(first):
        def post(row, at, col):
            flat[row, :, at] = get_b1(row, at) + masked(col.astype(BF16), mask, row, at)

        conv_columns(get_h2, [first + q for q in range(D2)], D2, wc2, post, tail=False)

    hidden_one(0)
    block_one(0)
    hidden_one(1)
    hidden_two(0)
    block_one(1)
    last(0)
    hidden_two(1)
    last(2 * D2)
    turn_out(flat, out)


def forward_outer(*args):
    return call(
        outer_kernel, "forward_outer", [SM] + [VM] * 9,
        [
            jax.ShapeDtypeStruct((C, R, W), BF16),
            pltpu.VMEM((2, OUTER, C, E), BF16),
            pltpu.VMEM((2, OUTER, C, E), BF16),
        ],
        [
            pltpu.VMEM((2, HALO, C, 128), BF16),
            pltpu.VMEM((2, HALO, C, E), BF16),
            pltpu.VMEM((R, C, W), BF16),
            pltpu.VMEM((3, 16, E), BF16),
        ],
        14, 16, *args,
    )


PIECES = 32
PIECE = 6 * C // PIECES
REST = D1 + D2


def backward_kernel(
    tiles, above, below, wr, wc, c, ct, cm, a2, cg1, g1, col_in, row_in, x, h1, b1, b1s, h2, h2s,
    taps, a1, g1_out,
    cmh, a2s, cg1s, g1s, col_acc, row_acc, mask, sems,
):
    saves = [pltpu.make_async_copy(g1, g1_out.at[D2 : R - D2], sems.at[0])]
    saves[0].start()
    build_mask(tiles, mask)
    wr1, wr2 = backward_matrix(wr[0]), backward_matrix(wr[1])
    wc1, wc2 = backward_matrix(wc[0], (2, 1, 0)), backward_matrix(wc[1], (2, 1, 0))
    wc1w, wc2w = two_rows(wc1), two_rows(wc2)
    per = 128 // CEDGE
    for side, ref, skip in ((0, above, 2 * per - HALO), (1, below, 0)):
        first = (-HALO, R)[side]
        tile = [ref[HALO, :, t * 128 : (t + 1) * 128] for t in range(4)]
        for q in range(HALO):
            g, k = divmod(q + skip, per)
            for at in MAIN:
                cmh[side, q, :, at] = masked(ref[q, :, at], mask, first + q, at)
            cmh[side, q, :, TAIL] = masked(unpack(tile[g], tile[2 + g], k, CEDGE), mask, first + q, TAIL)
    get_c = Rows((-HALO, HALO, held(cmh, 0)), (0, R, with_tail(c, ct)), (R, HALO, held(cmh, 1)))
    get_cm = Rows((-HALO, HALO, held(cmh, 0)), (0, R, held(cm)), (R, HALO, held(cmh, 1)))
    get_b1 = Rows((-D2, OUTER, held(b1s, 0)), (D1, INNER, held(b1)), (R - D1, OUTER, held(b1s, 1)))
    get_h2 = Rows((-D2, OUTER, held(h2s, 0)), (D1, INNER, held(h2)), (R - D1, OUTER, held(h2s, 1)))
    get_a2 = Rows((-D1, REST, held(a2s, 0)), (D2, MIDDLE, held(a2)), (R - D2, REST, held(a2s, 1)))
    get_cg1 = Rows((-D1, REST, held(cg1s, 0)), (D2, MIDDLE, held(cg1)), (R - D2, REST, held(cg1s, 1)))
    get_h1 = Rows((0, R, held(h1)))
    get_a1 = Rows((0, R, held(a1)))
    get_x = Rows((0, R, held(x)))
    firsts = (-D1, R - D2)

    col_acc[0] = col_in[...]
    row_acc[0] = row_in[...]
    col_acc[1] = jnp.zeros_like(col_in)
    row_acc[1] = jnp.zeros_like(row_in)
    for side, first in enumerate(firsts):

        def post_two(row, at, hid):
            slope = 1.0 + jnp.minimum(get_h2(row, at), 0).astype(F32)
            a2s[side, row - first, :, at] = masked((hid * slope).astype(BF16), mask, row, at)

        conv_columns(get_cm, [first + q for q in range(D1)], D2, wc2w, post_two)
        conv_columns(get_cm, [first + D1 + q for q in range(D1)], D2, wc2, post_two, taps=SINGLE)
    for side, first in enumerate(firsts):
        own = [r for r in range(first, first + REST) if 0 <= r < R]
        add_col_taps_single(col_acc.at[0], get_cm, get_h2, D2, own)

        def post_one(row, at, mixed):
            g = get_c(row, at).astype(F32) + mixed
            cg1s[side, row - first, :, at] = masked(g.astype(BF16), mask, row, at)
            if at != TAIL and row in own:
                g1s[side, row - own[0], :, at] = g

        rows = list(range(first, first + REST))
        stacks = conv_rows(get_a2, rows, D2, True, wr2, post_one)
        kept = [(r, stack) for r, stack in zip(rows, stacks) if r in own]
        add_row_taps(row_acc.at[0], get_b1, [k[0] for k in kept], [k[1] for k in kept])
        saves.append(pltpu.make_async_copy(g1s.at[side], g1_out.at[own[0] : own[0] + D2], sems.at[1 + side]))
        saves[-1].start()

    for first in range(0, R, 2 * D1):

        def post(row, at, hid):
            slope = 1.0 + jnp.minimum(h1[row, :, at], 0).astype(F32)
            a1[row, :, at] = masked((hid * slope).astype(BF16), mask, row, at)

        rows = [first + q for q in range(D1)]
        conv_columns(get_cg1, rows, D1, wc1w, post)
        add_col_taps(col_acc.at[1], get_cg1, get_h1, D1, rows)
        rows = list(range(first, first + 2 * D1))
        add_row_taps(row_acc.at[1], get_x, rows, [row_stack(get_a1.row(r), D1, True) for r in rows])

    for k in range(2):
        acc = col_acc[k]
        low, high = acc[:C].T, acc[C:].T
        col = [low[(2 - q) * C : (3 - q) * C] + high[(3 - q) * C : (4 - q) * C] for q in range(3)]
        both = jnp.concatenate([jnp.concatenate(col, axis=0), row_acc[k].T], axis=1)
        for q in range(PIECES // 2):
            taps[k * PIECES // 2 + q] = both[q * PIECE : (q + 1) * PIECE]
    for save in saves:
        save.wait()


def backward(*args):
    return call(
        backward_kernel, "backward", [SM] + [VM] * 18,
        [
            jax.ShapeDtypeStruct((PIECES, PIECE, 2 * C), F32),
            pltpu.VMEM((R, C, E), BF16),
            pltpu.HBM((R, C, W), F32),
        ],
        [
            pltpu.VMEM((2, HALO, C, E), BF16),
            pltpu.VMEM((2, REST, C, E), BF16),
            pltpu.VMEM((2, REST, C, E), BF16),
            pltpu.VMEM((2, D2, C, W), F32),
            pltpu.VMEM((2, 2 * C, 4 * C), F32),
            pltpu.VMEM((2, C, 3 * C), F32),
            pltpu.VMEM((3, 16, E), BF16),
            pltpu.SemaphoreType.DMA((3,)),
        ],
        16, 20, *args,
    )


def map_kernel(a1, g1_in, wr, out, g1, flat, sems):
    loads = [pltpu.make_async_copy(g1_in.at[r : r + 8], g1.at[r : r + 8], sems.at[r // 8]) for r in range(0, R, 8)]
    for load in loads:
        load.start()
    wr1 = backward_matrix(wr[0])
    get_a1 = Rows((0, R, held(a1)))

    def post(row, at, mixed):
        flat[row, :, at] = (g1[row, :, at] + mixed).astype(BF16)

    for load, first in zip(loads, range(0, R, 8)):
        load.wait()
        conv_rows(get_a1, [first + q for q in range(8)], D1, True, wr1, post, tail=False)
    turn_out(flat, out)


def backward_map(*args):
    return call(
        map_kernel, "backward_map", [VM, ANY, VM],
        [jax.ShapeDtypeStruct((C, R, W), BF16)],
        [pltpu.VMEM((R, C, W), F32), pltpu.VMEM((R, C, W), BF16), pltpu.SemaphoreType.DMA((R // 8,))],
        4, 14, *args,
    )[0]


def tap_sum(taps, beside):
    part = lax.all_to_all(taps, "rows", 0, 0, tiled=True)
    part = lax.all_gather(part.sum(0), COLS).sum(0)
    spread = jnp.broadcast_to(part[None], taps.shape)
    whole = lax.all_to_all(spread, "rows", 0, 0, tiled=True)
    return whole.reshape(2, 3, C, 2 * C), beside


COLS = ("y_hi", "core")


def in_hbm(array):
    return pltpu.with_memory_space_constraint(array, pltpu.HBM)


def in_vmem(array):
    return pltpu.with_memory_space_constraint(array, pltpu.VMEM)


def on_device(x, tile_mask, wr, wc, cot):
    n_rows, n_cols = lax.axis_size("rows"), lax.axis_size(COLS)
    factor = 1.0 / math.sqrt(R * n_rows * W * n_cols)
    down = [(i, i + 1) for i in range(n_rows - 1)]
    up = [(i + 1, i) for i in range(n_rows - 1)]
    right = [(i, i + 1) for i in range(n_cols - 1)]
    left = [(i + 1, i) for i in range(n_cols - 1)]

    to_left, to_right = pack_edges(in_hbm(x), in_hbm(cot))
    from_right = in_vmem(lax.ppermute(to_left, COLS, left))
    from_left = in_vmem(lax.ppermute(to_right, COLS, right))
    xt, x_up, x_down, ct, c_up, c_down = turn_both(x, cot)
    x_up, x_down, c_up, c_down = fill((x_up, x_down, c_up, c_down), from_left, from_right)
    x_above = in_vmem(lax.ppermute(x_down, "rows", down))
    x_below = in_vmem(lax.ppermute(x_up, "rows", up))
    c_above = in_vmem(lax.ppermute(c_down, "rows", down))
    c_below = in_vmem(lax.ppermute(c_up, "rows", up))

    xt, ct = in_vmem(xt), in_vmem(ct)
    x_tail, h1, b1, h2, c_tail, cm, a2, cg1, g1, col_taps, row_taps = map(
        in_vmem, forward_inner(tile_mask, xt, ct, from_left, from_right, wr, wc)
    )
    final, b1s, h2s = forward_outer(tile_mask, x_above, x_below, xt, x_tail, h1, b1, h2, wr, wc)
    b1s, h2s = in_vmem(b1s), in_vmem(h2s)
    taps, a1, g1 = backward(
        tile_mask, c_above, c_below, wr, wc, ct, c_tail, cm, a2, cg1, g1, col_taps, row_taps,
        xt, h1, b1, b1s, h2, h2s,
    )
    total, map_grad = tap_sum(taps, backward_map(in_vmem(a1), in_hbm(g1), wr))
    total = total[::-1] * factor
    return final, map_grad, total[..., C:], total[..., :C]


def solution(mesh):
    n_rows, n_cols = mesh.devices.shape
    inner = Mesh(mesh.devices.reshape(n_rows, n_cols // 2, 2), ("rows",) + COLS)
    blocks = P(None, "rows", COLS)
    return jax.shard_map(
        on_device,
        mesh=inner,
        in_specs=(blocks, P(), P(), P(), blocks),
        out_specs=(blocks, blocks, P(), P()),
        check_vma=False,
    )
```
